32 devices in a mesh: wide: 8 (over y, x, core), narrow: 4 (over z).
Axes of the slice: x: 2, y: 2, z: 4, core: 2. Of those that a mesh axis runs over, the one named last changes fastest.
Arguments:
- long_in: bfloat16 [2, 32, 512, 768], P(None, ('wide', 'narrow')), may hold values from -6 to 6
- glob_in: bfloat16 [2, 32, 32, 768], P(None, ('wide', 'narrow')), may hold values from -6 to 6
- lengths: int32 [2, 32], P(None, ('wide', 'narrow')), may hold values from 128 to 512, as said below
- ln1_gain: bfloat16 [768], P(('wide', 'narrow')), may hold values from 0.5 to 1.5
- ln1_bias: bfloat16 [768], P(('wide', 'narrow')), may hold values from -1.5 to 1.5
- w_qkv: bfloat16 [768, 2304], P(('wide', 'narrow')), may hold values from -0.21875 to 0.21875
- qv_bias: bfloat16 [1536], P(('wide', 'narrow')), may hold values from -1.5 to 1.5
- rel_embed: bfloat16 [768, 169], P(('wide', 'narrow')), may hold values from -6 to 6
- w_out: bfloat16 [768, 768], P(('wide', 'narrow')), may hold values from -3 to 3
- out_bias: bfloat16 [768], P(('wide', 'narrow')), may hold values from -1.5 to 1.5
- ln2_gain: bfloat16 [768], P(('wide', 'narrow')), may hold values from 0.5 to 1.5
- ln2_bias: bfloat16 [768], P(('wide', 'narrow')), may hold values from -1.5 to 1.5
- w_in: bfloat16 [768, 3072], P(('wide', 'narrow')), may hold values from -0.21875 to 0.21875
- in_bias: bfloat16 [3072], P(('wide', 'narrow')), may hold values from -1.5 to 1.5
- w_down: bfloat16 [3072, 768], P(('wide', 'narrow')), may hold values from -0.109375 to 0.109375
- down_bias: bfloat16 [768], P(('wide', 'narrow')), may hold values from -1.5 to 1.5
- cot_long: bfloat16 [2, 32, 512, 768], P(None, ('wide', 'narrow')), may hold values from -6 to 6
- cot_glob: bfloat16 [2, 32, 32, 768], P(None, ('wide', 'narrow')), may hold values from -6 to 6
Outputs:
- block_long: bfloat16 [2, 32, 512, 768], P(None, ('wide', 'narrow'))
- block_glob: bfloat16 [2, 32, 32, 768], P(None, ('wide', 'narrow'))
- grad_long: bfloat16 [2, 32, 512, 768], P(None, ('wide', 'narrow'))
- grad_glob: bfloat16 [2, 32, 32, 768], P(None, ('wide', 'narrow'))
- grad_ln1_gain: float32 [768], P(('wide', 'narrow'))
- grad_ln1_bias: float32 [768], P(('wide', 'narrow'))
- grad_w_qkv: float32 [768, 2304], P(('wide', 'narrow'))
- grad_qv_bias: float32 [1536], P(('wide', 'narrow'))
- grad_rel_embed: float32 [768, 169], P(('wide', 'narrow'))
- grad_w_out: float32 [768, 768], P(('wide', 'narrow'))
- grad_out_bias: float32 [768], P(('wide', 'narrow'))
- grad_ln2_gain: float32 [768], P(('wide', 'narrow'))
- grad_ln2_bias: float32 [768], P(('wide', 'narrow'))
- grad_w_in: float32 [768, 3072], P(('wide', 'narrow'))
- grad_in_bias: float32 [3072], P(('wide', 'narrow'))
- grad_w_down: float32 [3072, 768], P(('wide', 'narrow'))
- grad_down_bias: float32 [768], P(('wide', 'narrow'))
The draws below stay inside these ranges and needn't reach their ends.
Inputs may be any that keep to these rules, and one draw needn't show every extreme that they name: lengths[u, n] is the number of live long tokens of sequence n in micro-batch u; rows at or beyond it are padding. Every draw has an entry equal to 512 and one equal to 128.
All inputs are finite; a program needn't handle non-finite values.
Results may differ from the reference program's by a relative error of at most 0.012.
Values may be sent and summed in bfloat16 or wider, within the bound.
No kernel may reach another device: no remote copies, remote signals or barrier semaphores. Data moves between devices by JAX's collectives and lax.ppermute only.
A program may use at most 320 MiB of HBM per device.

```python
import jax
import jax.numpy as jnp
from jax import lax

D = 768
HEADS = 12
HEAD_DIM = 64
FF = 3072
RADIUS = 84
GLOBAL_STRIDE = 16
SEQ = 512
BLOCK = 512
MARGIN = 112
MICRO = 2
RELS = 169
GLOB = 32
NSEQ = 32


def draw_lengths(key, part):
    entries = MICRO * NSEQ
    key_len, key_top, key_low = jax.random.split(key, 3)
    lengths_drawn = jax.random.randint(key_len, (entries,), SEQ // 4, SEQ + 1, dtype=jnp.int32)
    top_at = jax.random.randint(key_top, (), 0, entries, dtype=jnp.int32)
    low_at = (top_at + 1 + jax.random.randint(key_low, (), 0, entries - 1, dtype=jnp.int32)) % entries
    positions = jnp.arange(entries, dtype=jnp.int32)
    lengths_drawn = jnp.where(positions == top_at, SEQ, lengths_drawn)
    lengths_drawn = jnp.where(positions == low_at, SEQ // 4, lengths_drawn)
    return lengths_drawn.reshape(MICRO, NSEQ)


def levels(rng, extent, cuts, least, high):
    def one(dim, parts):
        draws = jax.random.uniform(jax.random.fold_in(jax.random.fold_in(rng, 6), dim), (parts,), jnp.float32, least / len(cuts), high / len(cuts))
        return jnp.repeat(jnp.exp(draws), extent[dim] // parts).reshape((-1,) + (1,) * (len(extent) - dim - 1))

    gain = one(*cuts[0])
    for cut in cuts[1:]:
        gain = gain * one(*cut)
    return gain


def noise(stream_key, extent, width, limit, cuts=(), kind=jnp.bfloat16):
    values = jax.random.normal(stream_key, extent, jnp.float32) * width
    if len(cuts) > 0:
        values = levels(stream_key, extent, cuts, -0.22, 0.18) * values
    return jnp.clip(values, min=-limit, max=limit).astype(kind)


def setup_inputs(seed: int = 0) -> dict:
    keys = jax.random.split(jax.random.key(seed), 19)
    return {
        "long_in": noise(keys[0], (MICRO, NSEQ, SEQ, D), 1.0, 6.0, ((1, 32),)),
        "glob_in": noise(keys[1], (MICRO, NSEQ, GLOB, D), 1.0, 6.0, ((1, 32),)),
        "lengths": draw_lengths(jax.random.fold_in(keys[18], 71), 0),
        "ln1_gain": jnp.clip(1.0 + 0.1 * jax.random.normal(keys[3], (D,), jnp.float32), 0.5, 1.5).astype(jnp.bfloat16),
        "ln1_bias": noise(keys[4], (D,), 0.3, 1.5, ((0, 32),)),
        "w_qkv": noise(keys[5], (D, 3 * D), D ** -0.5, 0.21875, ((0, 32),)),
        "qv_bias": noise(keys[6], (2 * D,), 0.3, 1.5, ((0, 32),)),
        "rel_embed": noise(keys[7], (D, RELS), 1.0, 6.0, ((0, 32),)),
        "w_out": noise(keys[8], (D, D), (D // 192) ** -0.5, 3.0, ((0, 32),)),
        "out_bias": noise(keys[9], (D,), 0.3, 1.5, ((0, 32),)),
        "ln2_gain": jnp.clip(1.0 + 0.1 * jax.random.normal(keys[10], (D,), jnp.float32), 0.5, 1.5).astype(jnp.bfloat16),
        "ln2_bias": noise(keys[11], (D,), 0.3, 1.5, ((0, 32),)),
        "w_in": noise(keys[12], (D, FF), D ** -0.5, 0.21875, ((0, 32),)),
        "in_bias": noise(keys[13], (FF,), 0.3, 1.5, ((0, 32),)),
        "w_down": noise(keys[14], (FF, D), FF ** -0.5, 0.109375, ((0, 32),)),
        "down_bias": noise(keys[15], (D,), 0.3, 1.5, ((0, 32),)),
        "cot_long": noise(keys[16], (MICRO, NSEQ, SEQ, D), 1.0, 6.0, ((1, 32),)),
        "cot_glob": noise(keys[17], (MICRO, NSEQ, GLOB, D), 1.0, 6.0, ((1, 32),)),
    }


eps_norm = 1e-06
neg_big = -1e+30
highest = lax.Precision.HIGHEST

@jax.custom_vjp
def low(v):
    return lax.optimization_barrier(v.astype(jnp.bfloat16)).astype(jnp.float32)

@jax.custom_vjp
def low_back(v):
    return v

def low_keep(v):
    return (low(v), None)

def low_pass(kept, grad):
    return (grad,)

def back_keep(v):
    return (v, None)

def back_low(kept, grad):
    return (low(grad),)
low.defvjp(low_keep, low_pass)
low_back.defvjp(back_keep, back_low)

def matmul(left_side, right_side):
    return jnp.dot(left_side, right_side, precision=highest, preferred_element_type=jnp.float32)

def norm_apply(values, gain_vec, shift_vec):
    centred = values - lax.optimization_barrier(jnp.mean(values, axis=-1, keepdims=True))
    spread = lax.optimization_barrier(jnp.mean(centred * centred, axis=-1, keepdims=True))
    return centred * lax.rsqrt(spread + eps_norm) * gain_vec + shift_vec

def skew_rows(rel_scores):
    head_count = rel_scores.shape[0]
    win_cols = BLOCK + 2 * MARGIN
    lead_cols = MARGIN - RADIUS
    placed = jnp.pad(rel_scores, ((0, 0), (0, 0), (lead_cols, win_cols + 1 - lead_cols - RELS)))
    flat_rows = placed.reshape(head_count, BLOCK * (win_cols + 1))[:, :BLOCK * win_cols]
    return flat_rows.reshape(head_count, BLOCK, win_cols)

def live_rows(length):
    glob_count = (length + GLOBAL_STRIDE - 1) // GLOBAL_STRIDE
    glob_ok = jnp.arange(GLOB, dtype=jnp.int32) < glob_count
    long_ok = jnp.arange(SEQ, dtype=jnp.int32) < length
    return (glob_ok, long_ok)

def long_allowed(row_start, length, glob_ok):
    win_cols = BLOCK + 2 * MARGIN
    row_pos = row_start + jnp.arange(BLOCK, dtype=jnp.int32)
    col_pos = row_start - MARGIN + jnp.arange(win_cols, dtype=jnp.int32)
    near_band = jnp.abs(col_pos[None, :] - row_pos[:, None]) <= RADIUS
    inside = (col_pos >= 0) & (col_pos < length)
    glob_part = jnp.broadcast_to(glob_ok[None, :], (BLOCK, GLOB))
    return jnp.concatenate([glob_part, near_band & inside[None, :]], axis=1)

def block_inputs(queries, key_rows, value_rows, glob_ok, long_ok, length, block_num):
    if block_num < 0:
        allowed = jnp.broadcast_to(jnp.concatenate([glob_ok, long_ok])[None, :], (GLOB, GLOB + SEQ))
        return (queries[:GLOB], key_rows, value_rows, allowed)
    row_start = block_num * BLOCK
    win_cols = BLOCK + 2 * MARGIN
    pad_spec = ((MARGIN, MARGIN), (0, 0), (0, 0))
    keys_win = jnp.pad(key_rows[GLOB:], pad_spec)[row_start:row_start + win_cols]
    values_win = jnp.pad(value_rows[GLOB:], pad_spec)[row_start:row_start + win_cols]
    cols_k = jnp.concatenate([key_rows[:GLOB], keys_win], axis=0)
    cols_v = jnp.concatenate([value_rows[:GLOB], values_win], axis=0)
    block_q = queries[GLOB + row_start:GLOB + row_start + BLOCK]
    return (block_q, cols_k, cols_v, long_allowed(row_start, length, glob_ok))

def attend(block_q, cols_k, cols_v, rel_heads, allowed, with_rel):
    scores = jnp.einsum('qhd,khd->hqk', block_q, cols_k, precision=highest)
    if with_rel:
        rel_scores = jnp.einsum('qhd,hdl->hql', block_q, rel_heads, precision=highest)
        scores = scores + jnp.pad(skew_rows(rel_scores), ((0, 0), (0, 0), (GLOB, 0)))
    scores = low_back(jnp.where(allowed[None], scores * 0.125, neg_big))
    row_max = lax.optimization_barrier(jnp.max(scores, axis=-1, keepdims=True))
    exp_terms = jnp.exp(scores - row_max)
    soft_weights = low(exp_terms / lax.optimization_barrier(jnp.sum(exp_terms, axis=-1, keepdims=True)))
    return jnp.einsum('hqk,khd->qhd', soft_weights, cols_v, precision=highest)

def layer(long_rows, glob_rows, length, params):
    ln1_gain, ln1_bias, w_qkv, qv_bias, rel_embed, w_out, out_bias, ln2_gain, ln2_bias, w_in, in_bias, w_down, down_bias = params
    row_count = GLOB + SEQ
    hidden_in = jnp.concatenate([glob_rows, long_rows], axis=0)
    normed = low(norm_apply(hidden_in, ln1_gain, ln1_bias))
    full_bias = jnp.concatenate([qv_bias[:D], jnp.zeros((D,), jnp.float32), qv_bias[D:]])
    projected = low(low_back(matmul(normed, w_qkv) + full_bias))
    head_view = projected.reshape(row_count, 3, HEADS, HEAD_DIM)
    queries = head_view[:, 0]
    key_rows = head_view[:, 1]
    value_rows = head_view[:, 2]
    rel_heads = rel_embed.reshape(HEADS, HEAD_DIM, RELS)
    glob_ok, long_ok = live_rows(length)
    pieces = []
    for block_num in range(-1, SEQ // BLOCK):
        block_q, cols_k, cols_v, allowed = block_inputs(queries, key_rows, value_rows, glob_ok, long_ok, length, block_num)
        pieces.append(attend(block_q, cols_k, cols_v, rel_heads, allowed, block_num >= 0))
    mixed_rows = low(low_back(jnp.concatenate(pieces, axis=0).reshape(row_count, D)))
    attn_out = low_back(matmul(mixed_rows, w_out) + out_bias)
    residual = hidden_in + attn_out
    normed2 = low(norm_apply(residual, ln2_gain, ln2_bias))
    pre_act = low_back(matmul(normed2, w_in) + in_bias)
    activated = low(jax.nn.gelu(pre_act, approximate=False))
    ffn_out = low_back(matmul(activated, w_down) + down_bias)
    live_mask = jnp.concatenate([glob_ok, long_ok])[:, None]
    result = jnp.where(live_mask, residual + ffn_out, 0.0)
    return (result[GLOB:], result[:GLOB])

def reference(long_in, glob_in, lengths, ln1_gain, ln1_bias, w_qkv, qv_bias, rel_embed, w_out, out_bias, ln2_gain, ln2_bias, w_in, in_bias, w_down, down_bias, cot_long, cot_glob):
    params = tuple((weight.astype(jnp.float32) for weight in (ln1_gain, ln1_bias, w_qkv, qv_bias, rel_embed, w_out, out_bias, ln2_gain, ln2_bias, w_in, in_bias, w_down, down_bias)))
    count_all = MICRO * NSEQ
    long_flat = long_in.astype(jnp.float32).reshape(count_all, SEQ, D)
    glob_flat = glob_in.astype(jnp.float32).reshape(count_all, GLOB, D)
    len_flat = lengths.reshape(count_all).astype(jnp.int32)

    def forward(weights, long_part, glob_part):
        step_fn = jax.checkpoint(lambda seq_parts: layer(seq_parts[0], seq_parts[1], seq_parts[2], weights))
        return lax.map(step_fn, (long_part, glob_part, len_flat))
    (out_long, out_glob), pullback = jax.vjp(forward, params, long_flat, glob_flat)
    weight_grads, grad_long_flat, grad_glob_flat = pullback((cot_long.astype(jnp.float32).reshape(count_all, SEQ, D), cot_glob.astype(jnp.float32).reshape(count_all, GLOB, D)))
    return (out_long.astype(jnp.bfloat16).reshape(MICRO, NSEQ, SEQ, D), out_glob.astype(jnp.bfloat16).reshape(MICRO, NSEQ, GLOB, D), grad_long_flat.astype(jnp.bfloat16).reshape(MICRO, NSEQ, SEQ, D), grad_glob_flat.astype(jnp.bfloat16).reshape(MICRO, NSEQ, GLOB, D), weight_grads[0], weight_grads[1], weight_grads[2], weight_grads[3], weight_grads[4], weight_grads[5], weight_grads[6], weight_grads[7], weight_grads[8], weight_grads[9], weight_grads[10], weight_grads[11], weight_grads[12])
```

```python
import functools
import jax
import jax.numpy as jnp
from jax import lax
from jax.experimental import pallas as pl
from jax.experimental.pallas import tpu as pltpu
from jax.sharding import PartitionSpec as P

HEAD_DIM = 64
RADIUS = 84
STRIDE = 16
SEQ = 512
GLOB = 32
RELS = 169
T = GLOB + SEQ
D = 768
FF = 3072
PAIRS = 6
LABELS = 256
LEAD = 4
BACK_LEAD = 3
EPS = 1e-06
NEG = -1e30
F32 = jnp.float32
BF16 = jnp.bfloat16
VMEM_LIMIT = 56 << 20
WINDOWS = ((0, 0, 256, 328, 0), (0, 0, 384, 72, 0), (1, 160, 384, 8, 352), (1, 288, 256, 8, 224))
OFFSETS = (0, 256, 640, 1024)
P_COLS = 1280
NN = (((1,), (0,)), ((), ()))
NT = (((1,), (1,)), ((), ()))
TN = (((0,), (0,)), ((), ()))


def dot(a, b, dims=NN):
    return lax.dot_general(a, b, dims, preferred_element_type=F32)


def params(*sem):
    return pltpu.CompilerParams(vmem_limit_bytes=VMEM_LIMIT, dimension_semantics=sem or None)


def iota(shape, dim):
    return lax.broadcasted_iota(jnp.int32, shape, dim)


def live_mask(length, cols):
    row = iota((T, cols), 0)
    glob_count = (length + STRIDE - 1) // STRIDE
    return row < jnp.where(row < GLOB, glob_count, length + GLOB)


def load_rows(pieces, pos_ref, lines, dst, sems, first_col):
    rows = dst.shape[0] // lines
    cols = dst.shape[1]
    copies = []
    k = 0
    for piece in pieces:
        for i in range(piece.shape[0] // rows):
            start = pl.multiple_of(pos_ref[k] * rows, 16)
            copies.append(
                pltpu.make_async_copy(
                    piece.at[pl.ds(i * rows, rows), pl.ds(first_col, cols)],
                    dst.at[pl.ds(start, rows), :],
                    sems.at[k],
                )
            )
            k += 1
    for copy in copies:
        copy.start()
    return copies


def project_kernel(lines, n_pieces, first_col, first_rel, pos_ref, hid_ref, gain_ref, bias_ref, full_bias_ref, *rest):
    pieces = rest[:n_pieces]
    normed_ref, proj_ref, rel_ref, relt_ref, w_s, sems = rest[n_pieces:]

    @pl.when(pl.program_id(0) == 0)
    def _():
        copies = load_rows(pieces, pos_ref, lines, w_s, sems.at[0], first_col)
        copies += load_rows(pieces, pos_ref, lines, rel_ref, sems.at[1], first_rel)
        for copy in copies:
            copy.wait()
        turned = rel_ref[...].astype(F32).T
        drop = LEAD - BACK_LEAD
        turned = jnp.concatenate([turned[drop:], turned[:drop]], axis=0)
        label = iota((LABELS, D), 0) - BACK_LEAD
        relt_ref[...] = jnp.where((label >= 0) & (label < RELS), turned, 0.0).astype(BF16)

    x = hid_ref[...].astype(F32)
    mean = jnp.mean(x, axis=1, keepdims=True)
    cen = x - mean
    var = jnp.mean(cen * cen, axis=1, keepdims=True)
    normed_ref[...] = (cen * lax.rsqrt(var + EPS) * gain_ref[...] + bias_ref[...]).astype(BF16)

    def step(j, _):
        col = pl.ds(pl.multiple_of(j * 256, 256), 256)
        proj_ref[:, col] = (dot(normed_ref[...], w_s[:, col]) + full_bias_ref[:, col]).astype(BF16)
        return 0

    lax.fori_loop(0, proj_ref.shape[1] // 256, step, 0)


def project(pos, hid, gain, bias, full_bias, pieces, first_col, first_rel):
    rows = hid.shape[0]
    n = len(pieces)
    lines = pos.shape[0]
    cols = full_bias.shape[1]
    spec = pl.BlockSpec((T, D), lambda s, *_: (s, 0))
    vec = lambda c: pl.BlockSpec((1, c), lambda s, *_: (0, 0))
    return pl.pallas_call(
        functools.partial(project_kernel, lines, n, first_col, first_rel),
        grid_spec=pltpu.PrefetchScalarGridSpec(
            num_scalar_prefetch=1,
            grid=(rows // T,),
            in_specs=[spec, vec(D), vec(D), vec(cols)] + [pl.BlockSpec(memory_space=pl.ANY)] * n,
            out_specs=[
                spec,
                pl.BlockSpec((T, cols), lambda s, *_: (s, 0)),
                pl.BlockSpec((D, LABELS), lambda s, *_: (0, 0)),
                pl.BlockSpec((LABELS, D), lambda s, *_: (0, 0)),
            ],
            scratch_shapes=[pltpu.VMEM((D, cols), BF16), pltpu.SemaphoreType.DMA((2, lines))],
        ),
        out_shape=[
            jax.ShapeDtypeStruct((rows, D), BF16),
            jax.ShapeDtypeStruct((rows, cols), BF16),
            jax.ShapeDtypeStruct((D, LABELS), BF16),
            jax.ShapeDtypeStruct((LABELS, D), BF16),
        ],
        compiler_params=params(),
        cost_estimate=pl.CostEstimate(flops=4 * rows * D * cols, bytes_accessed=12 << 20, transcendentals=0),
        name="project",
    )(pos, hid, gain, bias, full_bias, *pieces)


def flip_matrix():
    return (iota((128, 128), 0) + iota((128, 128), 1) == 127).astype(F32).astype(BF16)


def attend_kernel(len_ref, q_ref, k_ref, v_ref, rel_ref, mix_ref, p_ref, pg_ref, k_s, v_s):
    length = len_ref[pl.program_id(0)]
    live = live_mask(length, 128)
    lane = iota((T, 128), 1)
    q = q_ref[...].astype(F32) * 0.125
    k = k_ref[...].astype(F32)
    v = v_ref[...].astype(F32)
    rel = rel_ref[...].astype(F32)
    rel_row = iota((128, LABELS), 0)
    label = iota((128, LABELS), 1)
    outside = (label < LEAD) | (label >= LEAD + RELS)
    flip = flip_matrix()
    pad_tile = jnp.full((128, 128), NEG, F32)
    col = iota((128, 128), 1)
    out = [jnp.zeros((GLOB, 128), F32)] + [jnp.zeros((128, 128), F32) for _ in range(4)]
    for par in range(2):
        own = (lane // 64) == par
        flag = 64 * (1 - par)
        km = jnp.where(own, k, jnp.where((lane == flag) & ~live, NEG, 0.0)).astype(BF16)
        qm = jnp.where(own, q, jnp.where(lane == flag, 1.0, 0.0)).astype(BF16)
        vm = jnp.where(own, v, 0.0).astype(BF16)
        relm = jnp.where(
            (rel_row // 64) == par, rel, jnp.where((rel_row == flag) & outside, NEG, 0.0)
        ).astype(BF16)
        for s, m in ((k_s, km), (v_s, vm)):
            s[0] = m
            s[1, :SEQ] = m[GLOB:]
            s[1, SEQ:] = m[:GLOB]
        scores = dot(qm[:GLOB], km, NT)
        top = jnp.max(scores, axis=1, keepdims=True)
        e = jnp.exp(scores - top)
        p = (e * (1.0 / jnp.sum(e, axis=1, keepdims=True))).astype(BF16)
        pg_ref[0, 0, par] = p
        out[0] = out[0] + dot(p, vm)
        for b, (arr, first, width, shift, glob_at) in enumerate(WINDOWS):
            qb = qm[GLOB + 128 * b : GLOB + 128 * (b + 1)]
            scores = dot(qb, k_s[arr, first : first + width], NT)
            bias = dot(qb, relm)
            bias = pltpu.roll(
                jnp.concatenate([bias, pad_tile], axis=1), shift, 1, stride=1, stride_axis=0
            )
            tiles = [bias[:, 128 * i : 128 * (i + 1)] for i in range(width // 128)]
            tile, at = glob_at // 128, glob_at % 128
            tiles[tile] = jnp.where((col >= at) & (col < at + GLOB), 0.0, tiles[tile])
            scores = scores + jnp.concatenate(tiles, axis=1)
            top = jnp.max(scores, axis=1, keepdims=True)
            e = jnp.exp(scores - top)
            p = (e * (1.0 / jnp.sum(e, axis=1, keepdims=True))).astype(BF16)
            out[b + 1] = out[b + 1] + dot(p, v_s[arr, first : first + width])
            p_ref[0, 0, par, :, OFFSETS[b] : OFFSETS[b] + width] = dot(flip, p).astype(BF16)
    mix_ref[:GLOB] = out[0].astype(BF16)
    for b in range(4):
        mix_ref[GLOB + 128 * b : GLOB + 128 * (b + 1)] = out[b + 1].astype(BF16)


def attend(lengths, proj, rel, first_pair, n_pairs):
    rows = proj.shape[0]
    seqs = rows // T

    def part(n):
        return pl.BlockSpec((T, 128), lambda s, p, *_: (s, n * PAIRS + first_pair + p))

    return pl.pallas_call(
        attend_kernel,
        grid_spec=pltpu.PrefetchScalarGridSpec(
            num_scalar_prefetch=1,
            grid=(seqs, n_pairs),
            in_specs=[part(0), part(1), part(2), pl.BlockSpec((128, LABELS), lambda s, p, *_: (first_pair + p, 0))],
            out_specs=[
                pl.BlockSpec((T, 128), lambda s, p, *_: (s, p)),
                pl.BlockSpec((1, 1, 2, 128, P_COLS), lambda s, p, *_: (s, p, 0, 0, 0)),
                pl.BlockSpec((1, 1, 2, GLOB, T), lambda s, p, *_: (s, p, 0, 0, 0)),
            ],
            scratch_shapes=[pltpu.VMEM((2, T, 128), BF16)] * 2,
        ),
        out_shape=[
            jax.ShapeDtypeStruct((rows, n_pairs * 128), BF16),
            jax.ShapeDtypeStruct((seqs, n_pairs, 2, 128, P_COLS), BF16),
            jax.ShapeDtypeStruct((seqs, n_pairs, 2, GLOB, T), BF16),
        ],
        compiler_params=params(),
        cost_estimate=pl.CostEstimate(flops=n_pairs * 1600 << 20, bytes_accessed=n_pairs << 21, transcendentals=0),
        name="attend",
    )(lengths, proj, proj, proj, rel)


def attend_back_kernel(q_ref, k_ref, v_ref, relt_ref, do_ref, o_ref, p_ref, pg_ref, gq_ref, gk_ref, gv_ref, grel_ref, gk_s, gv_s, k_s, v_s, kt_s):
    s = pl.program_id(1)
    lane = iota((T, 128), 1)
    lane_b = iota((128, 128), 1)
    flip = flip_matrix()
    q = q_ref[...]
    k = k_ref[...]
    v = v_ref[...]
    do = do_ref[...]
    kf = k.astype(F32)
    v_s[0] = v
    v_s[1, :SEQ] = v[GLOB:]
    v_s[1, SEQ:] = v[:GLOB]
    for par in range(2):
        km = jnp.where((lane // 64) == par, kf, 0.0).astype(BF16)
        k_s[par, 0] = km
        k_s[par, 1, :SEQ] = km[GLOB:]
        k_s[par, 1, SEQ:] = km[:GLOB]

    @pl.when(s == 0)
    def _():
        grel_ref[...] = jnp.zeros_like(grel_ref)

    relt = relt_ref[...].astype(F32)
    rel_lane = iota((LABELS, 128), 1)
    reltm = [jnp.where((rel_lane // 64) == par, relt, 0.0).astype(BF16) for par in range(2)]
    qg_t = jnp.concatenate([q[:GLOB].astype(F32), jnp.zeros((96, 128), F32)], axis=0).T.astype(BF16)[:, :GLOB]
    dog_t = jnp.concatenate([do[:GLOB].astype(F32), jnp.zeros((96, 128), F32)], axis=0).T.astype(BF16)[:, :GLOB]
    do_g = do[:GLOB].astype(F32)
    prod = do_g * o_ref[:GLOB].astype(F32)
    gq = jnp.zeros((GLOB, 128), F32)
    gk_t, gv_t = [], []
    for par in range(2):
        own = (lane_b[:GLOB] // 64) == par
        dom = jnp.where(own, do_g, 0.0).astype(BF16)
        centre = jnp.sum(jnp.where(own, prod, 0.0), axis=1, keepdims=True)
        p = pg_ref[0, 0, par]
        ds = (p.astype(F32) * (dot(dom, v, NT) - centre)).astype(BF16)
        gq = gq + dot(ds, k_s[par, 0])
        gk_t.append(dot(qg_t[64 * par : 64 * par + 64], ds))
        gv_t.append(dot(dog_t[64 * par : 64 * par + 64], p))
    gq_ref[:GLOB] = (gq * 0.125).astype(BF16)
    kt_s[:, :T] = jnp.concatenate(gk_t, axis=0)
    kt_s[:, T:] = jnp.zeros((128, 640 - T), F32)
    gk_s[...] = kt_s[...].T[:T]
    kt_s[:, :T] = jnp.concatenate(gv_t, axis=0)
    gv_s[...] = kt_s[...].T[:T]
    for b, (arr, first, width, shift, glob_at) in enumerate(WINDOWS):
        rows = slice(GLOB + 128 * b, GLOB + 128 * (b + 1))
        qb = dot(flip, q[rows])
        dob = dot(flip, do[rows])
        prod = dob * dot(flip, o_ref[rows])
        qb_t = qb.T.astype(BF16)
        dob_t = dob.T.astype(BF16)
        v_win = v_s[arr, first : first + width]
        gq = jnp.zeros((128, 128), F32)
        gk_t, gv_t, grel = [], [], []
        for par in range(2):
            own = (lane_b // 64) == par
            dom = jnp.where(own, dob, 0.0).astype(BF16)
            centre = jnp.sum(jnp.where(own, prod, 0.0), axis=1, keepdims=True)
            p = p_ref[0, 0, par, :, OFFSETS[b] : OFFSETS[b] + width]
            ds = p.astype(F32) * (dot(dom, v_win, NT) - centre)
            ds16 = ds.astype(BF16)
            gq = gq + dot(ds16, k_s[par, arr, first : first + width])
            gk_t.append(dot(qb_t[64 * par : 64 * par + 64], ds16))
            gv_t.append(dot(dob_t[64 * par : 64 * par + 64], p))
            tiles = [ds[:, 128 * i : 128 * (i + 1)] for i in range(width // 128)]
            tile, at = glob_at // 128, glob_at % 128
            tiles[tile] = jnp.where((lane_b >= at) & (lane_b < at + GLOB), 0.0, tiles[tile])
            if width < 384:
                tiles.append(jnp.zeros((128, 128), F32))
            back = (256 - shift) % 384
            lab = pltpu.roll(jnp.concatenate(tiles, axis=1), back, 1, stride=1, stride_axis=0)
            lab = lab[:, :LABELS].astype(BF16)
            gq = gq + dot(lab, reltm[par])
            grel.append(dot(qb_t[64 * par : 64 * par + 64], lab))
        gq_ref[rows] = dot(flip, (gq * 0.125).astype(BF16)).astype(BF16)
        gk_b = jnp.concatenate(gk_t, axis=0).T
        gv_b = jnp.concatenate(gv_t, axis=0).T
        for acc, part in ((gk_s, gk_b), (gv_s, gv_b)):
            if arr == 0:
                acc[first : first + width] += part
            else:
                acc[GLOB + first : T] += part[: width - GLOB]
                acc[:GLOB] += part[width - GLOB :]
        grel_ref[...] += jnp.concatenate(grel, axis=0) * 0.125
    gk_ref[...] = (gk_s[...] * 0.125).astype(BF16)
    gv_ref[...] = gv_s[...].astype(BF16)


def attend_back(proj, relt, gmixed, mixed, p, pg, first_pair, n_pairs, mix_pair):
    rows = proj.shape[0]
    seqs = rows // T

    def part(n, at):
        return pl.BlockSpec((T, 128), lambda p, s: (s, n * PAIRS + at + p))

    grad = pl.BlockSpec((T, 128), lambda p, s: (s, p))
    return pl.pallas_call(
        attend_back_kernel,
        grid=(n_pairs, seqs),
        in_specs=[
            part(0, first_pair),
            part(1, first_pair),
            part(2, first_pair),
            pl.BlockSpec((LABELS, 128), lambda p, s: (0, first_pair + p)),
            part(0, first_pair),
            part(0, mix_pair),
            pl.BlockSpec((1, 1, 2, 128, P_COLS), lambda p, s: (s, p, 0, 0, 0)),
            pl.BlockSpec((1, 1, 2, GLOB, T), lambda p, s: (s, p, 0, 0, 0)),
        ],
        out_specs=[grad, grad, grad, pl.BlockSpec((128, LABELS), lambda p, s: (p, 0))],
        scratch_shapes=[
            pltpu.VMEM((T, 128), F32),
            pltpu.VMEM((T, 128), F32),
            pltpu.VMEM((2, 2, T, 128), BF16),
            pltpu.VMEM((2, T, 128), BF16),
            pltpu.VMEM((128, 640), F32),
        ],
        out_shape=[jax.ShapeDtypeStruct((rows, n_pairs * 128), BF16)] * 3
        + [jax.ShapeDtypeStruct((n_pairs * 128, LABELS), F32)],
        compiler_params=params(),
        cost_estimate=pl.CostEstimate(flops=n_pairs * 3200 << 20, bytes_accessed=n_pairs << 21, transcendentals=0),
        name="attend_back",
    )(proj, proj, proj, relt, gmixed, mixed, p, pg)


def norm_stats(x):
    cen = x - jnp.mean(x, axis=1, keepdims=True)
    rstd = lax.rsqrt(jnp.mean(cen * cen, axis=1, keepdims=True) + EPS)
    return cen * rstd, rstd


def mix_out_kernel(lines, n_pieces, first_col, n_mix, pos_ref, len_ref, hid_ref, bias_ref, gain2_ref, bias2_ref, cot_ref, *rest):
    mixed = rest[:n_mix]
    pieces = rest[n_mix : n_mix + n_pieces]
    res_ref, n2_ref, g_ref, w_s, sems = rest[n_mix + n_pieces :]
    s = pl.program_id(0)

    @pl.when(s == 0)
    def _():
        for copy in load_rows(pieces, pos_ref, lines, w_s, sems, first_col):
            copy.wait()

    def step(j, _):
        col = pl.ds(pl.multiple_of(j * 256, 256), 256)
        acc = hid_ref[:, col].astype(F32) + bias_ref[:, col]
        at = 0
        for m in mixed:
            acc = acc + dot(m[...], w_s[at : at + m.shape[1], col])
            at += m.shape[1]
        res_ref[:, col] = acc
        return 0

    lax.fori_loop(0, D // 256, step, 0)
    xhat, _ = norm_stats(res_ref[...])
    n2_ref[...] = (xhat * gain2_ref[...] + bias2_ref[...]).astype(BF16)
    live = live_mask(len_ref[s], D)
    g_ref[...] = jnp.where(live, cot_ref[...].astype(F32), 0.0).astype(BF16)


def mix_out(pos, lengths, hid, bias, gain2, bias2, cot, mixed, pieces, first_col):
    rows = hid.shape[0]
    n = len(pieces)
    lines = pos.shape[0]
    spec = pl.BlockSpec((T, D), lambda s, *_: (s, 0))
    vec = pl.BlockSpec((1, D), lambda s, *_: (0, 0))
    return pl.pallas_call(
        functools.partial(mix_out_kernel, lines, n, first_col, len(mixed)),
        grid_spec=pltpu.PrefetchScalarGridSpec(
            num_scalar_prefetch=2,
            grid=(rows // T,),
            in_specs=[spec, vec, vec, vec, spec]
            + [pl.BlockSpec((T, m.shape[1]), lambda s, *_: (s, 0)) for m in mixed]
            + [pl.BlockSpec(memory_space=pl.ANY)] * n,
            out_specs=[spec, spec, spec],
            scratch_shapes=[pltpu.VMEM((D, D), BF16), pltpu.SemaphoreType.DMA((lines,))],
        ),
        out_shape=[
            jax.ShapeDtypeStruct((rows, D), F32),
            jax.ShapeDtypeStruct((rows, D), BF16),
            jax.ShapeDtypeStruct((rows, D), BF16),
        ],
        compiler_params=params(),
        cost_estimate=pl.CostEstimate(flops=4 * rows * D * D, bytes_accessed=12 << 20, transcendentals=0),
        name="mix_out",
    )(pos, lengths, hid, bias, gain2, bias2, cot, *mixed, *pieces)


def store_rows(src, outs, rows, src_pos_ref, sems, first_col):
    cols = src.shape[1]
    copies = []
    k = 0
    for out in outs:
        for i in range(out.shape[0]):
            start = pl.multiple_of(src_pos_ref[k] * rows, 16)
            copies.append(
                pltpu.make_async_copy(
                    src.at[pl.ds(start, rows), :], out.at[i, :, pl.ds(first_col, cols)], sems.at[k]
                )
            )
            k += 1
    return copies


def gelu_parts(v):
    cdf = 0.5 * (1.0 + lax.erf(v * 0.7071067811865476))
    pdf = jnp.exp(v * v * -0.5) * 0.3989422804014327
    return v * cdf, cdf + v * pdf


def ffn_kernel(lines, n_in, first_in, first_down, n_parts, n_out, pos_ref, out_pos_ref, n2_ref, g_ref, b_ref, *rest):
    pieces = rest[:n_in]
    y_ref, gn2_ref, gb_ref = rest[n_in : n_in + 3]
    outs = rest[n_in + 3 : n_in + 3 + n_out]
    w_in_s, w_down_s, act_s, gpre_s, gw_s, sems, out_sems = rest[n_in + 3 + n_out :]
    part = pl.program_id(0)
    rows = n2_ref.shape[0]
    piece_rows = outs[0].shape[1]

    @pl.when(part == 0)
    def _():
        copies = load_rows(pieces, pos_ref, lines, w_in_s, sems.at[0], first_in)
        copies += load_rows(pieces, pos_ref, lines, w_down_s, sems.at[1], first_down)
        for copy in copies:
            copy.wait()
        y_ref[...] = jnp.zeros_like(y_ref)
        gn2_ref[...] = jnp.zeros_like(gn2_ref)

    cols = pl.ds(pl.multiple_of(part * D, 128), D)
    gb_ref[...] = jnp.zeros_like(gb_ref)
    tile = rows // 4

    def step(t, _):
        at = pl.ds(pl.multiple_of(t * tile, 16), tile)
        for n in range(D // 256):
            c = slice(256 * n, 256 * (n + 1))
            cc = pl.ds(pl.multiple_of(part * D + 256 * n, 128), 256)
            pre = dot(n2_ref[at, :], w_in_s[:, cc]) + b_ref[:, c]
            act, slope = gelu_parts(pre)
            act_s[at, c] = act.astype(BF16)
            gact = dot(g_ref[at, :], w_down_s[c, cols], NT)
            gpre = (gact * slope).astype(BF16)
            gpre_s[at, c] = gpre
            gb_ref[:, c] += jnp.sum(gpre.astype(F32), axis=0, keepdims=True)
        y_ref[at, :] += dot(act_s[at, :], w_down_s[:, cols])
        gn2_ref[at, :] += dot(gpre_s[at, :], w_in_s[:, cols], NT)
        return 0

    lax.fori_loop(0, 4, step, 0)

    def flush(which, first):
        return store_rows(gw_s.at[which], outs, piece_rows, out_pos_ref, out_sems.at[which], first)

    for which, (lhs, rhs) in enumerate(((n2_ref, gpre_s), (act_s, g_ref))):
        for n in range(D // 256):
            c = slice(256 * n, 256 * (n + 1))
            gw_s[which, :, c] = dot(lhs[...], rhs[:, c], TN).astype(BF16)
        for copy in flush(which, pl.multiple_of((which * n_parts + part) * D, 128)):
            copy.start()
    for which in range(2):
        for copy in flush(which, pl.multiple_of((which * n_parts + part) * D, 128)):
            copy.wait()


def ffn(pos, out_pos, n2, g, bias, pieces, first_in, first_down, n_parts, out_groups):
    rows = n2.shape[0]
    n = len(pieces)
    lines = pos.shape[0]
    full = pl.BlockSpec((rows, D), lambda q, *_: (0, 0))
    vec = pl.BlockSpec((1, D), lambda q, *_: (0, q))
    anywhere = pl.BlockSpec(memory_space=pl.ANY)
    return pl.pallas_call(
        functools.partial(ffn_kernel, lines, n, first_in, first_down, n_parts, len(out_groups)),
        grid_spec=pltpu.PrefetchScalarGridSpec(
            num_scalar_prefetch=2,
            grid=(n_parts,),
            in_specs=[full, full, vec] + [anywhere] * n,
            out_specs=[full, full, vec] + [anywhere] * len(out_groups),
            scratch_shapes=[
                pltpu.VMEM((D, n_parts * D), BF16),
                pltpu.VMEM((D, n_parts * D), BF16),
                pltpu.VMEM((rows, D), BF16),
                pltpu.VMEM((rows, D), BF16),
                pltpu.VMEM((2, D, D), BF16),
                pltpu.SemaphoreType.DMA((2, lines)),
                pltpu.SemaphoreType.DMA((2, lines)),
            ],
        ),
        out_shape=[
            jax.ShapeDtypeStruct((rows, D), F32),
            jax.ShapeDtypeStruct((rows, D), F32),
            jax.ShapeDtypeStruct((1, n_parts * D), F32),
        ]
        + [jax.ShapeDtypeStruct((k, D // lines, 2 * n_parts * D), BF16) for k in out_groups],
        compiler_params=params(),
        cost_estimate=pl.CostEstimate(flops=24 * n_parts * rows * D * D, bytes_accessed=30 << 20, transcendentals=0),
        name="ffn",
    )(pos, out_pos, n2, g, bias, *pieces)


def norm_back(grad, xhat, rstd, gain):
    gg = grad * gain
    return rstd * (
        gg - jnp.mean(gg, axis=1, keepdims=True) - xhat * jnp.mean(gg * xhat, axis=1, keepdims=True)
    )


def mid_kernel(lines, n_in, first_col, n_mix, n_part, pos_ref, len_ref, res_ref, g_ref, gain2_ref, down_ref, *rest):
    ys = rest[:n_part]
    gns = rest[n_part : 2 * n_part]
    mixed = rest[2 * n_part : 2 * n_part + n_mix]
    rest = rest[2 * n_part + n_mix :]
    pieces = rest[:n_in]
    long_ref, glob_ref, gres_ref, gmix_ref, small_ref, gw_ref = rest[n_in : n_in + 6]
    w_s, gattn_s, gw_s, sems = rest[n_in + 6 :]
    s = pl.program_id(0)

    @pl.when(s == 0)
    def _():
        for copy in load_rows(pieces, pos_ref, lines, w_s, sems, first_col):
            copy.wait()
        gw_s[...] = jnp.zeros_like(gw_s)
        small_ref[...] = jnp.zeros_like(small_ref)

    live = live_mask(len_ref[s], D)
    res = res_ref[...]
    y = res + down_ref[...]
    gn2 = gns[0][...]
    for ref in ys:
        y = y + ref[...]
    for ref in gns[1:]:
        gn2 = gn2 + ref[...]
    y = jnp.where(live, y, 0.0).astype(BF16)
    glob_ref[0, 0] = y[:GLOB]
    long_ref[0, 0] = y[GLOB:]
    xhat, rstd = norm_stats(res)
    g = g_ref[...].astype(F32)
    gres = g + norm_back(gn2, xhat, rstd, gain2_ref[...])
    gres_ref[...] = gres
    gattn = gres.astype(BF16)
    gattn_s[...] = gattn
    small_ref[0:1] += jnp.sum(gn2 * xhat, axis=0, keepdims=True)
    small_ref[1:2] += jnp.sum(gn2, axis=0, keepdims=True)
    small_ref[2:3] += jnp.sum(gattn.astype(F32), axis=0, keepdims=True)
    small_ref[3:4] += jnp.sum(g, axis=0, keepdims=True)

    for n in range(D // 256):
        c = slice(256 * n, 256 * (n + 1))
        gmix_ref[:, c] = dot(gattn_s[...], w_s[c, :], NT).astype(BF16)
        at = 0
        for m in mixed:
            gw_s[at : at + m.shape[1], c] += dot(m[...], gattn_s[:, c], TN)
            at += m.shape[1]

    @pl.when(s == pl.num_programs(0) - 1)
    def _():
        gw_ref[...] = gw_s[...].astype(BF16)


def mid(pos, lengths, res, g, gain2, down, ys, gns, mixed, pieces, first_col, long_shape, glob_shape):
    rows = res.shape[0]
    n = len(pieces)
    lines = pos.shape[0]
    spec = pl.BlockSpec((T, D), lambda s, *_: (s, 0))
    vec = pl.BlockSpec((1, D), lambda s, *_: (0, 0))
    anywhere = pl.BlockSpec(memory_space=pl.ANY)
    return pl.pallas_call(
        functools.partial(mid_kernel, lines, n, first_col, len(mixed), len(ys)),
        grid_spec=pltpu.PrefetchScalarGridSpec(
            num_scalar_prefetch=2,
            grid=(rows // T,),
            in_specs=[spec, spec, vec, vec]
            + [spec] * (2 * len(ys))
            + [pl.BlockSpec((T, m.shape[1]), lambda s, *_: (s, 0)) for m in mixed]
            + [anywhere] * n,
            out_specs=[
                pl.BlockSpec((1, 1, SEQ, D), lambda s, *_: (s, 0, 0, 0)),
                pl.BlockSpec((1, 1, GLOB, D), lambda s, *_: (s, 0, 0, 0)),
                spec,
                spec,
                pl.BlockSpec((8, D), lambda s, *_: (0, 0)),
                pl.BlockSpec((D, D), lambda s, *_: (0, 0)),
            ],
            scratch_shapes=[
                pltpu.VMEM((D, D), BF16),
                pltpu.VMEM((T, D), BF16),
                pltpu.VMEM((D, D), F32),
                pltpu.SemaphoreType.DMA((lines,)),
            ],
        ),
        out_shape=[
            jax.ShapeDtypeStruct(long_shape, BF16),
            jax.ShapeDtypeStruct(glob_shape, BF16),
            jax.ShapeDtypeStruct((rows, D), F32),
            jax.ShapeDtypeStruct((rows, D), BF16),
            jax.ShapeDtypeStruct((8, D), F32),
            jax.ShapeDtypeStruct((D, D), BF16),
        ],
        compiler_params=params(),
        cost_estimate=pl.CostEstimate(flops=8 * rows * D * D, bytes_accessed=30 << 20, transcendentals=0),
        name="mid",
    )(pos, lengths, res, g, gain2, down, *ys, *gns, *mixed, *pieces)


def weight_kernel(n_rhs, n_out, out_pos_ref, normed_ref, *rest):
    rhs = rest[:n_rhs]
    extra = rest[n_rhs : len(rest) - n_out - 2]
    outs = rest[len(rest) - n_out - 2 : len(rest) - 2]
    gw_s, out_sems = rest[len(rest) - 2 :]
    piece_rows = outs[0].shape[1]
    at = 0
    for ref in rhs:
        for n in range(ref.shape[1] // 128):
            c = slice(128 * n, 128 * (n + 1))
            gw_s[:, at : at + 128] = dot(normed_ref[...], ref[:, c], TN).astype(BF16)
            at += 128
    for ref in extra:
        gw_s[:, at : at + ref.shape[1]] = ref[...].astype(BF16)
        at += ref.shape[1]
    copies = store_rows(gw_s, outs, piece_rows, out_pos_ref, out_sems, 0)
    for copy in copies:
        copy.start()
    for copy in copies:
        copy.wait()


def weight_grad(out_pos, normed, rhs, extra, out_groups):
    rows = normed.shape[0]
    lines = sum(out_groups)
    cols = sum(r.shape[1] for r in rhs) + sum(r.shape[1] for r in extra)
    anywhere = pl.BlockSpec(memory_space=pl.ANY)
    vmem = pl.BlockSpec(memory_space=pltpu.VMEM)
    return pl.pallas_call(
        functools.partial(weight_kernel, len(rhs), len(out_groups)),
        grid_spec=pltpu.PrefetchScalarGridSpec(
            num_scalar_prefetch=1,
            grid=(1,),
            in_specs=[vmem] * (1 + len(rhs) + len(extra)),
            out_specs=[anywhere] * len(out_groups),
            scratch_shapes=[pltpu.VMEM((D, cols), BF16), pltpu.SemaphoreType.DMA((lines,))],
        ),
        out_shape=[jax.ShapeDtypeStruct((k, D // lines, cols), BF16) for k in out_groups],
        compiler_params=params(),
        cost_estimate=pl.CostEstimate(flops=4 * rows * D * cols, bytes_accessed=10 << 20, transcendentals=0),
        name="weight_grad",
    )(out_pos, normed, *rhs, *extra)


def input_kernel(lines, n_in, first_col, n_rhs, pos_ref, hid_ref, gres_ref, gain_ref, *rest):
    grads = rest[:n_rhs]
    pieces = rest[n_rhs : n_rhs + n_in]
    long_ref, glob_ref, small_ref, w_s, sems = rest[n_rhs + n_in :]
    s = pl.program_id(0)

    @pl.when(s == 0)
    def _():
        for copy in load_rows(pieces, pos_ref, lines, w_s, sems, first_col):
            copy.wait()
        small_ref[...] = jnp.zeros_like(small_ref)

    xhat, rstd = norm_stats(hid_ref[...].astype(F32))
    groups = n_rhs // 3
    gn1 = jnp.zeros((T, D), F32)
    for part in range(3):
        at = part * D
        for g in range(groups):
            ref = grads[3 * g + part]
            width = ref.shape[1]
            gn1 = gn1 + dot(ref[...], w_s[:, at : at + width], NT)
            if part != 1:
                row = 2 + part // 2
                first = at - part * D
                small_ref[row : row + 1, first : first + width] += jnp.sum(
                    ref[...].astype(F32), axis=0, keepdims=True
                )
            at += width
    small_ref[0:1] += jnp.sum(gn1 * xhat, axis=0, keepdims=True)
    small_ref[1:2] += jnp.sum(gn1, axis=0, keepdims=True)
    ghid = (gres_ref[...] + norm_back(gn1, xhat, rstd, gain_ref[...])).astype(BF16)
    glob_ref[0, 0] = ghid[:GLOB]
    long_ref[0, 0] = ghid[GLOB:]


def input_grad(pos, hid, gres, gain, grads, pieces, first_col, long_shape, glob_shape):
    rows = hid.shape[0]
    n = len(pieces)
    lines = pos.shape[0]
    spec = pl.BlockSpec((T, D), lambda s, *_: (s, 0))
    vec = pl.BlockSpec((1, D), lambda s, *_: (0, 0))
    anywhere = pl.BlockSpec(memory_space=pl.ANY)
    return pl.pallas_call(
        functools.partial(input_kernel, lines, n, first_col, len(grads)),
        grid_spec=pltpu.PrefetchScalarGridSpec(
            num_scalar_prefetch=1,
            grid=(rows // T,),
            in_specs=[spec, spec, vec]
            + [pl.BlockSpec((T, r.shape[1]), lambda s, *_: (s, 0)) for r in grads]
            + [anywhere] * n,
            out_specs=[
                pl.BlockSpec((1, 1, SEQ, D), lambda s, *_: (s, 0, 0, 0)),
                pl.BlockSpec((1, 1, GLOB, D), lambda s, *_: (s, 0, 0, 0)),
                pl.BlockSpec((8, D), lambda s, *_: (0, 0)),
            ],
            scratch_shapes=[pltpu.VMEM((D, 3 * D), BF16), pltpu.SemaphoreType.DMA((lines,))],
        ),
        out_shape=[
            jax.ShapeDtypeStruct(long_shape, BF16),
            jax.ShapeDtypeStruct(glob_shape, BF16),
            jax.ShapeDtypeStruct((8, D), F32),
        ],
        compiler_params=params(),
        cost_estimate=pl.CostEstimate(flops=12 * rows * D * D, bytes_accessed=20 << 20, transcendentals=0),
        name="input_grad",
    )(pos, hid, gres, gain, *grads, *pieces)


AXES = ("wide", "narrow")


class Links:
    def __init__(self, mesh):
        self.wide = mesh.shape["wide"]
        self.narrow = mesh.shape["narrow"]
        self.count = self.wide * self.narrow
        self.pairwise = self.wide == 8 and self.narrow == 4
        self.lines = self.wide if self.pairwise else 1

    def setup(self):
        if not self.pairwise:
            self.pos = jnp.zeros((1,), jnp.int32)
            return
        w = lax.axis_index("wide")
        self.z = lax.axis_index("narrow")
        near = jnp.where(w % 2 == 0, 2, 4)
        far = 6 - near
        order = [0, near, far, 6, 1, 1 ^ far, 1 ^ near, 7]
        self.pos = jnp.stack([w ^ m for m in order]).astype(jnp.int32)

    def swap(self, x, wide_mask=0, narrow_mask=0):
        masks = wide_mask if isinstance(wide_mask, tuple) else (wide_mask, wide_mask)
        pairs = []
        for w in range(self.wide):
            for z in range(self.narrow):
                pairs.append(
                    (w * self.narrow + z, (w ^ masks[w % 2]) * self.narrow + (z ^ narrow_mask))
                )
        return lax.ppermute(x, AXES, pairs)

    def gather(self, x):
        if not self.pairwise:
            return [lax.all_gather(x, AXES, axis=0, tiled=True)]
        for mask in (1, 2):
            other = self.swap(x, 0, mask)
            low = (self.z & mask) == 0
            x = jnp.concatenate([jnp.where(low, x, other), jnp.where(low, other, x)], axis=0)
        near = self.swap(x, (2, 4))
        own = jnp.concatenate([x, near], axis=0)
        own_core = self.swap(own, 1)
        far = self.swap(own, (4, 2))
        far_core = self.swap(far, 1)
        return [own, far, own_core, far_core]

    def gather_small(self, x):
        if not self.pairwise:
            return lax.all_gather(x, AXES, axis=0, tiled=True)
        pieces = jnp.concatenate(self.gather(x), axis=0).reshape(self.lines, self.narrow, -1)
        place = (self.pos[None, :] == jnp.arange(self.lines)[:, None]).astype(jnp.bfloat16)
        flat = pieces.reshape(self.lines, -1)
        return jnp.dot(place, flat, preferred_element_type=jnp.float32).reshape(self.count, -1)

    def groups(self):
        return (2, 2, 2, 2) if self.pairwise else (1,)

    def add(self, *parts):
        total = parts[0].astype(F32)
        for p in parts[1:]:
            total = total + p.astype(F32)
        return total

    def sum(self, parts):
        if not self.pairwise:
            return lax.psum_scatter(parts[0][0].astype(F32), AXES, scatter_dimension=0, tiled=True)
        kind = parts[0].dtype
        keep_a, keep_b, send_a, send_b = parts
        got_b = self.swap(send_b, 1)
        got_a = self.swap(send_a, 1)
        far = self.swap(self.add(keep_b, got_b).astype(kind), (4, 2))
        near = self.swap(self.add(keep_a[1], got_a[1], far[1]).astype(kind), (2, 4))
        x = self.add(keep_a[0], got_a[0], far[0], near)
        for mask in (2, 1):
            half = x.shape[0] // 2
            low = (self.z & mask) == 0
            mine = jnp.where(low, x[:half], x[half:])
            theirs = jnp.where(low, x[half:], x[:half])
            x = mine + self.swap(theirs.astype(kind), 0, mask).astype(F32)
        return x

    def sum_small(self, x):
        if not self.pairwise:
            return lax.psum_scatter(x, AXES, scatter_dimension=0, tiled=True)
        blocks = x.reshape(self.lines, self.narrow, -1)
        blocks = jnp.take(blocks, self.pos, axis=0)
        return self.sum([blocks[0:2], blocks[2:4], blocks[4:6], blocks[6:8]])


GROUPS = 2
CHUNKS = 2
PARTS = FF // D


def row_vector(v):
    return v.astype(F32).reshape(1, -1)


def body(links, long_in, glob_in, lengths, ln1_gain, ln1_bias, w_qkv, qv_bias, rel_embed, w_out, out_bias, ln2_gain, ln2_bias, w_in, in_bias, w_down, down_bias, cot_long, cot_glob):
    links.setup()
    pos = links.pos
    groups = links.groups()
    count = links.count
    micro = long_in.shape[0]
    r = w_qkv.shape[0]
    smalls = [ln1_gain, ln1_bias, qv_bias, out_bias, ln2_gain, ln2_bias, down_bias, in_bias]
    sizes = [v.shape[0] for v in smalls]

    rel = jnp.pad(rel_embed, ((0, 0), (LEAD, LABELS - LEAD - RELS)))
    attn_packed = jnp.concatenate([w_qkv, w_out, rel], axis=1)
    w_in_parts = w_in.reshape(r, count, PARTS, r).transpose(2, 0, 1, 3).reshape(PARTS, r, D)
    w_down_parts = w_down.reshape(PARTS, r, D)
    per = PARTS // CHUNKS
    ffn_packed = []
    for c in range(CHUNKS):
        which = range(per * c, per * (c + 1))
        ffn_packed.append(
            jnp.concatenate([w_in_parts[i] for i in which] + [w_down_parts[i] for i in which], axis=1)
        )

    small_all = links.gather_small(jnp.concatenate(smalls).reshape(1, -1))
    attn = links.gather(attn_packed)
    ffns = [links.gather(x) for x in ffn_packed]

    at = 0
    whole = []
    for n in sizes:
        whole.append(small_all[:, at : at + n])
        at += n
    gain1, bias1, qv, out_b, gain2, bias2, down_b = [row_vector(v) for v in whole[:7]]
    in_b = row_vector(whole[7].reshape(count, PARTS, r).transpose(1, 0, 2))
    full_bias = jnp.concatenate([qv[:, :D], jnp.zeros((1, D), F32), qv[:, D:]], axis=1)

    hid = jnp.concatenate([glob_in, long_in], axis=2).reshape(micro * T, D)
    cot = jnp.concatenate([cot_glob, cot_long], axis=2).reshape(micro * T, D)
    lens = lengths.reshape(micro)

    normed, proj, rel_all, rel_turned = project(pos, hid, gain1, bias1, full_bias, attn, 0, 4 * D)
    pairs = PAIRS // GROUPS
    heads = [attend(lens, proj, rel_all, pairs * g, pairs) for g in range(GROUPS)]
    mixed = [h[0] for h in heads]
    res, n2, g_ffn = mix_out(pos, lens, hid, out_b, gain2, bias2, cot, mixed, attn, 3 * D)
    ys, gns, gbs, w_sums = [], [], [], []
    for c in range(CHUNKS):
        cols = slice(per * c * D, per * (c + 1) * D)
        out = ffn(pos, pos, n2, g_ffn, in_b[:, cols], ffns[c], 0, per * D, per, groups)
        ys.append(out[0])
        gns.append(out[1])
        gbs.append(out[2])
        w_sums.append(links.sum(out[3:]))
    block_long, block_glob, gres, gmix, small2, gw_out = mid(
        pos, lens, res, g_ffn, gain2, down_b, ys, gns, mixed, attn, 3 * D, long_in.shape, glob_in.shape
    )
    grads, grels, a_sums = [], [], []
    for g in range(GROUPS):
        out = attend_back(proj, rel_turned, gmix, mixed[g], heads[g][1], heads[g][2], pairs * g, pairs, 0)
        grads.append(out[:3])
        grels.append(out[3])
        extra = []
        if g == 0:
            extra.append(gw_out)
        if g == GROUPS - 1:
            extra.append(jnp.concatenate(grels, axis=0))
        a_sums.append(links.sum(weight_grad(pos, normed, grads[g], extra, groups)))
    grad_long, grad_glob, small1 = input_grad(
        pos, hid, gres, gain1, [t for gr in grads for t in gr], attn, 0, long_in.shape, glob_in.shape
    )
    gin = jnp.concatenate(gbs, axis=1).reshape(PARTS, count, r).transpose(1, 0, 2).reshape(count, -1)
    small_parts = [
        small1[0].reshape(count, -1),
        small1[1].reshape(count, -1),
        small1[2:4].reshape(count, -1),
        small2[2].reshape(count, -1),
        small2[0].reshape(count, -1),
        small2[1].reshape(count, -1),
        small2[3].reshape(count, -1),
        gin,
    ]
    small_sum = links.sum_small(jnp.concatenate(small_parts, axis=1)).reshape(-1)
    small_grads = []
    at = 0
    for n in sizes:
        small_grads.append(small_sum[at : at + n])
        at += n
    g_gain1, g_bias1, g_qv, g_out_b, g_gain2, g_bias2, g_down_b, g_in_b = small_grads

    width = pairs * 128
    g_qkv = jnp.concatenate(
        [a_sums[g][:, width * n : width * (n + 1)] for n in range(3) for g in range(GROUPS)], axis=1
    )
    g_out = a_sums[0][:, 3 * width : 3 * width + D]
    at = 3 * width + (D if GROUPS == 1 else 0) + BACK_LEAD
    g_rel = a_sums[-1][:, at : at + RELS]
    g_in = jnp.stack(
        [w_sums[c][:, D * i : D * (i + 1)] for c in range(CHUNKS) for i in range(per)], axis=0
    )
    g_in = g_in.reshape(PARTS, r, count, r).transpose(1, 2, 0, 3).reshape(r, FF)
    g_down = jnp.concatenate(
        [w_sums[c][:, D * (per + i) : D * (per + i + 1)] for c in range(CHUNKS) for i in range(per)], axis=0
    )
    return (
        block_long, block_glob, grad_long, grad_glob,
        g_gain1, g_bias1, g_qkv, g_qv, g_rel, g_out, g_out_b,
        g_gain2, g_bias2, g_in, g_in_b, g_down, g_down_b,
    )


def solution(mesh):
    rows = P(None, AXES, None, None)
    vec = P(AXES)
    mat = P(AXES, None)
    placed = (rows, rows, P(None, AXES), vec, vec, mat, vec, mat, mat, vec, vec, vec, mat, vec, mat, vec, rows, rows)
    return jax.shard_map(
        functools.partial(body, Links(mesh)),
        mesh=mesh,
        in_specs=placed,
        out_specs=(rows, rows, rows, rows, vec, vec, mat, vec, mat, mat, vec, vec, vec, mat, vec, mat, vec),
        check_vma=False,
    )
```

```python
import functools
import jax
import jax.numpy as jnp
from jax import lax
from jax.experimental import pallas as pl
from jax.experimental.pallas import tpu as pltpu
from jax.sharding import PartitionSpec as P

HEAD_DIM = 64
RADIUS = 84
STRIDE = 16
SEQ = 512
GLOB = 32
RELS = 169
T = GLOB + SEQ
D = 768
FF = 3072
PAIRS = 6
LABELS = 256
LEAD = 4
BACK_LEAD = 3
LABEL_END = LEAD + RELS
EPS = 1e-06
NEG = -1e30
F32 = jnp.float32
BF16 = jnp.bfloat16
VMEM_LIMIT = 63 << 20
WINDOWS = ((0, 0, 256, 328, 0), (0, 0, 384, 72, 0), (1, 160, 384, 8, 352), (1, 288, 256, 8, 224))
OFFSETS = (0, 256, 640, 1024)
WAYS = 3 * 128
VEC_AT = 176
GAIN1, BIAS1, QV, OUT_B, GAIN2, BIAS2, DOWN_B, IN_B, VECS = 0, 1, 2, 4, 5, 6, 7, 8, 16
P_COLS = 1280
NN = (((1,), (0,)), ((), ()))
NT = (((1,), (1,)), ((), ()))
TN = (((0,), (0,)), ((), ()))


def dot(a, b, dims=NN):
    return lax.dot_general(a, b, dims, preferred_element_type=F32)


def run(kernel, deps, prefetch, inputs, out_shape, name, cost, grid, in_specs, out_specs, scratch_shapes):
    n = len(prefetch)

    def with_deps(*refs):
        kernel(*refs[:n], *refs[n + len(deps) :])

    anywhere = pl.BlockSpec(memory_space=pl.ANY)
    return pl.pallas_call(
        with_deps,
        grid_spec=pltpu.PrefetchScalarGridSpec(
            num_scalar_prefetch=n,
            grid=grid,
            in_specs=[anywhere] * len(deps) + in_specs,
            out_specs=out_specs,
            scratch_shapes=scratch_shapes,
        ),
        out_shape=out_shape,
        compiler_params=pltpu.CompilerParams(vmem_limit_bytes=VMEM_LIMIT),
        cost_estimate=pl.CostEstimate(flops=int(cost * 1.15e9), bytes_accessed=1 << 20, transcendentals=0),
        name=name,
    )(*prefetch, *deps, *inputs)


def after(x, deps):
    anywhere = pl.BlockSpec(memory_space=pl.ANY)
    return pl.pallas_call(
        lambda *refs: None,
        in_specs=[anywhere] * (1 + len(deps)),
        out_specs=anywhere,
        out_shape=jax.ShapeDtypeStruct(x.shape, x.dtype),
        input_output_aliases={0: 0},
        name="after",
    )(x, *deps)


def iota(shape, dim):
    return lax.broadcasted_iota(jnp.int32, shape, dim)


def norm_stats(x):
    cen = x - jnp.mean(x, axis=1, keepdims=True)
    rstd = lax.rsqrt(jnp.mean(cen * cen, axis=1, keepdims=True) + EPS)
    return cen * rstd, rstd


def norm_back(grad, xhat, rstd, gain):
    gg = grad * gain
    return rstd * (
        gg - jnp.mean(gg, axis=1, keepdims=True) - xhat * jnp.mean(gg * xhat, axis=1, keepdims=True)
    )


def tiles(cols, size=256):
    return [slice(at, min(at + size, cols)) for at in range(0, cols, size)]


def live_mask(length, cols):
    row = iota((T, cols), 0)
    glob_count = (length + STRIDE - 1) // STRIDE
    return row < jnp.where(row < GLOB, glob_count, length + GLOB)


def load_rows(pieces, pos_ref, lines, dst, sems, first_col):
    rows = dst.shape[0] // lines
    cols = dst.shape[1]
    copies = []
    k = 0
    for piece in pieces:
        for i in range(piece.shape[0] // rows):
            start = pl.multiple_of(pos_ref[k] * rows, 16)
            copies.append(
                pltpu.make_async_copy(
                    piece.at[pl.ds(i * rows, rows), pl.ds(first_col, cols)],
                    dst.at[pl.ds(start, rows), :],
                    sems.at[k],
                )
            )
            k += 1
    for copy in copies:
        copy.start()
    return copies


FIRST = 2 * 128
SECOND = D - FIRST


def owner_order(rows):
    k = iota((D, 1), 0)
    late = (k >= D // 2).astype(jnp.int32)
    k = k - late * (D // 2)
    owner = ((k.astype(F32) + 0.5) * (1.0 / rows)).astype(jnp.int32)
    col = rows * owner + k + late * rows
    return (iota((D, D), 1) == col).astype(F32).astype(BF16)


def project_kernel(lines, n_pieces, first, rows, pos_ref, *rest):
    if first:
        long_ref, glob_ref = rest[:2]
    else:
        normed_ref, vec_ref = rest[:2]
    pieces = rest[2 : 2 + n_pieces]
    if first:
        proj_ref, normed_ref, rel_ref, relt_ref, vec_ref, w_s, sems = rest[2 + n_pieces :]
    else:
        proj_ref, w_s, sems = rest[2 + n_pieces :]
    cols = proj_ref.shape[1]
    width = cols // 3
    copies = load_rows(pieces, pos_ref, lines, w_s, sems.at[0], 0)
    if first:
        for copy in load_rows(pieces, pos_ref, lines, rel_ref, sems.at[1], cols):
            copy.wait()
        turned = rel_ref[...].astype(F32).T
        vec_ref[...] = turned[VEC_AT : VEC_AT + VECS]
        drop = LEAD - BACK_LEAD
        labels = jnp.concatenate([turned[drop:], turned[:drop]], axis=0)
        label = iota((LABELS, D), 0) - BACK_LEAD
        relt_ref[...] = jnp.where((label >= 0) & (label < RELS), labels, 0.0).astype(BF16)
        a, b = vec_ref[QV : QV + 1], vec_ref[QV + 1 : QV + 2]
        half = D // 2
        sides = jnp.concatenate(
            [
                jnp.concatenate([a[:, :half], b[:, :half]], axis=1),
                jnp.concatenate([a[:, half:], b[:, half:]], axis=1),
            ],
            axis=0,
        )
        vec_ref[QV : QV + 2] = dot(sides.astype(BF16), owner_order(rows))
        for s in range(long_ref.shape[0]):
            for part, at, size in ((glob_ref, T * s, GLOB), (long_ref, T * s + GLOB, SEQ)):
                xhat, _ = norm_stats(part[s, 0].astype(F32))
                normed_ref[at : at + size] = (
                    xhat * vec_ref[GAIN1 : GAIN1 + 1] + vec_ref[BIAS1 : BIAS1 + 1]
                ).astype(BF16)
    own = slice(0, width) if first else slice(D - width, D)
    full_bias = jnp.concatenate(
        [vec_ref[QV : QV + 1, own], jnp.zeros((1, width), F32), vec_ref[QV + 1 : QV + 2, own]], axis=1
    )
    for copy in copies:
        copy.wait()
    for c in tiles(cols):
        out = (dot(normed_ref[...], w_s[:, c]) + full_bias[:, c]).astype(BF16)
        for at in range(c.start, c.stop, 128):
            to = by_pair(at, width)
            proj_ref[:, to : to + 128] = out[:, at - c.start : at - c.start + 128]


def by_pair(col, width):
    return WAYS * (col % width // 128) + 128 * (col // width)


VMEM = pl.BlockSpec(memory_space=pltpu.VMEM)
ANY = pl.BlockSpec(memory_space=pl.ANY)


def project_first(deps, pos, long_in, glob_in, pieces, owned, cols):
    rows = long_in.shape[0] * T
    lines = pos.shape[0]
    shape = lambda *dims: jax.ShapeDtypeStruct(dims, BF16)
    return run(
        functools.partial(project_kernel, lines, len(pieces), True, owned),
        deps,
        [pos],
        [long_in, glob_in, *pieces],
        [
            shape(rows, cols),
            shape(rows, D),
            shape(D, LABELS),
            shape(LABELS, D),
            jax.ShapeDtypeStruct((VECS, D), F32),
        ],
        "project",
        9,
        grid=(1,),
        in_specs=[VMEM] * 2 + [ANY] * len(pieces),
        out_specs=[VMEM] * 5,
        scratch_shapes=[pltpu.VMEM((D, cols), BF16), pltpu.SemaphoreType.DMA((2, lines))],
    )


def project_next(deps, pos, normed, vec, pieces, cols):
    rows = normed.shape[0]
    lines = pos.shape[0]
    return run(
        functools.partial(project_kernel, lines, len(pieces), False, 0),
        deps,
        [pos],
        [normed, vec, *pieces],
        [jax.ShapeDtypeStruct((rows, cols), BF16)],
        "project",
        8,
        grid=(1,),
        in_specs=[VMEM] * 2 + [ANY] * len(pieces),
        out_specs=[VMEM],
        scratch_shapes=[pltpu.VMEM((D, cols), BF16), pltpu.SemaphoreType.DMA((2, lines))],
    )[0]


def flip_matrix(size):
    row, col = iota((size, size), 0), iota((size, size), 1)
    return ((row // 128 == col // 128) & (row % 128 + col % 128 == 127)).astype(F32).astype(BF16)


def by_head(x):
    even = iota(x.shape, 1) < HEAD_DIM
    return jnp.concatenate([jnp.where(even, x, 0.0), jnp.where(even, 0.0, x)], axis=0)


def by_lane(x):
    half = x.shape[0] // 2
    even = iota((half, x.shape[1]), 1) < HEAD_DIM
    return jnp.where(even, x[:half], x[half:])


def spread(x, b):
    _, _, width, shift, _ = WINDOWS[b]
    shift = shift if shift < 256 else shift - 384
    lane = iota((64, 128), 1)
    none = jnp.full((64, 128), NEG, F32)
    parts = []
    for at in range(0, 256, 64):
        start = shift + at % 128
        turned = pltpu.roll(x[at : at + 64], start % 256, 1, stride=1, stride_axis=0)
        low, high = turned[:, :128], turned[:, 128:]
        if start < 0:
            cols = [low, jnp.where(lane < 64, high, NEG), none]
        elif start + 64 + LABEL_END <= 256:
            cols = [low, high, none]
        elif start >= 128:
            cols = [none, high, low]
        else:
            cols = [jnp.where(lane >= 64, low, NEG), high, jnp.where(lane < 64, low, NEG)]
        parts.append(jnp.concatenate(cols[: width // 128], axis=1))
    return jnp.concatenate(parts, axis=0)


def collect(cols, b):
    _, _, width, shift, _ = WINDOWS[b]
    shift = shift if shift < 256 else shift - 384
    lane = iota((64, 128), 1)
    parts = []
    for at in range(0, 256, 64):
        start = shift + 64 - at % 128
        tiles_ = [c[at : at + 64] for c in cols]
        if start < 0:
            low, high = tiles_[0], jnp.where(lane < 64, tiles_[1], 0.0)
        elif start + 64 + LABEL_END <= 256:
            low, high = tiles_[0], tiles_[1]
        elif start >= 128:
            low, high = tiles_[2], tiles_[1]
        elif len(tiles_) > 2:
            low, high = jnp.where(lane >= 64, tiles_[0], tiles_[2]), tiles_[1]
        else:
            low, high = jnp.where(lane >= 64, tiles_[0], 0.0), tiles_[1]
        back = (BACK_LEAD - LEAD - 63 - start) % 256
        parts.append(
            pltpu.roll(jnp.concatenate([low, high], axis=1), back, 1, stride=1, stride_axis=0)
        )
    return jnp.concatenate(parts, axis=0)


def zero_glob(x, at):
    cols = [x[:, 128 * i : 128 * (i + 1)] for i in range(x.shape[1] // 128)]
    lane = iota(cols[0].shape, 1) - at % 128
    cols[at // 128] = jnp.where((lane >= 0) & (lane < GLOB), 0.0, cols[at // 128])
    return cols


def attend_kernel(len_ref, qkv_ref, rel_ref, mix_ref, inv_ref, p_ref, pg_ref, k_s, v_s, rel_s):
    dead = jnp.where(live_mask(len_ref[pl.program_id(0)], 128), 0.0, NEG)
    flag = iota((T, 128), 1) == 0
    k = jnp.concatenate(
        [qkv_ref[:, 128:256], jnp.where(flag, dead, 0.0).astype(BF16)], axis=1
    )
    v = jnp.concatenate([qkv_ref[:, 256:384], jnp.ones((T, 128), BF16)], axis=1)
    for s, m in ((k_s, k), (v_s, v)):
        s[0] = m
        s[1, :SEQ] = m[GLOB:]
        s[1, SEQ:] = m[:GLOB]
    label = iota((128, LABELS), 1)
    outside = ((label < LEAD) | (label >= LEAD + RELS)) & (iota((128, LABELS), 0) == 0)
    rel_s[:128] = rel_ref[...]
    rel_s[128:] = jnp.where(outside, NEG, 0.0).astype(BF16)
    flip = flip_matrix(256)

    def queries(rows):
        x = by_head(qkv_ref[rows, :128].astype(F32) * 0.125)
        one = (iota(x.shape, 1) == 0).astype(F32)
        return jnp.concatenate([x, one], axis=1).astype(BF16)

    def weights(scores):
        return jnp.exp(scores - jnp.max(scores, axis=1, keepdims=True)).astype(BF16)

    rows = [slice(0, GLOB)] + [slice(GLOB + 128 * b, GLOB + 128 * (b + 1)) for b in range(4)]
    wins = [(0, slice(0, T))] + [(arr, slice(first, first + width)) for arr, first, width, _, _ in WINDOWS]
    qs = [queries(r) for r in rows]
    scores = [dot(q, k_s[arr, win], NT) for q, (arr, win) in zip(qs, wins)]
    biases = [dot(q, rel_s[...]) for q in qs[1:]]
    for b, window in enumerate(WINDOWS):
        bias = zero_glob(spread(biases[b], b), window[-1])
        scores[b + 1] = scores[b + 1] + jnp.concatenate(bias, axis=1)
    ps = [weights(x) for x in scores]
    pg_ref[0, 0] = ps[0]
    outs = [dot(p, v_s[arr, win]) for p, (arr, win) in zip(ps, wins)]
    turned = [dot(flip, p) for p in ps[1:]]
    for r, out in zip(rows, outs):
        inv = by_lane(1.0 / out[:, 128:])
        inv_ref[r] = inv
        mix_ref[r] = (by_lane(out[:, :128]) * inv).astype(BF16)
    for b, p in enumerate(turned):
        p_ref[0, 0, :, OFFSETS[b] : OFFSETS[b] + p.shape[1]] = p.astype(BF16)


def attend(deps, lengths, proj, rel, first_pair):
    rows = proj.shape[0]
    seqs = rows // T
    pairs = proj.shape[1] // WAYS
    return run(
        attend_kernel,
        deps,
        [lengths],
        [proj, rel],
        [
            jax.ShapeDtypeStruct((rows, pairs * 128), BF16),
            jax.ShapeDtypeStruct((rows, pairs * 128), F32),
            jax.ShapeDtypeStruct((seqs, pairs, 256, P_COLS), BF16),
            jax.ShapeDtypeStruct((seqs, pairs, 2 * GLOB, T), BF16),
        ],
        "attend",
        6.2 * pairs,
        grid=(seqs, pairs),
        in_specs=[
            pl.BlockSpec((T, WAYS), lambda s, p, *_: (s, p)),
            pl.BlockSpec((128, LABELS), lambda s, p, *_: (first_pair + p, 0)),
        ],
        out_specs=[
            pl.BlockSpec((T, 128), lambda s, p, *_: (s, p)),
            pl.BlockSpec((T, 128), lambda s, p, *_: (s, p)),
            pl.BlockSpec((1, 1, 256, P_COLS), lambda s, p, *_: (s, p, 0, 0)),
            pl.BlockSpec((1, 1, 2 * GLOB, T), lambda s, p, *_: (s, p, 0, 0)),
        ],
        scratch_shapes=[
            pltpu.VMEM((2, T, 256), BF16),
            pltpu.VMEM((2, T, 256), BF16),
            pltpu.VMEM((256, LABELS), BF16),
        ],
    )


def attend_back_kernel(qkv_ref, relt_ref, do_ref, o_ref, inv_ref, p_ref, pg_ref, grad_ref, grel_ref, gk_s, gv_s, k_s, v_s):
    k = qkv_ref[:, 128:256]
    v = qkv_ref[:, 256:384]
    for s, m in ((k_s, k), (v_s, v)):
        s[0] = m
        s[1, :SEQ] = m[GLOB:]
        s[1, SEQ:] = m[:GLOB]
    flip = flip_matrix(128)

    @pl.when(pl.program_id(1) == 0)
    def _():
        grel_ref[...] = jnp.zeros_like(grel_ref)

    ones = jnp.ones((256, 128), BF16)

    def score_grads(do, o, p, v_win):
        prod = by_head(do * o)
        high = prod.astype(BF16)
        low = (prod - high.astype(F32)).astype(BF16)
        centre = dot(jnp.concatenate([high, low], axis=1), ones)
        dom = by_head(do).astype(BF16)
        dp = dot(dom, v_win, NT)
        width = dp.shape[1]
        cols = [dp[:, c] - centre[:, : c.stop - c.start] for c in tiles(width, 128)]
        return dom, p.astype(F32) * jnp.concatenate(cols, axis=1)

    do = (do_ref[:GLOB].astype(F32) * inv_ref[:GLOB]).astype(BF16).astype(F32)
    p = pg_ref[0, 0]
    dom, ds = score_grads(do, o_ref[:GLOB].astype(F32), p, v_s[0])
    ds = ds.astype(BF16)
    qm = by_head(qkv_ref[:GLOB, :128].astype(F32)).astype(BF16)
    grad_ref[:GLOB, :128] = (by_lane(dot(ds, k_s[0])) * 0.125).astype(BF16)
    gk_s[...] = dot(ds, qm, TN)
    gv_s[...] = dot(p, dom, TN)
    blocks = range(4)
    rows = [slice(GLOB + 128 * b, GLOB + 128 * (b + 1)) for b in blocks]
    wins = [(arr, slice(first, first + width)) for arr, first, width, _, _ in WINDOWS]
    turned = [
        dot(
            flip,
            jnp.concatenate(
                [
                    qkv_ref[r, :128],
                    (do_ref[r].astype(F32) * inv_ref[r]).astype(BF16),
                    o_ref[r],
                ],
                axis=1,
            ),
        )
        for r in rows
    ]
    qms = [by_head(x[:, :128]) for x in turned]
    qm_ts = [x.T.astype(BF16) for x in qms]
    qms = [x.astype(BF16) for x in qms]
    ps = [p_ref[0, 0, :, OFFSETS[b] : OFFSETS[b] + WINDOWS[b][2]] for b in blocks]
    grads = [
        score_grads(x[:, 128:256], x[:, 256:], p, v_s[arr, win])
        for x, p, (arr, win) in zip(turned, ps, wins)
    ]
    doms = [dom for dom, _ in grads]
    dss = [ds.astype(BF16) for _, ds in grads]
    labs = []
    for b, window in enumerate(WINDOWS):
        labs.append(collect(zero_glob(grads[b][1], window[-1]), b).astype(BF16))
    gqs = [
        by_lane(dot(ds, k_s[arr, win]) + dot(lab, relt_ref[...])) * 0.125
        for ds, lab, (arr, win) in zip(dss, labs, wins)
    ]
    gks = [dot(ds, qm, TN) for ds, qm in zip(dss, qms)]
    gvs = [dot(p, dom, TN) for p, dom in zip(ps, doms)]
    grel = sum(dot(qm_t, lab) for qm_t, lab in zip(qm_ts, labs))
    grel_ref[...] += grel * 0.125
    for r, gq in zip(rows, gqs):
        grad_ref[r, :128] = dot(flip, gq.astype(BF16)).astype(BF16)
    for b, (arr, first, width, _, _) in enumerate(WINDOWS):
        win = wins[b][1]
        for acc, part in ((gk_s, gks[b]), (gv_s, gvs[b])):
            if arr == 0:
                acc[win] += part
            else:
                acc[GLOB + first : T] += part[: width - GLOB]
                acc[:GLOB] += part[width - GLOB :]
    grad_ref[:, 128:256] = (gk_s[...] * 0.125).astype(BF16)
    grad_ref[:, 256:384] = gv_s[...].astype(BF16)


def attend_back(deps, proj, relt, gmixed, mixed, inv, p, pg, first_pair, start, pairs):
    rows = proj.shape[0]
    seqs = rows // T
    return run(
        attend_back_kernel,
        deps,
        [],
        [proj, relt, gmixed, mixed, inv, p, pg],
        [
            jax.ShapeDtypeStruct((rows, pairs * WAYS), BF16),
            jax.ShapeDtypeStruct((pairs * 128, LABELS), F32),
        ],
        "attend_back",
        8 * pairs,
        grid=(pairs, seqs),
        in_specs=[
            pl.BlockSpec((T, WAYS), lambda p, s: (s, start + p)),
            pl.BlockSpec((LABELS, 128), lambda p, s: (0, first_pair + start + p)),
            pl.BlockSpec((T, 128), lambda p, s: (s, first_pair + start + p)),
            pl.BlockSpec((T, 128), lambda p, s: (s, start + p)),
            pl.BlockSpec((T, 128), lambda p, s: (s, start + p)),
            pl.BlockSpec((1, 1, 256, P_COLS), lambda p, s: (s, start + p, 0, 0)),
            pl.BlockSpec((1, 1, 2 * GLOB, T), lambda p, s: (s, start + p, 0, 0)),
        ],
        out_specs=[pl.BlockSpec((T, WAYS), lambda p, s: (s, p)), pl.BlockSpec((128, LABELS), lambda p, s: (p, 0))],
        scratch_shapes=[
            pltpu.VMEM((T, 128), F32),
            pltpu.VMEM((T, 128), F32),
            pltpu.VMEM((2, T, 128), BF16),
            pltpu.VMEM((2, T, 128), BF16),
        ],
    )


def mix_out_kernel(lines, n_pieces, first_col, n_mix, pos_ref, len_ref, long_ref, glob_ref, clong_ref, cglob_ref, vec_ref, *rest):
    mixed = rest[:n_mix]
    pieces = rest[n_mix : n_mix + n_pieces]
    res_ref, n2_ref, g_ref, w_s, sems = rest[n_mix + n_pieces :]
    copies = load_rows(pieces, pos_ref, lines, w_s, sems, first_col)
    seqs = long_ref.shape[0]
    for s in range(seqs):
        live = live_mask(len_ref[s], D)
        at = T * s
        g_ref[at : at + GLOB] = jnp.where(live[:GLOB], cglob_ref[s, 0].astype(F32), 0.0).astype(BF16)
        g_ref[at + GLOB : at + T] = jnp.where(live[GLOB:], clong_ref[s, 0].astype(F32), 0.0).astype(BF16)
    for copy in copies:
        copy.wait()
    for c in tiles(D):
        acc = vec_ref[OUT_B : OUT_B + 1, c]
        at = 0
        for m in mixed:
            acc = acc + dot(m[...], w_s[at : at + m.shape[1], c])
            at += m.shape[1]
        res_ref[:, c] = acc
    for s in range(seqs):
        for part, at, size in ((glob_ref, T * s, GLOB), (long_ref, T * s + GLOB, SEQ)):
            res = res_ref[at : at + size] + part[s, 0].astype(F32)
            res_ref[at : at + size] = res
            xhat, _ = norm_stats(res)
            n2_ref[at : at + size] = (
                xhat * vec_ref[GAIN2 : GAIN2 + 1] + vec_ref[BIAS2 : BIAS2 + 1]
            ).astype(BF16)


def mix_out(deps, pos, lengths, long_in, glob_in, cot_long, cot_glob, vec, mixed, pieces, first_col):
    rows = long_in.shape[0] * T
    lines = pos.shape[0]
    return run(
        functools.partial(mix_out_kernel, lines, len(pieces), first_col, len(mixed)),
        deps,
        [pos, lengths],
        [long_in, glob_in, cot_long, cot_glob, vec, *mixed, *pieces],
        [
            jax.ShapeDtypeStruct((rows, D), F32),
            jax.ShapeDtypeStruct((rows, D), BF16),
            jax.ShapeDtypeStruct((rows, D), BF16),
        ],
        "mix_out",
        10,
        grid=(1,),
        in_specs=[VMEM] * (5 + len(mixed)) + [ANY] * len(pieces),
        out_specs=[VMEM] * 3,
        scratch_shapes=[pltpu.VMEM((D, D), BF16), pltpu.SemaphoreType.DMA((lines,))],
    )


def store_rows(src, outs, rows, src_pos_ref, sems, first_col):
    cols = src.shape[1]
    copies = []
    k = 0
    for out in outs:
        for i in range(out.shape[0]):
            start = pl.multiple_of(src_pos_ref[k] * rows, 16)
            copies.append(
                pltpu.make_async_copy(
                    src.at[pl.ds(start, rows), :], out.at[i, :, pl.ds(first_col, cols)], sems.at[k]
                )
            )
            k += 1
    return copies


def gelu_parts(v):
    cdf = 0.5 * (1.0 + lax.erf(v * 0.7071067811865476))
    pdf = jnp.exp(v * v * -0.5) * 0.3989422804014327
    return v * cdf, cdf + v * pdf


def ffn_kernel(lines, n_in, n_parts, n_out, first, pos_ref, n2_ref, g_ref, vec_ref, *rest):
    pieces = rest[:n_in]
    y_ref, gn2_ref, gb_ref = rest[n_in : n_in + 3]
    outs = rest[n_in + 3 : n_in + 3 + n_out]
    w_in_s, w_down_s, act_s, gpre_s, gw_s, sems, out_sems = rest[n_in + 3 + n_out :]
    part = pl.program_id(0)
    piece_rows = outs[0].shape[1]

    @pl.when(part == 0)
    def _():
        copies = []
        for i in range(n_parts):
            copies += load_rows(pieces, pos_ref, lines, w_in_s.at[i], sems.at[2 * i], (2 * first + i) * D)
            copies += load_rows(pieces, pos_ref, lines, w_down_s.at[i], sems.at[2 * i + 1], (2 * first + n_parts + i) * D)
        for copy in copies:
            copy.wait()

    for c in tiles(D):
        pre = dot(n2_ref[...], w_in_s[part, :, c]) + vec_ref[pl.ds(IN_B + first + part, 1), c]
        act, slope = gelu_parts(pre)
        act_s[:, c] = act.astype(BF16)
        gpre = (dot(g_ref[...], w_down_s[part, c, :], NT) * slope).astype(BF16)
        gpre_s[:, c] = gpre
        gb_ref[:, c] = jnp.sum(gpre.astype(F32), axis=0, keepdims=True)

    def flush(which):
        first = pl.multiple_of((which * n_parts + part) * D, 128)
        return store_rows(gw_s.at[which], outs, piece_rows, pos_ref, out_sems.at[which], first)

    for which, (lhs, rhs) in enumerate(((n2_ref, gpre_s), (act_s, g_ref))):
        for c in tiles(D):
            gw_s[which, :, c] = dot(lhs[...], rhs[:, c], TN).astype(BF16)
        for copy in flush(which):
            copy.start()

    def outputs(add):
        for c in tiles(D):
            y = dot(act_s[...], w_down_s[part, :, c])
            gn2 = dot(gpre_s[...], w_in_s[part, c, :], NT)
            y_ref[:, c] = y_ref[:, c] + y if add else y
            gn2_ref[:, c] = gn2_ref[:, c] + gn2 if add else gn2

    pl.when(part == 0)(lambda: outputs(False))
    if n_parts > 1:
        pl.when(part > 0)(lambda: outputs(True))
    for which in range(2):
        for copy in flush(which):
            copy.wait()


def ffn(deps, pos, n2, g, vec, pieces, first, n_parts, out_groups):
    rows = n2.shape[0]
    lines = pos.shape[0]
    full = pl.BlockSpec((rows, D), lambda q, *_: (0, 0))
    return run(
        functools.partial(ffn_kernel, lines, len(pieces), n_parts, len(out_groups), first),
        deps,
        [pos],
        [n2, g, vec, *pieces],
        [
            jax.ShapeDtypeStruct((rows, D), F32),
            jax.ShapeDtypeStruct((rows, D), F32),
            jax.ShapeDtypeStruct((1, n_parts * D), F32),
        ]
        + [jax.ShapeDtypeStruct((k, D // lines, 2 * n_parts * D), BF16) for k in out_groups],
        "ffn",
        28,
        grid=(n_parts,),
        in_specs=[full, full, VMEM] + [ANY] * len(pieces),
        out_specs=[full, full, pl.BlockSpec((1, D), lambda q, *_: (0, q))] + [ANY] * len(out_groups),
        scratch_shapes=[
            pltpu.VMEM((n_parts, D, D), BF16),
            pltpu.VMEM((n_parts, D, D), BF16),
            pltpu.VMEM((rows, D), BF16),
            pltpu.VMEM((rows, D), BF16),
            pltpu.VMEM((2, D, D), BF16),
            pltpu.SemaphoreType.DMA((2 * n_parts, lines)),
            pltpu.SemaphoreType.DMA((2, lines)),
        ],
    )


def mid_kernel(lines, n_in, first_col, n_mix, n_part, pos_ref, len_ref, res_ref, g_ref, vec_ref, *rest):
    ys = rest[:n_part]
    gns = rest[n_part : 2 * n_part]
    mixed = rest[2 * n_part : 2 * n_part + n_mix]
    rest = rest[2 * n_part + n_mix :]
    pieces = rest[:n_in]
    long_ref, glob_ref, gres_ref, gmix_ref, small_ref, gw_ref = rest[n_in : n_in + 6]
    w_s, gattn_s, gw_s, sems = rest[n_in + 6 :]
    s = pl.program_id(0)

    @pl.when(s == 0)
    def _():
        for copy in load_rows(pieces, pos_ref, lines, w_s, sems, first_col):
            copy.wait()
        gw_s[...] = jnp.zeros_like(gw_s)
        small_ref[...] = jnp.zeros_like(small_ref)

    live = live_mask(len_ref[s], D)
    res = res_ref[...]
    y = res + vec_ref[DOWN_B : DOWN_B + 1]
    gn2 = gns[0][...]
    for ref in ys:
        y = y + ref[...]
    for ref in gns[1:]:
        gn2 = gn2 + ref[...]
    y = jnp.where(live, y, 0.0).astype(BF16)
    glob_ref[0, 0] = y[:GLOB]
    long_ref[0, 0] = y[GLOB:]
    xhat, rstd = norm_stats(res)
    g = g_ref[...].astype(F32)
    gres = g + norm_back(gn2, xhat, rstd, vec_ref[GAIN2 : GAIN2 + 1])
    gres_ref[...] = gres
    gattn = gres.astype(BF16)
    gattn_s[...] = gattn
    small_ref[0:1] += jnp.sum(gn2 * xhat, axis=0, keepdims=True)
    small_ref[1:2] += jnp.sum(gn2, axis=0, keepdims=True)
    small_ref[2:3] += jnp.sum(gattn.astype(F32), axis=0, keepdims=True)
    small_ref[3:4] += jnp.sum(g, axis=0, keepdims=True)

    for c in tiles(D):
        gmix_ref[:, c] = dot(gattn_s[...], w_s[c, :], NT).astype(BF16)
        at = 0
        for m in mixed:
            gw_s[at : at + m.shape[1], c] += dot(m[...], gattn_s[:, c], TN)
            at += m.shape[1]

    @pl.when(s == pl.num_programs(0) - 1)
    def _():
        gw_ref[...] = gw_s[...].astype(BF16)


def mid(deps, pos, lengths, res, g, vec, ys, gns, mixed, pieces, first_col, long_shape, glob_shape):
    rows = res.shape[0]
    lines = pos.shape[0]
    spec = pl.BlockSpec((T, D), lambda s, *_: (s, 0))
    return run(
        functools.partial(mid_kernel, lines, len(pieces), first_col, len(mixed), len(ys)),
        deps,
        [pos, lengths],
        [res, g, vec, *ys, *gns, *mixed, *pieces],
        [
            jax.ShapeDtypeStruct(long_shape, BF16),
            jax.ShapeDtypeStruct(glob_shape, BF16),
            jax.ShapeDtypeStruct((rows, D), F32),
            jax.ShapeDtypeStruct((rows, D), BF16),
            jax.ShapeDtypeStruct((8, D), F32),
            jax.ShapeDtypeStruct((D, D), BF16),
        ],
        "mid",
        17,
        grid=(rows // T,),
        in_specs=[spec, spec, VMEM]
        + [spec] * (2 * len(ys))
        + [pl.BlockSpec((T, m.shape[1]), lambda s, *_: (s, 0)) for m in mixed]
        + [ANY] * len(pieces),
        out_specs=[
            pl.BlockSpec((1, 1, SEQ, D), lambda s, *_: (s, 0, 0, 0)),
            pl.BlockSpec((1, 1, GLOB, D), lambda s, *_: (s, 0, 0, 0)),
            spec,
            spec,
            pl.BlockSpec((8, D), lambda s, *_: (0, 0)),
            pl.BlockSpec((D, D), lambda s, *_: (0, 0)),
        ],
        scratch_shapes=[
            pltpu.VMEM((D, D), BF16),
            pltpu.VMEM((T, D), BF16),
            pltpu.VMEM((D, D), F32),
            pltpu.SemaphoreType.DMA((lines,)),
        ],
    )


def weight_kernel(n_grads, n_out, owned, pos_ref, normed_ref, *rest):
    grads = rest[:n_grads]
    extra = rest[n_grads : len(rest) - n_out - 2]
    outs = rest[len(rest) - n_out - 2 : len(rest) - 2]
    gw_s, out_sems = rest[len(rest) - 2 :]
    piece_rows = outs[0].shape[1]
    width = sum(ref.shape[1] for ref in grads) // 3
    at = 3 * width
    if owned:
        grels, (small2_ref, small1_ref, qv_ref, *gbs) = extra[:3], extra[3:]
        sides = dot(qv_ref[:2].astype(BF16), owner_order(owned), NT)
        half = D // 2
        a = jnp.concatenate([sides[:1, :half], sides[1:, :half]], axis=1)
        b = jnp.concatenate([sides[:1, half:], sides[1:, half:]], axis=1)
        vecs = [small1_ref[:2], a, b, small2_ref[:4]]
        vecs += [ref[:, D * i : D * (i + 1)] for ref in gbs for i in range(ref.shape[1] // D)]
        vecs = jnp.concatenate(vecs + [jnp.zeros((128 - 12, D), F32)], axis=0).T
        gw_s[:, at + LABELS :] = vecs.astype(BF16)
        row = 0
        for ref in grels:
            gw_s[row : row + ref.shape[0], at : at + LABELS] = ref[...].astype(BF16)
            row += ref.shape[0]
    else:
        for ref in extra:
            gw_s[:, at : at + ref.shape[1]] = ref[...].astype(BF16)
            at += ref.shape[1]
    first_pair = 0
    for grad_ref in grads:
        cols = grad_ref.shape[1]
        for c in tiles(cols):
            out = dot(normed_ref[...], grad_ref[:, c], TN).astype(BF16)
            for at in range(c.start, c.stop, 128):
                pair, part = at // WAYS, at % WAYS // 128
                to = width * part + 128 * (first_pair + pair)
                gw_s[:, to : to + 128] = out[:, at - c.start : at - c.start + 128]
        first_pair += cols // WAYS
    copies = store_rows(gw_s, outs, piece_rows, pos_ref, out_sems, 0)
    for copy in copies:
        copy.start()
    for copy in copies:
        copy.wait()


def weight_grad(deps, pos, normed, grads, extra, out_groups, owned=0):
    rows = normed.shape[0]
    lines = pos.shape[0]
    cols = sum(g.shape[1] for g in grads)
    cols += LABELS + 128 if owned else sum(r.shape[1] for r in extra)
    return run(
        functools.partial(weight_kernel, len(grads), len(out_groups), owned),
        deps,
        [pos],
        [normed, *grads, *extra],
        [jax.ShapeDtypeStruct((k, D // lines, cols), BF16) for k in out_groups],
        "weight_grad",
        cols / 200,
        grid=(1,),
        in_specs=[VMEM] * (1 + len(grads) + len(extra)),
        out_specs=[ANY] * len(out_groups),
        scratch_shapes=[pltpu.VMEM((D, cols), BF16), pltpu.SemaphoreType.DMA((lines,))],
    )


def input_kernel(lines, n_grads, n_in, pos_ref, long_in_ref, glob_in_ref, gres_ref, vec_ref, *rest):
    grads = rest[:n_grads]
    pieces = rest[n_grads : n_grads + 2 * n_in]
    long_ref, glob_ref, small_ref, qv_ref, w_s, gn1_s, sems = rest[n_grads + 2 * n_in :]
    copies = []
    to = 0
    for i, width in enumerate((FIRST, SECOND)):
        for pair in range(width // 128):
            for part in range(3):
                copies += load_rows(
                    pieces[n_in * i : n_in * (i + 1)],
                    pos_ref,
                    lines,
                    w_s.at[:, to : to + 128],
                    sems.at[to // 128],
                    width * part + 128 * pair,
                )
                to += 128
    at = 0
    for ref in grads:
        for pair in range(ref.shape[1] // WAYS):
            for row, part in ((0, 0), (1, 2)):
                col = WAYS * pair + 128 * part
                qv_ref[row : row + 1, at : at + 128] = jnp.sum(
                    ref[:, col : col + 128].astype(F32), axis=0, keepdims=True
                )
            at += 128
    for copy in copies:
        copy.wait()
    for c in tiles(D):
        total = 0.0
        at = 0
        for ref in grads:
            total = total + dot(ref[...], w_s[c, at : at + ref.shape[1]], NT)
            at += ref.shape[1]
        gn1_s[:, c] = total
    for s in range(long_in_ref.shape[0]):
        for src, dst, at, size in (
            (glob_in_ref, glob_ref, T * s, GLOB),
            (long_in_ref, long_ref, T * s + GLOB, SEQ),
        ):
            rows = slice(at, at + size)
            xhat, rstd = norm_stats(src[s, 0].astype(F32))
            gn1 = gn1_s[rows]
            dst[s, 0] = (gres_ref[rows] + norm_back(gn1, xhat, rstd, vec_ref[GAIN1 : GAIN1 + 1])).astype(BF16)
            sums = [jnp.sum(gn1 * xhat, axis=0, keepdims=True), jnp.sum(gn1, axis=0, keepdims=True)]
            for row in range(2):
                if s == 0 and src is glob_in_ref:
                    small_ref[row : row + 1] = sums[row]
                else:
                    small_ref[row : row + 1] += sums[row]


def input_grad(deps, pos, long_in, glob_in, gres, vec, grads, pieces):
    rows = gres.shape[0]
    lines = pos.shape[0]
    n = len(grads)
    return run(
        functools.partial(input_kernel, lines, n, len(pieces[0])),
        deps,
        [pos],
        [long_in, glob_in, gres, vec, *grads, *[p for group in pieces for p in group]],
        [
            jax.ShapeDtypeStruct(long_in.shape, BF16),
            jax.ShapeDtypeStruct(glob_in.shape, BF16),
            jax.ShapeDtypeStruct((8, D), F32),
            jax.ShapeDtypeStruct((8, D), F32),
        ],
        "input_grad",
        15,
        grid=(1,),
        in_specs=[VMEM] * (4 + n) + [ANY] * sum(len(p) for p in pieces),
        out_specs=[VMEM] * 4,
        scratch_shapes=[
            pltpu.VMEM((D, 3 * D), BF16),
            pltpu.VMEM((rows, D), F32),
            pltpu.SemaphoreType.DMA((3 * D // 128, lines)),
        ],
    )


def pack_kernel(w_qkv_ref, rel_ref, vec_ref, out_ref):
    width = FIRST
    for n in range(3):
        out_ref[:, width * n : width * (n + 1)] = w_qkv_ref[:, D * n : D * n + width]
    rows = rel_ref.shape[0]
    after_labels = VEC_AT - LEAD - RELS
    rest = LABELS - VEC_AT - vec_ref.shape[1]
    rel = jnp.concatenate(
        [
            jnp.zeros((rows, LEAD), F32),
            rel_ref[...].astype(F32),
            jnp.zeros((rows, after_labels), F32),
            vec_ref[...].astype(F32),
            jnp.zeros((rows, rest), F32),
        ],
        axis=1,
    )
    out_ref[:, 3 * width :] = rel.astype(BF16)


def pack(w_qkv, rel_embed, vec):
    rows = w_qkv.shape[0]
    return run(
        pack_kernel,
        [],
        [],
        [w_qkv, rel_embed, vec],
        [jax.ShapeDtypeStruct((rows, 3 * FIRST + LABELS), BF16)],
        "pack",
        1.5,
        grid=(1,),
        in_specs=[VMEM] * 3,
        out_specs=[VMEM],
        scratch_shapes=[],
    )[0]


def pack_next_kernel(w_qkv_ref, w_out_ref, out_ref):
    width = SECOND
    for n in range(3):
        out_ref[:, width * n : width * (n + 1)] = w_qkv_ref[:, D * (n + 1) - width : D * (n + 1)]
    out_ref[:, 3 * width :] = w_out_ref[...]


def pack_next(deps, w_qkv, w_out):
    rows = w_qkv.shape[0]
    return run(
        pack_next_kernel,
        deps,
        [],
        [w_qkv, w_out],
        [jax.ShapeDtypeStruct((rows, 3 * SECOND + D), BF16)],
        "pack",
        1.5,
        grid=(1,),
        in_specs=[VMEM] * 2,
        out_specs=[VMEM],
        scratch_shapes=[],
    )[0]


def pack_ffn_kernel(chunks, w_in_ref, w_down_ref, out_ref):
    rows = w_in_ref.shape[0]
    parts = FF // D
    per = parts // chunks
    down = w_down_ref[...].astype(F32)
    for c in range(chunks):
        at = 2 * per * D * c
        out_ref[:, at : at + per * D] = w_in_ref[:, per * D * c : per * D * (c + 1)]
        for i in range(per):
            q = per * c + i
            to = at + (per + i) * D
            out_ref[:, to : to + D] = down[rows * q : rows * (q + 1)].astype(BF16)


def pack_ffn(deps, w_in, w_down, chunks):
    rows = w_in.shape[0]
    return run(
        functools.partial(pack_ffn_kernel, chunks),
        deps,
        [],
        [w_in, w_down],
        [jax.ShapeDtypeStruct((rows, 2 * FF), BF16)],
        "pack",
        1.5,
        grid=(1,),
        in_specs=[VMEM] * 2,
        out_specs=[VMEM],
        scratch_shapes=[],
    )[0]


def unpack_kernel(n, *refs):
    g_qkv_ref, g_out_ref, g_rel_ref, small_ref = refs[2 * n :]
    for g, width in enumerate((FIRST, SECOND)):
        total = refs[n * g][...].astype(F32)
        for ref in refs[n * g + 1 : n * (g + 1)]:
            total = total + ref[...].astype(F32)
        for part in range(3):
            at = D * part + FIRST * g
            g_qkv_ref[:, at : at + width] = total[:, width * part : width * (part + 1)]
        if g == 1:
            g_out_ref[...] = total[:, 3 * width :]
        else:
            g_rel_ref[...] = total[:, 3 * width + BACK_LEAD : 3 * width + BACK_LEAD + RELS]
            rows = total.shape[0]
            vecs = total[:, 3 * width + LABELS :]
            vecs = jnp.concatenate([vecs, jnp.zeros((128 - rows, 128), F32)], axis=0).T
            small_ref[...] = vecs[:16, :rows]


def unpack(first, second):
    rows = first[0].shape[0]
    shape = lambda cols: jax.ShapeDtypeStruct((rows, cols), F32)
    return run(
        functools.partial(unpack_kernel, len(first)),
        [],
        [],
        [*first, *second],
        [shape(3 * D), shape(D), shape(RELS), jax.ShapeDtypeStruct((16, rows), F32)],
        "unpack",
        2,
        grid=(1,),
        in_specs=[VMEM] * (2 * len(first)),
        out_specs=[VMEM] * 4,
        scratch_shapes=[],
    )


def order_kernel(z_ref, *refs):
    parts, out_ref, total_s = refs[:-2], refs[-2], refs[-1]
    for mask, part in enumerate(parts):
        total_s[z_ref[0] ^ mask] = part[...].astype(F32)
    out_ref[...] = total_s[...].reshape(out_ref.shape).astype(out_ref.dtype)


def order(deps, z, parts):
    rows, cols = parts[0].shape
    lines = len(parts)
    return run(
        order_kernel,
        deps,
        [z],
        parts,
        [jax.ShapeDtypeStruct((lines * rows, cols), parts[0].dtype)],
        "order",
        1.5,
        grid=(1,),
        in_specs=[VMEM] * lines,
        out_specs=[VMEM],
        scratch_shapes=[pltpu.VMEM((lines, rows, cols), F32)],
    )[0]


def join_kernel(x_ref, y_ref, out_ref):
    rows = x_ref.shape[0]
    out_ref[:rows] = x_ref[...]
    out_ref[rows:] = y_ref[...]


def join(deps, x, y):
    rows, cols = x.shape
    parts = 4 if cols % 512 == 0 else 1
    return run(
        join_kernel,
        deps,
        [],
        [x, y],
        [jax.ShapeDtypeStruct((2 * rows, cols), x.dtype)],
        "join",
        1.5,
        grid=(parts,),
        in_specs=[pl.BlockSpec((rows, cols // parts), lambda i: (0, i))] * 2,
        out_specs=[pl.BlockSpec((2 * rows, cols // parts), lambda i: (0, i))],
        scratch_shapes=[],
    )[0]


def split_kernel(lines, z_ref, *refs):
    terms = refs[: len(refs) - lines - 1]
    outs = refs[len(terms) : len(terms) + lines]
    total_s = refs[-1]
    total = terms[0][...].reshape(terms[0].shape[-2:]).astype(F32)
    for ref in terms[1:]:
        total = total + ref[...].reshape(ref.shape[-2:]).astype(F32)
    total_s[...] = total.reshape(total_s.shape)
    for mask, out in enumerate(outs):
        out[...] = total_s[z_ref[0] ^ mask].astype(out.dtype)


def split(deps, z, terms, lines):
    rows, cols = terms[0].shape[-2:]
    kind = terms[0].dtype
    specs = []
    for t in terms:
        if t.ndim == 3:
            specs.append(pl.BlockSpec((1, rows, cols), lambda i, *_: (0, 0, 0)))
        else:
            specs.append(pl.BlockSpec((rows, cols), lambda i, *_: (0, 0)))
    rows = rows // lines
    return run(
        functools.partial(split_kernel, lines),
        deps,
        [z],
        terms,
        [jax.ShapeDtypeStruct((rows, cols), F32 if m == 0 else kind) for m in range(lines)],
        "split",
        2,
        grid=(1,),
        in_specs=specs,
        out_specs=[VMEM] * lines,
        scratch_shapes=[pltpu.VMEM((lines, rows, cols), F32)],
    )


def sum_kernel(*refs):
    total = refs[0][...].astype(F32)
    for ref in refs[1:-1]:
        total = total + ref[...].astype(F32)
    refs[-1][...] = total.reshape(refs[-1].shape).astype(refs[-1].dtype)


def second(deps, terms):
    _, rows, cols = terms[0].shape
    return run(
        sum_kernel,
        deps,
        [],
        terms,
        [jax.ShapeDtypeStruct((rows, cols), terms[0].dtype)],
        "second",
        2,
        grid=(1,),
        in_specs=[pl.BlockSpec((1, rows, cols), lambda i: (1, 0, 0))] * len(terms),
        out_specs=[VMEM],
        scratch_shapes=[],
    )[0]


def both(deps, terms):
    lines, rows, cols = terms[0].shape
    spec = pl.BlockSpec((1, rows, cols), lambda i: (i, 0, 0))
    return run(
        sum_kernel,
        deps,
        [],
        terms,
        [jax.ShapeDtypeStruct(terms[0].shape, terms[0].dtype)],
        "both",
        2,
        grid=(lines,),
        in_specs=[spec] * len(terms),
        out_specs=[spec],
        scratch_shapes=[],
    )[0]


AXES = ("wide", "narrow")


class Links:
    def __init__(self, mesh):
        self.wide = mesh.shape["wide"]
        self.narrow = mesh.shape["narrow"]
        self.count = self.wide * self.narrow
        self.pairwise = self.wide == 8 and self.narrow == 4
        self.lines = self.wide if self.pairwise else 1
        self.groups = (2, 2, 2, 2) if self.pairwise else (1,)

    def setup(self):
        if not self.pairwise:
            self.pos = jnp.zeros((1,), jnp.int32)
            return
        w = lax.axis_index("wide")
        self.z = lax.axis_index("narrow")
        near = jnp.where(w % 2 == 0, 2, 4)
        far = 6 - near
        order = [0, near, far, 6, 1, 1 ^ far, 1 ^ near, 7]
        self.pos = jnp.stack([w ^ m for m in order]).astype(jnp.int32)

    def slot(self, *marks):
        self.marks = list(marks)

    def swap(self, x, wide_mask=0, narrow_mask=0):
        masks = wide_mask if isinstance(wide_mask, tuple) else (wide_mask, wide_mask)
        pairs = []
        for w in range(self.wide):
            for z in range(self.narrow):
                pairs.append(
                    (w * self.narrow + z, (w ^ masks[w % 2]) * self.narrow + (z ^ narrow_mask))
                )
        return lax.ppermute(x, AXES, pairs)

    def line(self, x):
        if not self.pairwise:
            return [lax.all_gather(x, AXES, axis=0, tiled=True)]
        return [x] + [self.swap(x, 0, mask) for mask in (1, 2, 3)]

    def near(self, parts):
        if not self.pairwise:
            return parts
        x = order(self.marks, self.z.reshape(1), parts)
        return [x, self.swap(x, (2, 4))]

    def far(self, parts):
        if not self.pairwise:
            return parts
        own = join(self.marks, *parts)
        return [own, self.swap(own, (4, 2)), self.swap(own, 1)]

    def core(self, pieces):
        if not self.pairwise:
            return pieces
        own, far, own_core = pieces
        if self.marks:
            far = after(far, self.marks)
        return [own, far, own_core, self.swap(far, 1)]

    def add(self, *parts):
        total = parts[0].astype(F32)
        for p in parts[1:]:
            total = total + p.astype(F32)
        return total


class Sum:
    def __init__(self, links, parts):
        self.links = links
        self.parts = parts
        self.kind = parts[0].dtype

    def core(self):
        links = self.links
        if not links.pairwise:
            self.out = lax.psum_scatter(self.parts[0][0].astype(F32), AXES, scatter_dimension=0, tiled=True)
            return (self.out,)
        self.got_b = links.swap(self.parts[3], 1)
        self.got_a = links.swap(self.parts[2], 1)
        return (self.got_b, self.got_a)

    def far(self):
        links = self.links
        if not links.pairwise:
            return (self.out,)
        self.from_far = links.swap(both(links.marks, [self.parts[1], self.got_b]), (4, 2))
        return (self.from_far,)

    def near(self):
        links = self.links
        if not links.pairwise:
            return (self.out,)
        self.from_near = links.swap(second(links.marks, [self.parts[0], self.got_a, self.from_far]), (2, 4))
        return (self.from_near,)

    def line(self):
        links = self.links
        if not links.pairwise:
            self.terms = [self.out]
            return (self.out,)
        terms = [self.parts[0], self.got_a, self.from_far, self.from_near]
        mine, *others = split(links.marks, links.z.reshape(1), terms, links.narrow)
        got = [links.swap(x, 0, mask) for mask, x in enumerate(others, 1)]
        self.terms = [mine] + got
        return tuple(got)

    def total(self):
        return self.links.add(*self.terms)


CHUNKS = 2
PARTS = FF // D
PAIRS = 6


def body(links, long_in, glob_in, lengths, ln1_gain, ln1_bias, w_qkv, qv_bias, rel_embed, w_out, out_bias, ln2_gain, ln2_bias, w_in, in_bias, w_down, down_bias, cot_long, cot_glob):
    links.setup()
    pos = links.pos
    groups = links.groups
    count = links.count
    micro = long_in.shape[0]
    r = w_qkv.shape[0]
    lens = lengths.reshape(micro)
    per = PARTS // CHUNKS
    first, second = 3 * FIRST, 3 * SECOND
    n_first, n_second = FIRST // 128, SECOND // 128

    columns = [ln1_gain, ln1_bias, qv_bias, out_bias, ln2_gain, ln2_bias, down_bias, in_bias]
    columns = jnp.concatenate([v.reshape(-1, r) for v in columns], axis=0).T
    w_in_parts = w_in.reshape(r, count, PARTS, r).transpose(0, 2, 1, 3).reshape(r, FF)

    links.slot()
    line_a0 = links.line(pack(w_qkv, rel_embed, columns))
    near_a0 = links.near(line_a0)
    line_a1 = links.line(pack_next([line_a0[-1]], w_qkv, w_out))
    ffn_shard = pack_ffn([], w_in_parts, w_down, CHUNKS)
    links.slot(line_a1[0], ffn_shard)
    far_a0 = links.far(near_a0)
    links.slot(line_a1[-1])
    attn = [links.core(far_a0)]
    line_f = links.line(after(ffn_shard, [attn[0][-1]]))

    proj0, normed, rel_all, rel_turned, vec = project_first([], pos, long_in, glob_in, attn[0], r, first)
    links.slot(attn[0][-1])
    near_a1 = links.near(line_a1)
    mixed0, inv0, p0, pg0 = attend([near_a1[-1], line_f[-1]], lens, proj0, rel_all, 0)
    links.slot(proj0, near_a1[-1])
    far_a1 = links.far(near_a1)
    near_f = links.near(line_f)
    links.slot(mixed0)
    attn.append(links.core(far_a1))
    proj1 = project_next([near_f[-1], mixed0], pos, normed, vec, attn[1], second)
    links.slot(mixed0, far_a1[-1], near_f[-1])
    far_f = links.far(near_f)
    mixed1, inv1, p1, pg1 = attend([], lens, proj1, rel_all, n_first)
    mixed = [mixed0, mixed1]
    links.slot(mixed1)
    ffn_all = links.core(far_f)
    res, n2, g_ffn = mix_out(
        [ffn_all[len(ffn_all) // 4]], pos, lens, long_in, glob_in, cot_long, cot_glob, vec, mixed, attn[1], second
    )
    y0, gn0, gb0, *gw0 = ffn([], pos, n2, g_ffn, vec, ffn_all, 0, per, groups)
    sum0 = Sum(links, gw0)
    y1, gn1, gb1, *gw1 = ffn([y0], pos, n2, g_ffn, vec, ffn_all, per, per, groups)
    steps = sum0.core()
    sum1 = Sum(links, gw1)
    block_long, block_glob, gres, gmix, small2, gw_out = mid(
        [*steps], pos, lens, res, g_ffn, vec, [y0, y1], [gn0, gn1], mixed, attn[1], second, long_in.shape, glob_in.shape
    )
    links.slot(y1, *steps)
    steps = sum0.far() + sum1.core()
    gproj1, grel1 = attend_back([*steps], proj1, rel_turned, gmix, mixed1, inv1, p1, pg1, n_first, 0, 2)
    links.slot(gmix, *steps)
    steps = sum0.near() + sum1.far()
    gproj2, grel2 = attend_back([*steps], proj1, rel_turned, gmix, mixed1, inv1, p1, pg1, n_first, 2, 2)
    links.slot(gproj1, *steps)
    steps = sum0.line() + sum1.near()
    gw_a1 = weight_grad([*steps], pos, normed, [gproj1, gproj2], [gw_out], groups)
    sum2 = Sum(links, gw_a1)
    sum2.core()
    links.slot(gw_a1[0], *steps)
    steps = sum1.line() + sum2.far()
    gproj0, grel0 = attend_back([gw_a1[0]], proj0, rel_turned, gmix, mixed0, inv0, p0, pg0, 0, 0, n_first)
    grad_long, grad_glob, small1, small_qv = input_grad(
        [*steps], pos, long_in, glob_in, gres, vec, [gproj0, gproj1, gproj2], attn
    )
    links.slot(gproj0, *steps)
    steps = sum2.near()
    gw_a0 = weight_grad(
        [*steps], pos, normed, [gproj0], [grel0, grel1, grel2, small2, small1, small_qv, gb0, gb1], groups, r
    )
    sum3 = Sum(links, gw_a0)
    links.slot(small1, *steps)
    sum2.line()
    sum3.core()
    w_sums = [sum0.total(), sum1.total()]
    g_in = jnp.concatenate([w[:, : per * D] for w in w_sums], axis=1)
    g_in = g_in.reshape(r, PARTS, count, r).transpose(0, 2, 1, 3).reshape(r, FF)
    g_down = jnp.concatenate([w[:, D * (per + i) : D * (per + i + 1)] for w in w_sums for i in range(per)], axis=0)
    links.slot(gw_a0[0], *sum2.terms[1:])
    sum3.far()
    links.slot(g_in, g_down)
    sum3.near()
    links.slot()
    sum3.line()
    g_qkv, g_out, g_rel, small = unpack(sum3.terms, sum2.terms)
    g_gain1, g_bias1 = small[GAIN1], small[BIAS1]
    g_qv = small[2:4].reshape(-1)
    g_gain2, g_bias2, g_out_b, g_down_b = small[4], small[5], small[6], small[7]
    g_in_b = small[8:12].reshape(-1)
    return (
        block_long, block_glob, grad_long, grad_glob,
        g_gain1, g_bias1, g_qkv, g_qv, g_rel, g_out, g_out_b,
        g_gain2, g_bias2, g_in, g_in_b, g_down, g_down_b,
    )


def solution(mesh):
    rows = P(None, AXES, None, None)
    vec = P(AXES)
    mat = P(AXES, None)
    placed = (rows, rows, P(None, AXES), vec, vec, mat, vec, mat, mat, vec, vec, vec, mat, vec, mat, vec, rows, rows)
    return jax.shard_map(
        functools.partial(body, Links(mesh)),
        mesh=mesh,
        in_specs=placed,
        out_specs=(rows, rows, rows, rows, vec, vec, mat, vec, mat, mat, vec, vec, vec, mat, vec, mat, vec),
        check_vma=False,
    )
```

```python
import functools
import jax
import jax.numpy as jnp
from jax import lax
from jax.experimental import pallas as pl
from jax.experimental.pallas import tpu as pltpu
from jax.sharding import PartitionSpec as P

HEAD_DIM = 64
RADIUS = 84
STRIDE = 16
SEQ = 512
GLOB = 32
RELS = 169
T = GLOB + SEQ
D = 768
FF = 3072
PAIRS = 6
LABELS = 256
LEAD = 4
BACK_LEAD = 3
LABEL_END = LEAD + RELS
EPS = 1e-06
NEG = -1e30
F32 = jnp.float32
BF16 = jnp.bfloat16
VMEM_LIMIT = 63 << 20
WINDOWS = ((0, 0, 256, 328, 0), (0, 0, 384, 72, 0), (1, 160, 384, 8, 352), (1, 288, 256, 8, 224))
OFFSETS = (0, 256, 640, 1024)
WAYS = 3 * 128
VEC_AT = 176
GAIN1, BIAS1, QV, OUT_B, GAIN2, BIAS2, DOWN_B, IN_B, VECS = 0, 1, 2, 4, 5, 6, 7, 8, 16
P_COLS = 1280
NN = (((1,), (0,)), ((), ()))
NT = (((1,), (1,)), ((), ()))
TN = (((0,), (0,)), ((), ()))


def dot(a, b, dims=NN):
    return lax.dot_general(a, b, dims, preferred_element_type=F32)


def run(kernel, deps, prefetch, inputs, out_shape, name, cost, grid, in_specs, out_specs, scratch_shapes):
    n = len(prefetch)

    def with_deps(*refs):
        kernel(*refs[:n], *refs[n + len(deps) :])

    anywhere = pl.BlockSpec(memory_space=pl.ANY)
    return pl.pallas_call(
        with_deps,
        grid_spec=pltpu.PrefetchScalarGridSpec(
            num_scalar_prefetch=n,
            grid=grid,
            in_specs=[anywhere] * len(deps) + in_specs,
            out_specs=out_specs,
            scratch_shapes=scratch_shapes,
        ),
        out_shape=out_shape,
        compiler_params=pltpu.CompilerParams(vmem_limit_bytes=VMEM_LIMIT),
        cost_estimate=pl.CostEstimate(flops=int(cost * 1.15e9), bytes_accessed=1 << 20, transcendentals=0),
        name=name,
    )(*prefetch, *deps, *inputs)


def after(x, deps):
    anywhere = pl.BlockSpec(memory_space=pl.ANY)
    return pl.pallas_call(
        lambda *refs: None,
        in_specs=[anywhere] * (1 + len(deps)),
        out_specs=anywhere,
        out_shape=jax.ShapeDtypeStruct(x.shape, x.dtype),
        input_output_aliases={0: 0},
        name="after",
    )(x, *deps)


def iota(shape, dim):
    return lax.broadcasted_iota(jnp.int32, shape, dim)


def norm_stats(x):
    cen = x - jnp.mean(x, axis=1, keepdims=True)
    rstd = lax.rsqrt(jnp.mean(cen * cen, axis=1, keepdims=True) + EPS)
    return cen * rstd, rstd


def norm_back(grad, xhat, rstd, gain):
    gg = grad * gain
    return rstd * (
        gg - jnp.mean(gg, axis=1, keepdims=True) - xhat * jnp.mean(gg * xhat, axis=1, keepdims=True)
    )


def tiles(cols, size=256):
    return [slice(at, min(at + size, cols)) for at in range(0, cols, size)]


def live_mask(length, cols):
    row = iota((T, cols), 0)
    glob_count = (length + STRIDE - 1) // STRIDE
    return row < jnp.where(row < GLOB, glob_count, length + GLOB)


def load_rows(pieces, pos_ref, lines, dst, sems, first_col):
    rows = dst.shape[0] // lines
    cols = dst.shape[1]
    copies = []
    k = 0
    for piece in pieces:
        for i in range(piece.shape[0] // rows):
            start = pl.multiple_of(pos_ref[k] * rows, 16)
            copies.append(
                pltpu.make_async_copy(
                    piece.at[pl.ds(i * rows, rows), pl.ds(first_col, cols)],
                    dst.at[pl.ds(start, rows), :],
                    sems.at[k],
                )
            )
            k += 1
    for copy in copies:
        copy.start()
    return copies


FIRST = 2 * 128
SECOND = D - FIRST


def owner_order(rows):
    k = iota((D, 1), 0)
    late = (k >= D // 2).astype(jnp.int32)
    k = k - late * (D // 2)
    owner = ((k.astype(F32) + 0.5) * (1.0 / rows)).astype(jnp.int32)
    col = rows * owner + k + late * rows
    return (iota((D, D), 1) == col).astype(F32).astype(BF16)


def project_kernel(lines, n_pieces, first, rows, pos_ref, *rest):
    if first:
        long_ref, glob_ref = rest[:2]
    else:
        normed_ref, vec_ref = rest[:2]
    pieces = rest[2 : 2 + n_pieces]
    if first:
        proj_ref, normed_ref, rel_ref, relt_ref, vec_ref, w_s, sems = rest[2 + n_pieces :]
    else:
        proj_ref, w_s, sems = rest[2 + n_pieces :]
    cols = proj_ref.shape[1]
    width = cols // 3
    copies = load_rows(pieces, pos_ref, lines, w_s, sems.at[0], 0)
    if first:
        for copy in load_rows(pieces, pos_ref, lines, rel_ref, sems.at[1], cols):
            copy.wait()
        turned = rel_ref[...].astype(F32).T
        vec_ref[...] = turned[VEC_AT : VEC_AT + VECS]
        drop = LEAD - BACK_LEAD
        labels = jnp.concatenate([turned[drop:], turned[:drop]], axis=0)
        label = iota((LABELS, D), 0) - BACK_LEAD
        relt_ref[...] = jnp.where((label >= 0) & (label < RELS), labels, 0.0).astype(BF16)
        a, b = vec_ref[QV : QV + 1], vec_ref[QV + 1 : QV + 2]
        half = D // 2
        sides = jnp.concatenate(
            [
                jnp.concatenate([a[:, :half], b[:, :half]], axis=1),
                jnp.concatenate([a[:, half:], b[:, half:]], axis=1),
            ],
            axis=0,
        )
        vec_ref[QV : QV + 2] = dot(sides.astype(BF16), owner_order(rows))
        for s in range(long_ref.shape[0]):
            for part, at, size in ((glob_ref, T * s, GLOB), (long_ref, T * s + GLOB, SEQ)):
                xhat, _ = norm_stats(part[s, 0].astype(F32))
                normed_ref[at : at + size] = (
                    xhat * vec_ref[GAIN1 : GAIN1 + 1] + vec_ref[BIAS1 : BIAS1 + 1]
                ).astype(BF16)
    own = slice(0, width) if first else slice(D - width, D)
    full_bias = jnp.concatenate(
        [vec_ref[QV : QV + 1, own], jnp.zeros((1, width), F32), vec_ref[QV + 1 : QV + 2, own]], axis=1
    )
    for copy in copies:
        copy.wait()
    for c in tiles(cols):
        out = (dot(normed_ref[...], w_s[:, c]) + full_bias[:, c]).astype(BF16)
        for at in range(c.start, c.stop, 128):
            to = by_pair(at, width)
            proj_ref[:, to : to + 128] = out[:, at - c.start : at - c.start + 128]


def by_pair(col, width):
    return WAYS * (col % width // 128) + 128 * (col // width)


VMEM = pl.BlockSpec(memory_space=pltpu.VMEM)
ANY = pl.BlockSpec(memory_space=pl.ANY)


def project_first(deps, pos, long_in, glob_in, pieces, owned, cols):
    rows = long_in.shape[0] * T
    lines = pos.shape[0]
    shape = lambda *dims: jax.ShapeDtypeStruct(dims, BF16)
    return run(
        functools.partial(project_kernel, lines, len(pieces), True, owned),
        deps,
        [pos],
        [long_in, glob_in, *pieces],
        [
            shape(rows, cols),
            shape(rows, D),
            shape(D, LABELS),
            shape(LABELS, D),
            jax.ShapeDtypeStruct((VECS, D), F32),
        ],
        "project",
        9,
        grid=(1,),
        in_specs=[VMEM] * 2 + [ANY] * len(pieces),
        out_specs=[VMEM] * 5,
        scratch_shapes=[pltpu.VMEM((D, cols), BF16), pltpu.SemaphoreType.DMA((2, lines))],
    )


def project_next(deps, pos, normed, vec, pieces, cols):
    rows = normed.shape[0]
    lines = pos.shape[0]
    return run(
        functools.partial(project_kernel, lines, len(pieces), False, 0),
        deps,
        [pos],
        [normed, vec, *pieces],
        [jax.ShapeDtypeStruct((rows, cols), BF16)],
        "project",
        8,
        grid=(1,),
        in_specs=[VMEM] * 2 + [ANY] * len(pieces),
        out_specs=[VMEM],
        scratch_shapes=[pltpu.VMEM((D, cols), BF16), pltpu.SemaphoreType.DMA((2, lines))],
    )[0]


def flip_matrix(size):
    row, col = iota((size, size), 0), iota((size, size), 1)
    return ((row // 128 == col // 128) & (row % 128 + col % 128 == 127)).astype(F32).astype(BF16)


def by_head(x):
    even = iota(x.shape, 1) < HEAD_DIM
    return jnp.concatenate([jnp.where(even, x, 0.0), jnp.where(even, 0.0, x)], axis=0)


def by_lane(x):
    half = x.shape[0] // 2
    even = iota((half, x.shape[1]), 1) < HEAD_DIM
    return jnp.where(even, x[:half], x[half:])


def spread(x, b):
    _, _, width, shift, _ = WINDOWS[b]
    shift = shift if shift < 256 else shift - 384
    lane = iota((64, 128), 1)
    none = jnp.full((64, 128), NEG, F32)
    parts = []
    for at in range(0, 256, 64):
        start = shift + at % 128
        turned = pltpu.roll(x[at : at + 64], start % 256, 1, stride=1, stride_axis=0)
        low, high = turned[:, :128], turned[:, 128:]
        if start < 0:
            cols = [low, jnp.where(lane < 64, high, NEG), none]
        elif start + 64 + LABEL_END <= 256:
            cols = [low, high, none]
        elif start >= 128:
            cols = [none, high, low]
        else:
            cols = [jnp.where(lane >= 64, low, NEG), high, jnp.where(lane < 64, low, NEG)]
        parts.append(jnp.concatenate(cols[: width // 128], axis=1))
    return jnp.concatenate(parts, axis=0)


def collect(cols, b):
    _, _, width, shift, _ = WINDOWS[b]
    shift = shift if shift < 256 else shift - 384
    lane = iota((64, 128), 1)
    parts = []
    for at in range(0, 256, 64):
        start = shift + 64 - at % 128
        tiles_ = [c[at : at + 64] for c in cols]
        if start < 0:
            low, high = tiles_[0], jnp.where(lane < 64, tiles_[1], 0.0)
        elif start + 64 + LABEL_END <= 256:
            low, high = tiles_[0], tiles_[1]
        elif start >= 128:
            low, high = tiles_[2], tiles_[1]
        elif len(tiles_) > 2:
            low, high = jnp.where(lane >= 64, tiles_[0], tiles_[2]), tiles_[1]
        else:
            low, high = jnp.where(lane >= 64, tiles_[0], 0.0), tiles_[1]
        back = (BACK_LEAD - LEAD - 63 - start) % 256
        parts.append(
            pltpu.roll(jnp.concatenate([low, high], axis=1), back, 1, stride=1, stride_axis=0)
        )
    return jnp.concatenate(parts, axis=0)


def zero_glob(x, at):
    cols = [x[:, 128 * i : 128 * (i + 1)] for i in range(x.shape[1] // 128)]
    lane = iota(cols[0].shape, 1) - at % 128
    cols[at // 128] = jnp.where((lane >= 0) & (lane < GLOB), 0.0, cols[at // 128])
    return cols


def attend_kernel(len_ref, qkv_ref, rel_ref, mix_ref, inv_ref, p_ref, pg_ref, k_s, v_s, rel_s):
    dead = jnp.where(live_mask(len_ref[pl.program_id(0)], 128), 0.0, NEG)
    flag = iota((T, 128), 1) == 0
    k = jnp.concatenate(
        [qkv_ref[:, 128:256], jnp.where(flag, dead, 0.0).astype(BF16)], axis=1
    )
    v = jnp.concatenate([qkv_ref[:, 256:384], jnp.ones((T, 128), BF16)], axis=1)
    for s, m in ((k_s, k), (v_s, v)):
        s[0] = m
        s[1, :SEQ] = m[GLOB:]
        s[1, SEQ:] = m[:GLOB]
    label = iota((128, LABELS), 1)
    outside = ((label < LEAD) | (label >= LEAD + RELS)) & (iota((128, LABELS), 0) == 0)
    rel_s[:128] = rel_ref[...]
    rel_s[128:] = jnp.where(outside, NEG, 0.0).astype(BF16)
    flip = flip_matrix(256)

    def queries(rows):
        x = by_head(qkv_ref[rows, :128].astype(F32) * 0.125)
        one = (iota(x.shape, 1) == 0).astype(F32)
        return jnp.concatenate([x, one], axis=1).astype(BF16)

    def weights(scores):
        return jnp.exp(scores - jnp.max(scores, axis=1, keepdims=True)).astype(BF16)

    rows = [slice(0, GLOB)] + [slice(GLOB + 128 * b, GLOB + 128 * (b + 1)) for b in range(4)]
    wins = [(0, slice(0, T))] + [(arr, slice(first, first + width)) for arr, first, width, _, _ in WINDOWS]
    qs = [queries(r) for r in rows]
    scores = [dot(q, k_s[arr, win], NT) for q, (arr, win) in zip(qs, wins)]
    biases = [dot(q, rel_s[...]) for q in qs[1:]]
    for b, window in enumerate(WINDOWS):
        bias = zero_glob(spread(biases[b], b), window[-1])
        scores[b + 1] = scores[b + 1] + jnp.concatenate(bias, axis=1)
    ps = [weights(x) for x in scores]
    pg_ref[0, 0] = ps[0]
    outs = [dot(p, v_s[arr, win]) for p, (arr, win) in zip(ps, wins)]
    turned = [dot(flip, p) for p in ps[1:]]
    for r, out in zip(rows, outs):
        inv = by_lane(1.0 / out[:, 128:])
        inv_ref[r] = inv
        mix_ref[r] = (by_lane(out[:, :128]) * inv).astype(BF16)
    for b, p in enumerate(turned):
        p_ref[0, 0, :, OFFSETS[b] : OFFSETS[b] + p.shape[1]] = p.astype(BF16)


def attend(deps, lengths, proj, rel, first_pair):
    rows = proj.shape[0]
    seqs = rows // T
    pairs = proj.shape[1] // WAYS
    return run(
        attend_kernel,
        deps,
        [lengths],
        [proj, rel],
        [
            jax.ShapeDtypeStruct((rows, pairs * 128), BF16),
            jax.ShapeDtypeStruct((rows, pairs * 128), F32),
            jax.ShapeDtypeStruct((seqs, pairs, 256, P_COLS), BF16),
            jax.ShapeDtypeStruct((seqs, pairs, 2 * GLOB, T), BF16),
        ],
        "attend",
        6.2 * pairs,
        grid=(seqs, pairs),
        in_specs=[
            pl.BlockSpec((T, WAYS), lambda s, p, *_: (s, p)),
            pl.BlockSpec((128, LABELS), lambda s, p, *_: (first_pair + p, 0)),
        ],
        out_specs=[
            pl.BlockSpec((T, 128), lambda s, p, *_: (s, p)),
            pl.BlockSpec((T, 128), lambda s, p, *_: (s, p)),
            pl.BlockSpec((1, 1, 256, P_COLS), lambda s, p, *_: (s, p, 0, 0)),
            pl.BlockSpec((1, 1, 2 * GLOB, T), lambda s, p, *_: (s, p, 0, 0)),
        ],
        scratch_shapes=[
            pltpu.VMEM((2, T, 256), BF16),
            pltpu.VMEM((2, T, 256), BF16),
            pltpu.VMEM((256, LABELS), BF16),
        ],
    )


def attend_back_kernel(qkv_ref, relt_ref, do_ref, o_ref, inv_ref, p_ref, pg_ref, grad_ref, grel_ref, gk_s, gv_s, k_s, v_s):
    k = qkv_ref[:, 128:256]
    v = qkv_ref[:, 256:384]
    for s, m in ((k_s, k), (v_s, v)):
        s[0] = m
        s[1, :SEQ] = m[GLOB:]
        s[1, SEQ:] = m[:GLOB]
    flip = flip_matrix(128)

    @pl.when(pl.program_id(1) == 0)
    def _():
        grel_ref[...] = jnp.zeros_like(grel_ref)

    ones = jnp.ones((256, 128), BF16)

    def score_grads(do, o, p, v_win):
        prod = by_head(do * o)
        high = prod.astype(BF16)
        low = (prod - high.astype(F32)).astype(BF16)
        centre = dot(jnp.concatenate([high, low], axis=1), ones)
        dom = by_head(do).astype(BF16)
        dp = dot(dom, v_win, NT)
        width = dp.shape[1]
        cols = [dp[:, c] - centre[:, : c.stop - c.start] for c in tiles(width, 128)]
        return dom, p.astype(F32) * jnp.concatenate(cols, axis=1)

    do = (do_ref[:GLOB].astype(F32) * inv_ref[:GLOB]).astype(BF16).astype(F32)
    p = pg_ref[0, 0]
    dom, ds = score_grads(do, o_ref[:GLOB].astype(F32), p, v_s[0])
    ds = ds.astype(BF16)
    qm = by_head(qkv_ref[:GLOB, :128].astype(F32)).astype(BF16)
    grad_ref[:GLOB, :128] = (by_lane(dot(ds, k_s[0])) * 0.125).astype(BF16)
    gk_s[...] = dot(ds, qm, TN)
    gv_s[...] = dot(p, dom, TN)
    blocks = range(4)
    rows = [slice(GLOB + 128 * b, GLOB + 128 * (b + 1)) for b in blocks]
    wins = [(arr, slice(first, first + width)) for arr, first, width, _, _ in WINDOWS]
    turned = [
        dot(
            flip,
            jnp.concatenate(
                [
                    qkv_ref[r, :128],
                    (do_ref[r].astype(F32) * inv_ref[r]).astype(BF16),
                    o_ref[r],
                ],
                axis=1,
            ),
        )
        for r in rows
    ]
    qms = [by_head(x[:, :128]) for x in turned]
    qm_ts = [x.T.astype(BF16) for x in qms]
    qms = [x.astype(BF16) for x in qms]
    ps = [p_ref[0, 0, :, OFFSETS[b] : OFFSETS[b] + WINDOWS[b][2]] for b in blocks]
    grads = [
        score_grads(x[:, 128:256], x[:, 256:], p, v_s[arr, win])
        for x, p, (arr, win) in zip(turned, ps, wins)
    ]
    doms = [dom for dom, _ in grads]
    dss = [ds.astype(BF16) for _, ds in grads]
    labs = []
    for b, window in enumerate(WINDOWS):
        labs.append(collect(zero_glob(grads[b][1], window[-1]), b).astype(BF16))
    gqs = [
        by_lane(dot(ds, k_s[arr, win]) + dot(lab, relt_ref[...])) * 0.125
        for ds, lab, (arr, win) in zip(dss, labs, wins)
    ]
    gks = [dot(ds, qm, TN) for ds, qm in zip(dss, qms)]
    gvs = [dot(p, dom, TN) for p, dom in zip(ps, doms)]
    grel = sum(dot(qm_t, lab) for qm_t, lab in zip(qm_ts, labs))
    grel_ref[...] += grel * 0.125
    for r, gq in zip(rows, gqs):
        grad_ref[r, :128] = dot(flip, gq.astype(BF16)).astype(BF16)
    for b, (arr, first, width, _, _) in enumerate(WINDOWS):
        win = wins[b][1]
        for acc, part in ((gk_s, gks[b]), (gv_s, gvs[b])):
            if arr == 0:
                acc[win] += part
            else:
                acc[GLOB + first : T] += part[: width - GLOB]
                acc[:GLOB] += part[width - GLOB :]
    grad_ref[:, 128:256] = (gk_s[...] * 0.125).astype(BF16)
    grad_ref[:, 256:384] = gv_s[...].astype(BF16)


def attend_back(deps, proj, relt, gmixed, mixed, inv, p, pg, first_pair, start, pairs):
    rows = proj.shape[0]
    seqs = rows // T
    return run(
        attend_back_kernel,
        deps,
        [],
        [proj, relt, gmixed, mixed, inv, p, pg],
        [
            jax.ShapeDtypeStruct((rows, pairs * WAYS), BF16),
            jax.ShapeDtypeStruct((pairs * 128, LABELS), F32),
        ],
        "attend_back",
        8 * pairs,
        grid=(pairs, seqs),
        in_specs=[
            pl.BlockSpec((T, WAYS), lambda p, s: (s, start + p)),
            pl.BlockSpec((LABELS, 128), lambda p, s: (0, first_pair + start + p)),
            pl.BlockSpec((T, 128), lambda p, s: (s, first_pair + start + p)),
            pl.BlockSpec((T, 128), lambda p, s: (s, start + p)),
            pl.BlockSpec((T, 128), lambda p, s: (s, start + p)),
            pl.BlockSpec((1, 1, 256, P_COLS), lambda p, s: (s, start + p, 0, 0)),
            pl.BlockSpec((1, 1, 2 * GLOB, T), lambda p, s: (s, start + p, 0, 0)),
        ],
        out_specs=[pl.BlockSpec((T, WAYS), lambda p, s: (s, p)), pl.BlockSpec((128, LABELS), lambda p, s: (p, 0))],
        scratch_shapes=[
            pltpu.VMEM((T, 128), F32),
            pltpu.VMEM((T, 128), F32),
            pltpu.VMEM((2, T, 128), BF16),
            pltpu.VMEM((2, T, 128), BF16),
        ],
    )


def mix_out_kernel(lines, n_pieces, first_col, n_mix, pos_ref, len_ref, long_ref, glob_ref, clong_ref, cglob_ref, vec_ref, *rest):
    mixed = rest[:n_mix]
    pieces = rest[n_mix : n_mix + n_pieces]
    res_ref, n2_ref, g_ref, w_s, sems = rest[n_mix + n_pieces :]
    copies = load_rows(pieces, pos_ref, lines, w_s, sems, first_col)
    seqs = long_ref.shape[0]
    for s in range(seqs):
        live = live_mask(len_ref[s], D)
        at = T * s
        g_ref[at : at + GLOB] = jnp.where(live[:GLOB], cglob_ref[s, 0].astype(F32), 0.0).astype(BF16)
        g_ref[at + GLOB : at + T] = jnp.where(live[GLOB:], clong_ref[s, 0].astype(F32), 0.0).astype(BF16)
    for copy in copies:
        copy.wait()
    for c in tiles(D):
        acc = vec_ref[OUT_B : OUT_B + 1, c]
        at = 0
        for m in mixed:
            acc = acc + dot(m[...], w_s[at : at + m.shape[1], c])
            at += m.shape[1]
        res_ref[:, c] = acc
    for s in range(seqs):
        for part, at, size in ((glob_ref, T * s, GLOB), (long_ref, T * s + GLOB, SEQ)):
            res = res_ref[at : at + size] + part[s, 0].astype(F32)
            res_ref[at : at + size] = res
            xhat, _ = norm_stats(res)
            n2_ref[at : at + size] = (
                xhat * vec_ref[GAIN2 : GAIN2 + 1] + vec_ref[BIAS2 : BIAS2 + 1]
            ).astype(BF16)


def mix_out(deps, pos, lengths, long_in, glob_in, cot_long, cot_glob, vec, mixed, pieces, first_col):
    rows = long_in.shape[0] * T
    lines = pos.shape[0]
    return run(
        functools.partial(mix_out_kernel, lines, len(pieces), first_col, len(mixed)),
        deps,
        [pos, lengths],
        [long_in, glob_in, cot_long, cot_glob, vec, *mixed, *pieces],
        [
            jax.ShapeDtypeStruct((rows, D), F32),
            jax.ShapeDtypeStruct((rows, D), BF16),
            jax.ShapeDtypeStruct((rows, D), BF16),
        ],
        "mix_out",
        10,
        grid=(1,),
        in_specs=[VMEM] * (5 + len(mixed)) + [ANY] * len(pieces),
        out_specs=[VMEM] * 3,
        scratch_shapes=[pltpu.VMEM((D, D), BF16), pltpu.SemaphoreType.DMA((lines,))],
    )


def store_rows(src, outs, rows, src_pos_ref, sems, first_col):
    cols = src.shape[1]
    copies = []
    k = 0
    for out in outs:
        for i in range(out.shape[0]):
            start = pl.multiple_of(src_pos_ref[k] * rows, 16)
            copies.append(
                pltpu.make_async_copy(
                    src.at[pl.ds(start, rows), :], out.at[i, :, pl.ds(first_col, cols)], sems.at[k]
                )
            )
            k += 1
    return copies


def gelu_parts(v):
    cdf = 0.5 * (1.0 + lax.erf(v * 0.7071067811865476))
    pdf = jnp.exp(v * v * -0.5) * 0.3989422804014327
    return v * cdf, cdf + v * pdf


def ffn_kernel(lines, n_in, n_parts, n_out, first, pos_ref, n2_ref, g_ref, vec_ref, *rest):
    pieces = rest[:n_in]
    y_ref, gn2_ref, gb_ref = rest[n_in : n_in + 3]
    outs = rest[n_in + 3 : n_in + 3 + n_out]
    w_in_s, w_down_s, act_s, gpre_s, gw_s, y_s, gn2_s, sems, out_sems = rest[n_in + 3 + n_out :]
    part = pl.program_id(0)
    piece_rows = outs[0].shape[1]

    @pl.when(part == 0)
    def _():
        copies = []
        for i in range(n_parts):
            copies += load_rows(pieces, pos_ref, lines, w_in_s.at[i], sems.at[2 * i], i * D)
            copies += load_rows(pieces, pos_ref, lines, w_down_s.at[i], sems.at[2 * i + 1], (n_parts + i) * D)
        for copy in copies:
            copy.wait()

    for c in tiles(D):
        pre = dot(n2_ref[...], w_in_s[part, :, c]) + vec_ref[pl.ds(IN_B + first + part, 1), c]
        act, slope = gelu_parts(pre)
        act_s[:, c] = act.astype(BF16)
        gpre = (dot(g_ref[...], w_down_s[part, c, :], NT) * slope).astype(BF16)
        gpre_s[:, c] = gpre
        gb_ref[:, c] = jnp.sum(gpre.astype(F32), axis=0, keepdims=True)

    def flush(which):
        first = pl.multiple_of((which * n_parts + part) * D, 128)
        return store_rows(gw_s.at[which], outs, piece_rows, pos_ref, out_sems.at[which], first)

    for which, (lhs, rhs) in enumerate(((n2_ref, gpre_s), (act_s, g_ref))):
        for c in tiles(D):
            gw_s[which, :, c] = dot(lhs[...], rhs[:, c], TN).astype(BF16)
        for copy in flush(which):
            copy.start()

    def outputs(first_part, last_part):
        for c in tiles(D):
            for total_s, out_ref, part_sum in (
                (y_s, y_ref, dot(act_s[...], w_down_s[part, :, c])),
                (gn2_s, gn2_ref, dot(gpre_s[...], w_in_s[part, c, :], NT)),
            ):
                if not first_part:
                    part_sum = total_s[:, c] + part_sum
                if last_part:
                    out_ref[:, c] = part_sum.astype(BF16)
                else:
                    total_s[:, c] = part_sum

    for i in range(n_parts):
        pl.when(part == i)(functools.partial(outputs, i == 0, i == n_parts - 1))
    for which in range(2):
        for copy in flush(which):
            copy.wait()


def ffn(deps, pos, n2, g, vec, pieces, first, n_parts, out_groups):
    rows = n2.shape[0]
    lines = pos.shape[0]
    full = pl.BlockSpec((rows, D), lambda q, *_: (0, 0))
    return run(
        functools.partial(ffn_kernel, lines, len(pieces), n_parts, len(out_groups), first),
        deps,
        [pos],
        [n2, g, vec, *pieces],
        [
            jax.ShapeDtypeStruct((rows, D), BF16),
            jax.ShapeDtypeStruct((rows, D), BF16),
            jax.ShapeDtypeStruct((1, n_parts * D), F32),
        ]
        + [jax.ShapeDtypeStruct((k, D // lines, 2 * n_parts * D), BF16) for k in out_groups],
        "ffn",
        28,
        grid=(n_parts,),
        in_specs=[full, full, VMEM] + [ANY] * len(pieces),
        out_specs=[full, full, pl.BlockSpec((1, D), lambda q, *_: (0, q))] + [ANY] * len(out_groups),
        scratch_shapes=[
            pltpu.VMEM((n_parts, D, D), BF16),
            pltpu.VMEM((n_parts, D, D), BF16),
            pltpu.VMEM((rows, D), BF16),
            pltpu.VMEM((rows, D), BF16),
            pltpu.VMEM((2, D, D), BF16),
            pltpu.VMEM((rows, D), F32),
            pltpu.VMEM((rows, D), F32),
            pltpu.SemaphoreType.DMA((2 * n_parts, lines)),
            pltpu.SemaphoreType.DMA((2, lines)),
        ],
    )


def mid_kernel(lines, n_in, first_col, n_mix, n_part, pos_ref, len_ref, res_ref, g_ref, vec_ref, *rest):
    ys = rest[:n_part]
    gns = rest[n_part : 2 * n_part]
    mixed = rest[2 * n_part : 2 * n_part + n_mix]
    rest = rest[2 * n_part + n_mix :]
    pieces = rest[:n_in]
    long_ref, glob_ref, gres_ref, gmix_ref, small_ref, gw_ref = rest[n_in : n_in + 6]
    w_s, gattn_s, gw_s, sems = rest[n_in + 6 :]
    s = pl.program_id(0)

    @pl.when(s == 0)
    def _():
        for copy in load_rows(pieces, pos_ref, lines, w_s, sems, first_col):
            copy.wait()
        gw_s[...] = jnp.zeros_like(gw_s)
        small_ref[...] = jnp.zeros_like(small_ref)

    live = live_mask(len_ref[s], D)
    res = res_ref[...]
    y = res + vec_ref[DOWN_B : DOWN_B + 1]
    gn2 = gns[0][...].astype(F32)
    for ref in ys:
        y = y + ref[...].astype(F32)
    for ref in gns[1:]:
        gn2 = gn2 + ref[...].astype(F32)
    y = jnp.where(live, y, 0.0).astype(BF16)
    glob_ref[0, 0] = y[:GLOB]
    long_ref[0, 0] = y[GLOB:]
    xhat, rstd = norm_stats(res)
    g = g_ref[...].astype(F32)
    gres = g + norm_back(gn2, xhat, rstd, vec_ref[GAIN2 : GAIN2 + 1])
    gres_ref[...] = gres
    gattn = gres.astype(BF16)
    gattn_s[...] = gattn
    small_ref[0:1] += jnp.sum(gn2 * xhat, axis=0, keepdims=True)
    small_ref[1:2] += jnp.sum(gn2, axis=0, keepdims=True)
    small_ref[2:3] += jnp.sum(gattn.astype(F32), axis=0, keepdims=True)
    small_ref[3:4] += jnp.sum(g, axis=0, keepdims=True)

    for c in tiles(D):
        gmix_ref[:, c] = dot(gattn_s[...], w_s[c, :], NT).astype(BF16)
        at = 0
        for m in mixed:
            gw_s[at : at + m.shape[1], c] += dot(m[...], gattn_s[:, c], TN)
            at += m.shape[1]

    @pl.when(s == pl.num_programs(0) - 1)
    def _():
        gw_ref[...] = gw_s[...].astype(BF16)


def mid(deps, pos, lengths, res, g, vec, ys, gns, mixed, pieces, first_col, long_shape, glob_shape):
    rows = res.shape[0]
    lines = pos.shape[0]
    spec = pl.BlockSpec((T, D), lambda s, *_: (s, 0))
    return run(
        functools.partial(mid_kernel, lines, len(pieces), first_col, len(mixed), len(ys)),
        deps,
        [pos, lengths],
        [res, g, vec, *ys, *gns, *mixed, *pieces],
        [
            jax.ShapeDtypeStruct(long_shape, BF16),
            jax.ShapeDtypeStruct(glob_shape, BF16),
            jax.ShapeDtypeStruct((rows, D), F32),
            jax.ShapeDtypeStruct((rows, D), BF16),
            jax.ShapeDtypeStruct((8, D), F32),
            jax.ShapeDtypeStruct((D, D), BF16),
        ],
        "mid",
        17,
        grid=(rows // T,),
        in_specs=[spec, spec, VMEM]
        + [spec] * (2 * len(ys))
        + [pl.BlockSpec((T, m.shape[1]), lambda s, *_: (s, 0)) for m in mixed]
        + [ANY] * len(pieces),
        out_specs=[
            pl.BlockSpec((1, 1, SEQ, D), lambda s, *_: (s, 0, 0, 0)),
            pl.BlockSpec((1, 1, GLOB, D), lambda s, *_: (s, 0, 0, 0)),
            spec,
            spec,
            pl.BlockSpec((8, D), lambda s, *_: (0, 0)),
            pl.BlockSpec((D, D), lambda s, *_: (0, 0)),
        ],
        scratch_shapes=[
            pltpu.VMEM((D, D), BF16),
            pltpu.VMEM((T, D), BF16),
            pltpu.VMEM((D, D), F32),
            pltpu.SemaphoreType.DMA((lines,)),
        ],
    )


def weight_kernel(n_grads, n_out, owned, pos_ref, normed_ref, *rest):
    grads = rest[:n_grads]
    extra = rest[n_grads : len(rest) - n_out - 2]
    outs = rest[len(rest) - n_out - 2 : len(rest) - 2]
    gw_s, out_sems = rest[len(rest) - 2 :]
    piece_rows = outs[0].shape[1]
    width = sum(ref.shape[1] for ref in grads) // 3
    at = 3 * width
    if owned:
        grels, (small2_ref, small1_ref, qv_ref, *gbs) = extra[:2], extra[2:]
        sides = dot(qv_ref[:2].astype(BF16), owner_order(owned), NT)
        half = D // 2
        a = jnp.concatenate([sides[:1, :half], sides[1:, :half]], axis=1)
        b = jnp.concatenate([sides[:1, half:], sides[1:, half:]], axis=1)
        vecs = [small1_ref[:2], a, b, small2_ref[:4]]
        vecs += [ref[:, D * i : D * (i + 1)] for ref in gbs for i in range(ref.shape[1] // D)]
        vecs = jnp.concatenate(vecs + [jnp.zeros((128 - 12, D), F32)], axis=0).T
        gw_s[:, at + LABELS :] = vecs.astype(BF16)
        row = 0
        for ref in grels:
            gw_s[row : row + ref.shape[0], at : at + LABELS] = ref[...].astype(BF16)
            row += ref.shape[0]
    else:
        for ref in extra:
            gw_s[:, at : at + ref.shape[1]] = ref[...].astype(BF16)
            at += ref.shape[1]
    first_pair = 0
    for grad_ref in grads:
        cols = grad_ref.shape[1]
        for c in tiles(cols):
            out = dot(normed_ref[...], grad_ref[:, c], TN).astype(BF16)
            for at in range(c.start, c.stop, 128):
                pair, part = at // WAYS, at % WAYS // 128
                to = width * part + 128 * (first_pair + pair)
                gw_s[:, to : to + 128] = out[:, at - c.start : at - c.start + 128]
        first_pair += cols // WAYS
    copies = store_rows(gw_s, outs, piece_rows, pos_ref, out_sems, 0)
    for copy in copies:
        copy.start()
    for copy in copies:
        copy.wait()


def weight_grad(deps, pos, normed, grads, extra, out_groups, owned=0):
    rows = normed.shape[0]
    lines = pos.shape[0]
    cols = sum(g.shape[1] for g in grads)
    cols += LABELS + 128 if owned else sum(r.shape[1] for r in extra)
    return run(
        functools.partial(weight_kernel, len(grads), len(out_groups), owned),
        deps,
        [pos],
        [normed, *grads, *extra],
        [jax.ShapeDtypeStruct((k, D // lines, cols), BF16) for k in out_groups],
        "weight_grad",
        cols / 200,
        grid=(1,),
        in_specs=[VMEM] * (1 + len(grads) + len(extra)),
        out_specs=[ANY] * len(out_groups),
        scratch_shapes=[pltpu.VMEM((D, cols), BF16), pltpu.SemaphoreType.DMA((lines,))],
    )


def input_kernel(lines, n_grads, n_in, pos_ref, long_in_ref, glob_in_ref, gres_ref, vec_ref, *rest):
    grads = rest[:n_grads]
    pieces = rest[n_grads : n_grads + 2 * n_in]
    long_ref, glob_ref, small_ref, qv_ref, w_s, gn1_s, sems = rest[n_grads + 2 * n_in :]
    copies = []
    to = 0
    for i, width in enumerate((FIRST, SECOND)):
        for pair in range(width // 128):
            for part in range(3):
                copies += load_rows(
                    pieces[n_in * i : n_in * (i + 1)],
                    pos_ref,
                    lines,
                    w_s.at[:, to : to + 128],
                    sems.at[to // 128],
                    width * part + 128 * pair,
                )
                to += 128
    at = 0
    for ref in grads:
        for pair in range(ref.shape[1] // WAYS):
            for row, part in ((0, 0), (1, 2)):
                col = WAYS * pair + 128 * part
                qv_ref[row : row + 1, at : at + 128] = jnp.sum(
                    ref[:, col : col + 128].astype(F32), axis=0, keepdims=True
                )
            at += 128
    for copy in copies:
        copy.wait()
    for c in tiles(D):
        total = 0.0
        at = 0
        for ref in grads:
            total = total + dot(ref[...], w_s[c, at : at + ref.shape[1]], NT)
            at += ref.shape[1]
        gn1_s[:, c] = total
    for s in range(long_in_ref.shape[0]):
        for src, dst, at, size in (
            (glob_in_ref, glob_ref, T * s, GLOB),
            (long_in_ref, long_ref, T * s + GLOB, SEQ),
        ):
            rows = slice(at, at + size)
            xhat, rstd = norm_stats(src[s, 0].astype(F32))
            gn1 = gn1_s[rows]
            dst[s, 0] = (gres_ref[rows] + norm_back(gn1, xhat, rstd, vec_ref[GAIN1 : GAIN1 + 1])).astype(BF16)
            sums = [jnp.sum(gn1 * xhat, axis=0, keepdims=True), jnp.sum(gn1, axis=0, keepdims=True)]
            for row in range(2):
                if s == 0 and src is glob_in_ref:
                    small_ref[row : row + 1] = sums[row]
                else:
                    small_ref[row : row + 1] += sums[row]


def input_grad(deps, pos, long_in, glob_in, gres, vec, grads, pieces):
    rows = gres.shape[0]
    lines = pos.shape[0]
    n = len(grads)
    return run(
        functools.partial(input_kernel, lines, n, len(pieces[0])),
        deps,
        [pos],
        [long_in, glob_in, gres, vec, *grads, *[p for group in pieces for p in group]],
        [
            jax.ShapeDtypeStruct(long_in.shape, BF16),
            jax.ShapeDtypeStruct(glob_in.shape, BF16),
            jax.ShapeDtypeStruct((8, D), F32),
            jax.ShapeDtypeStruct((8, D), F32),
        ],
        "input_grad",
        15,
        grid=(1,),
        in_specs=[VMEM] * (4 + n) + [ANY] * sum(len(p) for p in pieces),
        out_specs=[VMEM] * 4,
        scratch_shapes=[
            pltpu.VMEM((D, 3 * D), BF16),
            pltpu.VMEM((rows, D), F32),
            pltpu.SemaphoreType.DMA((3 * D // 128, lines)),
        ],
    )


def pack_kernel(w_qkv_ref, rel_ref, *rest):
    vec_refs, out_ref = rest[:-1], rest[-1]
    width = FIRST
    for n in range(3):
        out_ref[:, width * n : width * (n + 1)] = w_qkv_ref[:, D * n : D * n + width]
    rows = rel_ref.shape[0]
    vecs = []
    for ref in vec_refs:
        v = ref[...].astype(F32)
        vecs += [v[at : at + rows].reshape(1, rows) for at in range(0, v.shape[0], rows)]
    vecs = jnp.concatenate(vecs + [jnp.zeros((128 - len(vecs), rows), F32)], axis=0).T
    rel = jnp.concatenate(
        [
            jnp.zeros((rows, LEAD), F32),
            rel_ref[...].astype(F32),
            jnp.zeros((rows, VEC_AT - LEAD - RELS), F32),
            vecs[:, : LABELS - VEC_AT],
        ],
        axis=1,
    )
    out_ref[:, 3 * width :] = rel.astype(BF16)


def pack(w_qkv, rel_embed, vecs):
    rows = w_qkv.shape[0]
    return run(
        pack_kernel,
        [],
        [],
        [w_qkv, rel_embed, *vecs],
        [jax.ShapeDtypeStruct((rows, 3 * FIRST + LABELS), BF16)],
        "pack",
        1.5,
        grid=(1,),
        in_specs=[VMEM] * (2 + len(vecs)),
        out_specs=[VMEM],
        scratch_shapes=[],
    )[0]


def pack_next_kernel(w_qkv_ref, w_out_ref, out_ref):
    width = SECOND
    for n in range(3):
        out_ref[:, width * n : width * (n + 1)] = w_qkv_ref[:, D * (n + 1) - width : D * (n + 1)]
    out_ref[:, 3 * width :] = w_out_ref[...]


def pack_next(deps, w_qkv, w_out):
    rows = w_qkv.shape[0]
    return run(
        pack_next_kernel,
        deps,
        [],
        [w_qkv, w_out],
        [jax.ShapeDtypeStruct((rows, 3 * SECOND + D), BF16)],
        "pack",
        1.5,
        grid=(1,),
        in_specs=[VMEM] * 2,
        out_specs=[VMEM],
        scratch_shapes=[],
    )[0]


def pack_ffn_kernel(chunks, w_in_ref, w_down_ref, out_ref):
    rows = w_in_ref.shape[0]
    parts = FF // D
    per = parts // chunks
    down = w_down_ref[...].astype(F32)
    for c in range(chunks):
        at = 2 * per * D * c
        out_ref[:, at : at + per * D] = w_in_ref[:, per * D * c : per * D * (c + 1)]
        for i in range(per):
            q = per * c + i
            to = at + (per + i) * D
            out_ref[:, to : to + D] = down[rows * q : rows * (q + 1)].astype(BF16)


def pack_ffn(deps, w_in, w_down, chunks):
    rows = w_in.shape[0]
    return run(
        functools.partial(pack_ffn_kernel, chunks),
        deps,
        [],
        [w_in, w_down],
        [jax.ShapeDtypeStruct((rows, 2 * FF), BF16)],
        "pack",
        1.5,
        grid=(1,),
        in_specs=[VMEM] * 2,
        out_specs=[VMEM],
        scratch_shapes=[],
    )[0]


def unpack_kernel(n, *refs):
    g_qkv_ref, g_out_ref, g_rel_ref, *vec_refs = refs[2 * n :]
    for g, width in enumerate((FIRST, SECOND)):
        total = refs[n * g][...].astype(F32)
        for ref in refs[n * g + 1 : n * (g + 1)]:
            total = total + ref[...].astype(F32)
        for part in range(3):
            at = D * part + FIRST * g
            g_qkv_ref[:, at : at + width] = total[:, width * part : width * (part + 1)]
        if g == 1:
            g_out_ref[...] = total[:, 3 * width :]
        else:
            g_rel_ref[...] = total[:, 3 * width + BACK_LEAD : 3 * width + BACK_LEAD + RELS]
            rows = total.shape[0]
            vecs = total[:, 3 * width + LABELS :]
            vecs = jnp.concatenate([vecs, jnp.zeros((128 - rows, 128), F32)], axis=0).T
            row = 0
            for ref in vec_refs:
                for at in range(0, ref.shape[0], rows):
                    ref[pl.ds(at, rows)] = vecs[row : row + 1, :rows].reshape(rows)
                    row += 1


def unpack(first, second, sizes):
    rows = first[0].shape[0]
    shape = lambda cols: jax.ShapeDtypeStruct((rows, cols), F32)
    return run(
        functools.partial(unpack_kernel, len(first)),
        [],
        [],
        [*first, *second],
        [shape(3 * D), shape(D), shape(RELS)] + [jax.ShapeDtypeStruct((n,), F32) for n in sizes],
        "unpack",
        2,
        grid=(1,),
        in_specs=[VMEM] * (2 * len(first)),
        out_specs=[VMEM] * (3 + len(sizes)),
        scratch_shapes=[],
    )


def order_kernel(count, z_ref, *refs):
    parts, outs, total_s = refs[: -1 - count], refs[-1 - count : -1], refs[-1]
    for mask, part in enumerate(parts):
        total_s[z_ref[0] ^ mask] = part[...].astype(F32)
    cols = outs[0].shape[1]
    for i, out in enumerate(outs):
        out[...] = total_s[:, :, cols * i : cols * (i + 1)].reshape(out.shape).astype(out.dtype)


def order(deps, z, parts, count):
    rows, cols = parts[0].shape
    lines = len(parts)
    return run(
        functools.partial(order_kernel, count),
        deps,
        [z],
        parts,
        [jax.ShapeDtypeStruct((lines * rows, cols // count), parts[0].dtype)] * count,
        "order",
        1.5,
        grid=(1,),
        in_specs=[VMEM] * lines,
        out_specs=[VMEM] * count,
        scratch_shapes=[pltpu.VMEM((lines, rows, cols), F32)],
    )


def unpack_ffn_kernel(chunks, *refs):
    terms, (g_in_ref, g_down_ref) = refs[:-2], refs[-2:]
    rows = g_in_ref.shape[0]
    parts = FF // D
    per = parts // chunks
    for q in range(parts):
        at = 2 * per * D * (q // per) + D * (q % per)
        for out, first in ((g_in_ref, at), (g_down_ref, at + per * D)):
            total = terms[0][:, first : first + D].astype(F32)
            for ref in terms[1:]:
                total = total + ref[:, first : first + D].astype(F32)
            if out is g_in_ref:
                out[:, D * q : D * (q + 1)] = total
            else:
                out[rows * q : rows * (q + 1), :] = total


def unpack_ffn(deps, terms, chunks):
    rows = terms[0].shape[0]
    return run(
        functools.partial(unpack_ffn_kernel, chunks),
        deps,
        [],
        terms,
        [jax.ShapeDtypeStruct((rows, FF), F32), jax.ShapeDtypeStruct((rows * (FF // D), D), F32)],
        "unpack",
        2,
        grid=(1,),
        in_specs=[VMEM] * len(terms),
        out_specs=[VMEM] * 2,
        scratch_shapes=[],
    )


def split_kernel(lines, counts, z_ref, *refs):
    outs = refs[sum(counts) : sum(counts) + lines]
    total_s = refs[-1]
    first = 0
    at = 0
    for n in counts:
        terms = refs[first : first + n]
        rows, cols = terms[0].shape[-2:]
        total = terms[0][...].reshape(rows, cols).astype(F32)
        for ref in terms[1:]:
            total = total + ref[...].reshape(rows, cols).astype(F32)
        total_s[:, :, at : at + cols] = total.reshape(lines, rows // lines, cols)
        first += n
        at += cols
    for mask, out in enumerate(outs):
        out[...] = total_s[z_ref[0] ^ mask].astype(out.dtype)


def split(deps, z, sums, lines):
    kind = sums[0][0].dtype
    specs = []
    for t in [t for terms in sums for t in terms]:
        if t.ndim == 3:
            specs.append(pl.BlockSpec((1,) + t.shape[1:], lambda i, *_: (0, 0, 0)))
        else:
            specs.append(pl.BlockSpec(t.shape, lambda i, *_: (0, 0)))
    rows = sums[0][0].shape[-2] // lines
    cols = sum(terms[0].shape[-1] for terms in sums)
    return run(
        functools.partial(split_kernel, lines, [len(terms) for terms in sums]),
        deps,
        [z],
        [t for terms in sums for t in terms],
        [jax.ShapeDtypeStruct((rows, cols), F32 if m == 0 else kind) for m in range(lines)],
        "split",
        2,
        grid=(1,),
        in_specs=specs,
        out_specs=[VMEM] * lines,
        scratch_shapes=[pltpu.VMEM((lines, rows, cols), F32)],
    )


def sum_kernel(*refs):
    total = refs[0][...].astype(F32)
    for ref in refs[1:-1]:
        total = total + ref[...].astype(F32)
    refs[-1][...] = total.reshape(refs[-1].shape).astype(refs[-1].dtype)


def second(deps, terms):
    _, rows, cols = terms[0].shape
    return run(
        sum_kernel,
        deps,
        [],
        terms,
        [jax.ShapeDtypeStruct((rows, cols), terms[0].dtype)],
        "second",
        2,
        grid=(1,),
        in_specs=[pl.BlockSpec((1, rows, cols), lambda i: (1, 0, 0))] * len(terms),
        out_specs=[VMEM],
        scratch_shapes=[],
    )[0]


def both(deps, terms):
    lines, rows, cols = terms[0].shape
    spec = pl.BlockSpec((1, rows, cols), lambda i: (i, 0, 0))
    return run(
        sum_kernel,
        deps,
        [],
        terms,
        [jax.ShapeDtypeStruct(terms[0].shape, terms[0].dtype)],
        "both",
        2,
        grid=(lines,),
        in_specs=[spec] * len(terms),
        out_specs=[spec],
        scratch_shapes=[],
    )[0]


AXES = ("wide", "narrow")


class Links:
    def __init__(self, mesh):
        self.wide = mesh.shape["wide"]
        self.narrow = mesh.shape["narrow"]
        self.count = self.wide * self.narrow
        self.pairwise = self.wide == 8 and self.narrow == 4
        self.lines = self.wide if self.pairwise else 1
        self.groups = (2, 2, 2, 2) if self.pairwise else (1,)

    def setup(self):
        if not self.pairwise:
            self.pos = jnp.zeros((1,), jnp.int32)
            return
        w = lax.axis_index("wide")
        self.z = lax.axis_index("narrow")
        near = jnp.where(w % 2 == 0, 2, 4)
        far = 6 - near
        order = [0, near, far, 6, 1, 1 ^ far, 1 ^ near, 7]
        self.pos = jnp.stack([w ^ m for m in order]).astype(jnp.int32)

    def slot(self, *marks):
        self.marks = list(marks)

    def swap(self, x, wide_mask=0, narrow_mask=0):
        masks = wide_mask if isinstance(wide_mask, tuple) else (wide_mask, wide_mask)
        pairs = []
        for w in range(self.wide):
            for z in range(self.narrow):
                pairs.append(
                    (w * self.narrow + z, (w ^ masks[w % 2]) * self.narrow + (z ^ narrow_mask))
                )
        return lax.ppermute(x, AXES, pairs)

    def line(self, x):
        if not self.pairwise:
            return [lax.all_gather(x, AXES, axis=0, tiled=True)]
        return [x] + [self.swap(x, 0, mask) for mask in (1, 2, 3)]

    def own(self, parts):
        if not self.pairwise:
            return parts
        (x,) = order(self.marks, self.z.reshape(1), parts, 1)
        return self.around(x)

    def around(self, x):
        return [x, self.swap(x, (2, 4)), self.swap(x, (4, 2)), self.swap(x, 1)]

    def onward(self, lines):
        if not self.pairwise:
            return lines
        own, near, far, own_core = lines
        if self.marks:
            near = after(near, self.marks)
            far = after(far, self.marks)
        return [own, near, far, self.swap(near, (4, 2)), own_core, self.swap(near, 1), self.swap(far, 1)]

    def core(self, lines):
        if not self.pairwise:
            return lines
        own, near, far, both, *core = lines
        if self.marks:
            both = after(both, self.marks)
        return [own, near, far, both, *core, self.swap(both, 1)]

    def add(self, *parts):
        total = parts[0].astype(F32)
        for p in parts[1:]:
            total = total + p.astype(F32)
        return total


class Sum:
    def __init__(self, links, parts):
        self.links = links
        self.parts = parts
        self.kind = parts[0].dtype

    def core(self, marks=()):
        links = self.links
        if not links.pairwise:
            self.src = self.out = lax.psum_scatter(self.parts[0][0].astype(F32), AXES, scatter_dimension=0, tiled=True)
            return (self.out,)
        send_a, send_b = self.parts[2], self.parts[3]
        if marks:
            send_a, send_b = after(send_a, marks), after(send_b, marks)
        self.got_b = links.swap(send_b, 1)
        self.got_a = links.swap(send_a, 1)
        return (self.got_b, self.got_a)

    def far(self):
        links = self.links
        if not links.pairwise:
            return (self.out,)
        self.src = both(links.marks, [self.parts[1], self.got_b])
        self.from_far = links.swap(self.src, (4, 2))
        return (self.from_far,)

    def near(self):
        links = self.links
        if not links.pairwise:
            return (self.out,)
        self.src = second(links.marks, [self.parts[0], self.got_a, self.from_far])
        self.from_near = links.swap(self.src, (2, 4))
        return (self.from_near,)

    def line(self, *more):
        links = self.links
        sums = (self,) + more
        if not links.pairwise:
            self.terms = [jnp.concatenate([x.out for x in sums], axis=1)]
            return self.terms
        terms = [[x.parts[0], x.got_a, x.from_far, x.from_near] for x in sums]
        mine, *others = split(links.marks, links.z.reshape(1), terms, links.narrow)
        self.src = mine
        self.terms = [mine] + [links.swap(x, 0, mask) for mask, x in enumerate(others, 1)]
        return self.terms[1:]

    def total(self):
        return self.links.add(*self.terms)


CHUNKS = 2
PARTS = FF // D
PAIRS = 6


def body(links, long_in, glob_in, lengths, ln1_gain, ln1_bias, w_qkv, qv_bias, rel_embed, w_out, out_bias, ln2_gain, ln2_bias, w_in, in_bias, w_down, down_bias, cot_long, cot_glob):
    links.setup()
    pos = links.pos
    groups = links.groups
    count = links.count
    micro = long_in.shape[0]
    r = w_qkv.shape[0]
    lens = lengths.reshape(micro)
    per = PARTS // CHUNKS
    first, second = 3 * FIRST, 3 * SECOND
    n_first, n_second = FIRST // 128, SECOND // 128

    vectors = [ln1_gain, ln1_bias, qv_bias, out_bias, ln2_gain, ln2_bias, down_bias, in_bias]
    w_in_parts = w_in.reshape(r, count, PARTS, r).transpose(0, 2, 1, 3).reshape(r, FF)

    links.slot()
    own_a0 = links.own(links.line(pack(w_qkv, rel_embed, vectors)))
    line_a1 = links.line(pack_next([own_a0[0]], w_qkv, w_out))
    ffn_shard = pack_ffn([], w_in_parts, w_down, CHUNKS)
    links.slot(own_a0[len(own_a0) // 2])
    most_a0 = links.onward(own_a0)
    links.slot(*line_a1[1:], ffn_shard)
    attn = [links.core(most_a0)]
    line_f = links.line(after(ffn_shard, [attn[0][-1]]))

    proj0, normed, rel_all, rel_turned, vec = project_first([], pos, long_in, glob_in, attn[0], r, first)
    links.slot(attn[0][-1])
    own_a1 = links.own(line_a1)
    mixed0, inv0, p0, pg0 = attend([own_a1[-1], own_a1[0]], lens, proj0, rel_all, 0)
    links.slot(proj0)
    most_a1 = links.onward(own_a1)
    links.slot(mixed0)
    if links.pairwise:
        line_f = order(links.marks, links.z.reshape(1), line_f, CHUNKS)
        own_f = [links.around(line_f[0])]
    else:
        own_f = [[line_f[0][:, 2 * per * D * c : 2 * per * D * (c + 1)]] for c in range(CHUNKS)]
    links.slot(mixed0)
    attn.append(links.core(most_a1))
    proj1 = project_next([mixed0, own_f[0][0]], pos, normed, vec, attn[1], second)
    mixed1, inv1, p1, pg1 = attend([], lens, proj1, rel_all, n_first)
    mixed = [mixed0, mixed1]
    if links.pairwise:
        own_f.append(links.around(after(line_f[1], [proj1])))
    links.slot(mixed1)
    most_f0 = links.onward(own_f[0])
    most_f1 = links.onward(own_f[1])
    res, n2, g_ffn = mix_out(
        [most_f0[0]], pos, lens, long_in, glob_in, cot_long, cot_glob, vec, mixed, attn[1], second
    )
    links.slot(n2)
    ffn0 = links.core(most_f0)
    y0, gn0, gb0, *gw0 = ffn([], pos, n2, g_ffn, vec, ffn0, 0, per, groups)
    links.slot(y0)
    ffn1 = links.core(most_f1)
    sum0 = Sum(links, gw0)
    y1, gn1, gb1, *gw1 = ffn([y0], pos, n2, g_ffn, vec, ffn1, per, per, groups)
    core0 = sum0.core()
    sum1 = Sum(links, gw1)
    links.slot(y1)
    far0 = sum0.far()
    block_long, block_glob, gres, gmix, small2, gw_out = mid(
        [sum0.src], pos, lens, res, g_ffn, vec, [y0, y1], [gn0, gn1], mixed, attn[1], second, long_in.shape, glob_in.shape
    )
    core1 = sum1.core()
    links.slot(gmix)
    near0 = sum0.near()
    sum1.far()
    gproj1, grel1 = attend_back([sum0.src, sum1.src], proj1, rel_turned, gmix, mixed1, inv1, p1, pg1, n_first, 0, n_second)
    links.slot(gproj1)
    sum1.near()
    gw_a1 = weight_grad([sum1.src, *near0], pos, normed, [gproj1], [gw_out], groups)
    sum2 = Sum(links, gw_a1)
    sum2.core()
    links.slot(gw_a1[0])
    line01 = sum0.line(sum1)
    gproj0, grel0 = attend_back([sum0.src], proj0, rel_turned, gmix, mixed0, inv0, p0, pg0, 0, 0, n_first)
    links.slot(gproj0)
    sum2.far()
    grad_long, grad_glob, small1, small_qv = input_grad(
        [sum2.src], pos, long_in, glob_in, gres, vec, [gproj0, gproj1], attn
    )
    links.slot(small1)
    near2 = sum2.near()
    gw_a0 = weight_grad(
        [sum2.src, *line01], pos, normed, [gproj0], [grel0, grel1, small2, small1, small_qv, gb0, gb1], groups, r
    )
    sum3 = Sum(links, gw_a0)
    sum3.core(near2)
    links.slot(gw_a0[0])
    sum3.far()
    links.slot(sum3.src)
    sum2.line()
    links.slot(sum2.src)
    sum3.near()
    g_in, g_down = unpack_ffn([sum3.src], sum0.terms, CHUNKS)
    g_in = g_in.reshape(r, PARTS, count, r).transpose(0, 2, 1, 3).reshape(r, FF)
    links.slot()
    sum3.line()
    order_out = [ln1_gain, ln1_bias, qv_bias, ln2_gain, ln2_bias, out_bias, down_bias, in_bias]
    g_qkv, g_out, g_rel, g_gain1, g_bias1, g_qv, g_gain2, g_bias2, g_out_b, g_down_b, g_in_b = unpack(
        sum3.terms, sum2.terms, [v.shape[0] for v in order_out]
    )
    return (
        block_long, block_glob, grad_long, grad_glob,
        g_gain1, g_bias1, g_qkv, g_qv, g_rel, g_out, g_out_b,
        g_gain2, g_bias2, g_in, g_in_b, g_down, g_down_b,
    )


def solution(mesh):
    rows = P(None, AXES, None, None)
    vec = P(AXES)
    mat = P(AXES, None)
    placed = (rows, rows, P(None, AXES), vec, vec, mat, vec, mat, mat, vec, vec, vec, mat, vec, mat, vec, rows, rows)
    return jax.shard_map(
        functools.partial(body, Links(mesh)),
        mesh=mesh,
        in_specs=placed,
        out_specs=(rows, rows, rows, rows, vec, vec, mat, vec, mat, mat, vec, vec, vec, mat, vec, mat, vec),
        check_vma=False,
    )
```

```python
import functools
import jax
import jax.numpy as jnp
from jax import lax
from jax.experimental import pallas as pl
from jax.experimental.pallas import tpu as pltpu
from jax.sharding import PartitionSpec as P

HEAD_DIM = 64
RADIUS = 84
STRIDE = 16
SEQ = 512
GLOB = 32
RELS = 169
T = GLOB + SEQ
D = 768
FF = 3072
PAIRS = 6
LABELS = 256
LEAD = 4
BACK_LEAD = 3
LABEL_END = LEAD + RELS
EPS = 1e-06
NEG = -1e30
F32 = jnp.float32
BF16 = jnp.bfloat16
VMEM_LIMIT = 63 << 20
WINDOWS = ((0, 0, 256, 328, 0), (0, 0, 384, 72, 0), (1, 160, 384, 8, 352), (1, 288, 256, 8, 224))
OFFSETS = (0, 256, 640, 1024)
WAYS = 3 * 128
VEC_AT = 176
GAIN1, BIAS1, QV, OUT_B, GAIN2, BIAS2, DOWN_B, IN_B, VECS = 0, 1, 2, 4, 5, 6, 7, 8, 16
P_COLS = 1280
NN = (((1,), (0,)), ((), ()))
NT = (((1,), (1,)), ((), ()))
TN = (((0,), (0,)), ((), ()))


def dot(a, b, dims=NN):
    return lax.dot_general(a, b, dims, preferred_element_type=F32)


def run(kernel, deps, prefetch, inputs, out_shape, name, cost, grid, in_specs, out_specs, scratch_shapes):
    n = len(prefetch)

    def with_deps(*refs):
        kernel(*refs[:n], *refs[n + len(deps) :])

    anywhere = pl.BlockSpec(memory_space=pl.ANY)
    return pl.pallas_call(
        with_deps,
        grid_spec=pltpu.PrefetchScalarGridSpec(
            num_scalar_prefetch=n,
            grid=grid,
            in_specs=[anywhere] * len(deps) + in_specs,
            out_specs=out_specs,
            scratch_shapes=scratch_shapes,
        ),
        out_shape=out_shape,
        compiler_params=pltpu.CompilerParams(vmem_limit_bytes=VMEM_LIMIT),
        cost_estimate=pl.CostEstimate(flops=int(cost * 1.15e9), bytes_accessed=1 << 20, transcendentals=0),
        name=name,
    )(*prefetch, *deps, *inputs)


def after(x, deps):
    anywhere = pl.BlockSpec(memory_space=pl.ANY)
    return pl.pallas_call(
        lambda *refs: None,
        in_specs=[anywhere] * (1 + len(deps)),
        out_specs=anywhere,
        out_shape=jax.ShapeDtypeStruct(x.shape, x.dtype),
        input_output_aliases={0: 0},
        name="after",
    )(x, *deps)


def iota(shape, dim):
    return lax.broadcasted_iota(jnp.int32, shape, dim)


def norm_stats(x):
    cen = x - jnp.mean(x, axis=1, keepdims=True)
    rstd = lax.rsqrt(jnp.mean(cen * cen, axis=1, keepdims=True) + EPS)
    return cen * rstd, rstd


def norm_back(grad, xhat, rstd, gain):
    gg = grad * gain
    return rstd * (
        gg - jnp.mean(gg, axis=1, keepdims=True) - xhat * jnp.mean(gg * xhat, axis=1, keepdims=True)
    )


def tiles(cols, size=256):
    return [slice(at, min(at + size, cols)) for at in range(0, cols, size)]


def live_mask(length, cols):
    row = iota((T, cols), 0)
    glob_count = (length + STRIDE - 1) // STRIDE
    return row < jnp.where(row < GLOB, glob_count, length + GLOB)


def load_rows(pieces, pos_ref, lines, dst, sems, first_col, start=True):
    rows = dst.shape[0] // lines
    cols = dst.shape[1]
    copies = []
    k = 0
    for piece in pieces:
        for i in range(piece.shape[0] // rows):
            to = pl.multiple_of(pos_ref[k] * rows, 16)
            copies.append(
                pltpu.make_async_copy(
                    piece.at[pl.ds(i * rows, rows), pl.ds(first_col, cols)],
                    dst.at[pl.ds(to, rows), :],
                    sems.at[k],
                )
            )
            k += 1
    if start:
        for copy in copies:
            copy.start()
    return copies


FIRST = 2 * 128
SECOND = D - FIRST


def owner_order(rows):
    k = iota((D, 1), 0)
    late = (k >= D // 2).astype(jnp.int32)
    k = k - late * (D // 2)
    owner = ((k.astype(F32) + 0.5) * (1.0 / rows)).astype(jnp.int32)
    col = rows * owner + k + late * rows
    return (iota((D, D), 1) == col).astype(F32).astype(BF16)


def project_kernel(lines, n_pieces, first, rows, pos_ref, *rest):
    if first:
        long_ref, glob_ref = rest[:2]
    else:
        normed_ref, vec_ref = rest[:2]
    pieces = rest[2 : 2 + n_pieces]
    if first:
        proj_ref, normed_ref, rel_ref, relt_ref, vec_ref, w_s, sems = rest[2 + n_pieces :]
    else:
        proj_ref, w_s, sems = rest[2 + n_pieces :]
    cols = proj_ref.shape[1]
    width = cols // 3
    copies = load_rows(pieces, pos_ref, lines, w_s, sems.at[0], 0)
    if first:
        for copy in load_rows(pieces, pos_ref, lines, rel_ref, sems.at[1], cols):
            copy.wait()
        turned = rel_ref[...].astype(F32).T
        vec_ref[...] = turned[VEC_AT : VEC_AT + VECS]
        drop = LEAD - BACK_LEAD
        labels = jnp.concatenate([turned[drop:], turned[:drop]], axis=0)
        label = iota((LABELS, D), 0) - BACK_LEAD
        relt_ref[...] = jnp.where((label >= 0) & (label < RELS), labels, 0.0).astype(BF16)
        a, b = vec_ref[QV : QV + 1], vec_ref[QV + 1 : QV + 2]
        half = D // 2
        sides = jnp.concatenate(
            [
                jnp.concatenate([a[:, :half], b[:, :half]], axis=1),
                jnp.concatenate([a[:, half:], b[:, half:]], axis=1),
            ],
            axis=0,
        )
        vec_ref[QV : QV + 2] = dot(sides.astype(BF16), owner_order(rows))
        for s in range(long_ref.shape[0]):
            for part, at, size in ((glob_ref, T * s, GLOB), (long_ref, T * s + GLOB, SEQ)):
                xhat, _ = norm_stats(part[s, 0].astype(F32))
                normed_ref[at : at + size] = (
                    xhat * vec_ref[GAIN1 : GAIN1 + 1] + vec_ref[BIAS1 : BIAS1 + 1]
                ).astype(BF16)
    own = slice(0, width) if first else slice(D - width, D)
    full_bias = jnp.concatenate(
        [vec_ref[QV : QV + 1, own], jnp.zeros((1, width), F32), vec_ref[QV + 1 : QV + 2, own]], axis=1
    )
    for copy in copies:
        copy.wait()
    for c in tiles(cols):
        out = (dot(normed_ref[...], w_s[:, c]) + full_bias[:, c]).astype(BF16)
        for at in range(c.start, c.stop, 128):
            to = by_pair(at, width)
            proj_ref[:, to : to + 128] = out[:, at - c.start : at - c.start + 128]


def by_pair(col, width):
    return WAYS * (col % width // 128) + 128 * (col // width)


VMEM = pl.BlockSpec(memory_space=pltpu.VMEM)
ANY = pl.BlockSpec(memory_space=pl.ANY)


def project_first(deps, pos, long_in, glob_in, pieces, owned, cols):
    rows = long_in.shape[0] * T
    lines = pos.shape[0]
    shape = lambda *dims: jax.ShapeDtypeStruct(dims, BF16)
    return run(
        functools.partial(project_kernel, lines, len(pieces), True, owned),
        deps,
        [pos],
        [long_in, glob_in, *pieces],
        [
            shape(rows, cols),
            shape(rows, D),
            shape(D, LABELS),
            shape(LABELS, D),
            jax.ShapeDtypeStruct((VECS, D), F32),
        ],
        "project",
        9,
        grid=(1,),
        in_specs=[VMEM] * 2 + [ANY] * len(pieces),
        out_specs=[VMEM] * 5,
        scratch_shapes=[pltpu.VMEM((D, cols), BF16), pltpu.SemaphoreType.DMA((2, lines))],
    )


def project_next(deps, pos, normed, vec, pieces, cols):
    rows = normed.shape[0]
    lines = pos.shape[0]
    return run(
        functools.partial(project_kernel, lines, len(pieces), False, 0),
        deps,
        [pos],
        [normed, vec, *pieces],
        [jax.ShapeDtypeStruct((rows, cols), BF16)],
        "project",
        8,
        grid=(1,),
        in_specs=[VMEM] * 2 + [ANY] * len(pieces),
        out_specs=[VMEM],
        scratch_shapes=[pltpu.VMEM((D, cols), BF16), pltpu.SemaphoreType.DMA((2, lines))],
    )[0]


def flip_matrix(size):
    row, col = iota((size, size), 0), iota((size, size), 1)
    return ((row // 128 == col // 128) & (row % 128 + col % 128 == 127)).astype(F32).astype(BF16)


def by_head(x):
    even = iota(x.shape, 1) < HEAD_DIM
    return jnp.concatenate([jnp.where(even, x, 0.0), jnp.where(even, 0.0, x)], axis=0)


def by_lane(x):
    half = x.shape[0] // 2
    even = iota((half, x.shape[1]), 1) < HEAD_DIM
    return jnp.where(even, x[:half], x[half:])


def spread(x, b):
    _, _, width, shift, _ = WINDOWS[b]
    shift = shift if shift < 256 else shift - 384
    lane = iota((64, 128), 1)
    none = jnp.full((64, 128), NEG, F32)
    parts = []
    for at in range(0, 256, 64):
        start = shift + at % 128
        turned = pltpu.roll(x[at : at + 64], start % 256, 1, stride=1, stride_axis=0)
        low, high = turned[:, :128], turned[:, 128:]
        if start < 0:
            cols = [low, jnp.where(lane < 64, high, NEG), none]
        elif start + 64 + LABEL_END <= 256:
            cols = [low, high, none]
        elif start >= 128:
            cols = [none, high, low]
        else:
            cols = [jnp.where(lane >= 64, low, NEG), high, jnp.where(lane < 64, low, NEG)]
        parts.append(jnp.concatenate(cols[: width // 128], axis=1))
    return jnp.concatenate(parts, axis=0)


def collect(cols, b):
    _, _, width, shift, _ = WINDOWS[b]
    shift = shift if shift < 256 else shift - 384
    lane = iota((64, 128), 1)
    parts = []
    for at in range(0, 256, 64):
        start = shift + 64 - at % 128
        tiles_ = [c[at : at + 64] for c in cols]
        if start < 0:
            low, high = tiles_[0], jnp.where(lane < 64, tiles_[1], 0.0)
        elif start + 64 + LABEL_END <= 256:
            low, high = tiles_[0], tiles_[1]
        elif start >= 128:
            low, high = tiles_[2], tiles_[1]
        elif len(tiles_) > 2:
            low, high = jnp.where(lane >= 64, tiles_[0], tiles_[2]), tiles_[1]
        else:
            low, high = jnp.where(lane >= 64, tiles_[0], 0.0), tiles_[1]
        back = (BACK_LEAD - LEAD - 63 - start) % 256
        parts.append(
            pltpu.roll(jnp.concatenate([low, high], axis=1), back, 1, stride=1, stride_axis=0)
        )
    return jnp.concatenate(parts, axis=0)


def zero_glob(x, at):
    cols = [x[:, 128 * i : 128 * (i + 1)] for i in range(x.shape[1] // 128)]
    lane = iota(cols[0].shape, 1) - at % 128
    cols[at // 128] = jnp.where((lane >= 0) & (lane < GLOB), 0.0, cols[at // 128])
    return cols


def attend_kernel(len_ref, qkv_ref, rel_ref, mix_ref, inv_ref, p_ref, pg_ref, k_s, v_s, rel_s):
    dead = jnp.where(live_mask(len_ref[pl.program_id(0)], 128), 0.0, NEG)
    flag = iota((T, 128), 1) == 0
    k = jnp.concatenate(
        [qkv_ref[:, 128:256], jnp.where(flag, dead, 0.0).astype(BF16)], axis=1
    )
    v = jnp.concatenate([qkv_ref[:, 256:384], jnp.ones((T, 128), BF16)], axis=1)
    for s, m in ((k_s, k), (v_s, v)):
        s[0] = m
        s[1, :SEQ] = m[GLOB:]
        s[1, SEQ:] = m[:GLOB]
    label = iota((128, LABELS), 1)
    outside = ((label < LEAD) | (label >= LEAD + RELS)) & (iota((128, LABELS), 0) == 0)
    rel_s[:128] = rel_ref[...]
    rel_s[128:] = jnp.where(outside, NEG, 0.0).astype(BF16)
    flip = flip_matrix(256)

    def queries(rows):
        x = by_head(qkv_ref[rows, :128].astype(F32) * 0.125)
        one = (iota(x.shape, 1) == 0).astype(F32)
        return jnp.concatenate([x, one], axis=1).astype(BF16)

    def weights(scores):
        return jnp.exp(scores - jnp.max(scores, axis=1, keepdims=True)).astype(BF16)

    rows = [slice(0, GLOB)] + [slice(GLOB + 128 * b, GLOB + 128 * (b + 1)) for b in range(4)]
    wins = [(0, slice(0, T))] + [(arr, slice(first, first + width)) for arr, first, width, _, _ in WINDOWS]
    qs = [queries(r) for r in rows]
    scores = [dot(q, k_s[arr, win], NT) for q, (arr, win) in zip(qs, wins)]
    biases = [dot(q, rel_s[...]) for q in qs[1:]]
    for b, window in enumerate(WINDOWS):
        bias = zero_glob(spread(biases[b], b), window[-1])
        scores[b + 1] = scores[b + 1] + jnp.concatenate(bias, axis=1)
    ps = [weights(x) for x in scores]
    pg_ref[0, 0] = ps[0]
    outs = [dot(p, v_s[arr, win]) for p, (arr, win) in zip(ps, wins)]
    turned = [dot(flip, p) for p in ps[1:]]
    for r, out in zip(rows, outs):
        inv = by_lane(1.0 / out[:, 128:])
        inv_ref[r] = inv
        mix_ref[r] = (by_lane(out[:, :128]) * inv).astype(BF16)
    for b, p in enumerate(turned):
        p_ref[0, 0, :, OFFSETS[b] : OFFSETS[b] + p.shape[1]] = p.astype(BF16)


def attend(deps, lengths, proj, rel, first_pair):
    rows = proj.shape[0]
    seqs = rows // T
    pairs = proj.shape[1] // WAYS
    return run(
        attend_kernel,
        deps,
        [lengths],
        [proj, rel],
        [
            jax.ShapeDtypeStruct((rows, pairs * 128), BF16),
            jax.ShapeDtypeStruct((rows, pairs * 128), F32),
            jax.ShapeDtypeStruct((seqs, pairs, 256, P_COLS), BF16),
            jax.ShapeDtypeStruct((seqs, pairs, 2 * GLOB, T), BF16),
        ],
        "attend",
        6.2 * pairs,
        grid=(seqs, pairs),
        in_specs=[
            pl.BlockSpec((T, WAYS), lambda s, p, *_: (s, p)),
            pl.BlockSpec((128, LABELS), lambda s, p, *_: (first_pair + p, 0)),
        ],
        out_specs=[
            pl.BlockSpec((T, 128), lambda s, p, *_: (s, p)),
            pl.BlockSpec((T, 128), lambda s, p, *_: (s, p)),
            pl.BlockSpec((1, 1, 256, P_COLS), lambda s, p, *_: (s, p, 0, 0)),
            pl.BlockSpec((1, 1, 2 * GLOB, T), lambda s, p, *_: (s, p, 0, 0)),
        ],
        scratch_shapes=[
            pltpu.VMEM((2, T, 256), BF16),
            pltpu.VMEM((2, T, 256), BF16),
            pltpu.VMEM((256, LABELS), BF16),
        ],
    )


def attend_back_kernel(qkv_ref, relt_ref, do_ref, o_ref, inv_ref, p_ref, pg_ref, grad_ref, grel_ref, gk_s, gv_s, k_s, v_s):
    k = qkv_ref[:, 128:256]
    v = qkv_ref[:, 256:384]
    for s, m in ((k_s, k), (v_s, v)):
        s[0] = m
        s[1, :SEQ] = m[GLOB:]
        s[1, SEQ:] = m[:GLOB]
    flip = flip_matrix(128)

    @pl.when(pl.program_id(1) == 0)
    def _():
        grel_ref[...] = jnp.zeros_like(grel_ref)

    ones = jnp.ones((256, 128), BF16)

    def score_grads(do, o, p, v_win):
        prod = by_head(do * o)
        high = prod.astype(BF16)
        low = (prod - high.astype(F32)).astype(BF16)
        centre = dot(jnp.concatenate([high, low], axis=1), ones)
        dom = by_head(do).astype(BF16)
        dp = dot(dom, v_win, NT)
        width = dp.shape[1]
        cols = [dp[:, c] - centre[:, : c.stop - c.start] for c in tiles(width, 128)]
        return dom, p.astype(F32) * jnp.concatenate(cols, axis=1)

    do = (do_ref[:GLOB].astype(F32) * inv_ref[:GLOB]).astype(BF16).astype(F32)
    p = pg_ref[0, 0]
    dom, ds = score_grads(do, o_ref[:GLOB].astype(F32), p, v_s[0])
    ds = ds.astype(BF16)
    qm = by_head(qkv_ref[:GLOB, :128].astype(F32)).astype(BF16)
    grad_ref[:GLOB, :128] = (by_lane(dot(ds, k_s[0])) * 0.125).astype(BF16)
    gk_s[...] = dot(ds, qm, TN)
    gv_s[...] = dot(p, dom, TN)
    blocks = range(4)
    rows = [slice(GLOB + 128 * b, GLOB + 128 * (b + 1)) for b in blocks]
    wins = [(arr, slice(first, first + width)) for arr, first, width, _, _ in WINDOWS]
    turned = [
        dot(
            flip,
            jnp.concatenate(
                [
                    qkv_ref[r, :128],
                    (do_ref[r].astype(F32) * inv_ref[r]).astype(BF16),
                    o_ref[r],
                ],
                axis=1,
            ),
        )
        for r in rows
    ]
    qms = [by_head(x[:, :128]) for x in turned]
    qm_ts = [x.T.astype(BF16) for x in qms]
    qms = [x.astype(BF16) for x in qms]
    ps = [p_ref[0, 0, :, OFFSETS[b] : OFFSETS[b] + WINDOWS[b][2]] for b in blocks]
    grads = [
        score_grads(x[:, 128:256], x[:, 256:], p, v_s[arr, win])
        for x, p, (arr, win) in zip(turned, ps, wins)
    ]
    doms = [dom for dom, _ in grads]
    dss = [ds.astype(BF16) for _, ds in grads]
    labs = []
    for b, window in enumerate(WINDOWS):
        labs.append(collect(zero_glob(grads[b][1], window[-1]), b).astype(BF16))
    gqs = [
        by_lane(dot(ds, k_s[arr, win]) + dot(lab, relt_ref[...])) * 0.125
        for ds, lab, (arr, win) in zip(dss, labs, wins)
    ]
    gks = [dot(ds, qm, TN) for ds, qm in zip(dss, qms)]
    gvs = [dot(p, dom, TN) for p, dom in zip(ps, doms)]
    grel = sum(dot(qm_t, lab) for qm_t, lab in zip(qm_ts, labs))
    grel_ref[...] += grel * 0.125
    for r, gq in zip(rows, gqs):
        grad_ref[r, :128] = dot(flip, gq.astype(BF16)).astype(BF16)
    for b, (arr, first, width, _, _) in enumerate(WINDOWS):
        win = wins[b][1]
        for acc, part in ((gk_s, gks[b]), (gv_s, gvs[b])):
            if arr == 0:
                acc[win] += part
            else:
                acc[GLOB + first : T] += part[: width - GLOB]
                acc[:GLOB] += part[width - GLOB :]
    grad_ref[:, 128:256] = (gk_s[...] * 0.125).astype(BF16)
    grad_ref[:, 256:384] = gv_s[...].astype(BF16)


def attend_back(deps, proj, relt, gmixed, mixed, inv, p, pg, first_pair, start, pairs):
    rows = proj.shape[0]
    seqs = rows // T
    return run(
        attend_back_kernel,
        deps,
        [],
        [proj, relt, gmixed, mixed, inv, p, pg],
        [
            jax.ShapeDtypeStruct((rows, pairs * WAYS), BF16),
            jax.ShapeDtypeStruct((pairs * 128, LABELS), F32),
        ],
        "attend_back",
        8 * pairs,
        grid=(pairs, seqs),
        in_specs=[
            pl.BlockSpec((T, WAYS), lambda p, s: (s, start + p)),
            pl.BlockSpec((LABELS, 128), lambda p, s: (0, first_pair + start + p)),
            pl.BlockSpec((T, 128), lambda p, s: (s, first_pair + start + p)),
            pl.BlockSpec((T, 128), lambda p, s: (s, start + p)),
            pl.BlockSpec((T, 128), lambda p, s: (s, start + p)),
            pl.BlockSpec((1, 1, 256, P_COLS), lambda p, s: (s, start + p, 0, 0)),
            pl.BlockSpec((1, 1, 2 * GLOB, T), lambda p, s: (s, start + p, 0, 0)),
        ],
        out_specs=[pl.BlockSpec((T, WAYS), lambda p, s: (s, p)), pl.BlockSpec((128, LABELS), lambda p, s: (p, 0))],
        scratch_shapes=[
            pltpu.VMEM((T, 128), F32),
            pltpu.VMEM((T, 128), F32),
            pltpu.VMEM((2, T, 128), BF16),
            pltpu.VMEM((2, T, 128), BF16),
        ],
    )


def mix_out_kernel(lines, n_pieces, first_col, n_mix, pos_ref, len_ref, long_ref, glob_ref, clong_ref, cglob_ref, vec_ref, *rest):
    mixed = rest[:n_mix]
    pieces = rest[n_mix : n_mix + n_pieces]
    res_ref, n2_ref, g_ref, w_s, sems = rest[n_mix + n_pieces :]
    copies = load_rows(pieces, pos_ref, lines, w_s, sems, first_col)
    seqs = long_ref.shape[0]
    for s in range(seqs):
        live = live_mask(len_ref[s], D)
        at = T * s
        g_ref[at : at + GLOB] = jnp.where(live[:GLOB], cglob_ref[s, 0].astype(F32), 0.0).astype(BF16)
        g_ref[at + GLOB : at + T] = jnp.where(live[GLOB:], clong_ref[s, 0].astype(F32), 0.0).astype(BF16)
    for copy in copies:
        copy.wait()
    for c in tiles(D):
        acc = vec_ref[OUT_B : OUT_B + 1, c]
        at = 0
        for m in mixed:
            acc = acc + dot(m[...], w_s[at : at + m.shape[1], c])
            at += m.shape[1]
        res_ref[:, c] = acc
    for s in range(seqs):
        for part, at, size in ((glob_ref, T * s, GLOB), (long_ref, T * s + GLOB, SEQ)):
            res = res_ref[at : at + size] + part[s, 0].astype(F32)
            res_ref[at : at + size] = res
            xhat, _ = norm_stats(res)
            n2_ref[at : at + size] = (
                xhat * vec_ref[GAIN2 : GAIN2 + 1] + vec_ref[BIAS2 : BIAS2 + 1]
            ).astype(BF16)


def mix_out(deps, pos, lengths, long_in, glob_in, cot_long, cot_glob, vec, mixed, pieces, first_col):
    rows = long_in.shape[0] * T
    lines = pos.shape[0]
    return run(
        functools.partial(mix_out_kernel, lines, len(pieces), first_col, len(mixed)),
        deps,
        [pos, lengths],
        [long_in, glob_in, cot_long, cot_glob, vec, *mixed, *pieces],
        [
            jax.ShapeDtypeStruct((rows, D), F32),
            jax.ShapeDtypeStruct((rows, D), BF16),
            jax.ShapeDtypeStruct((rows, D), BF16),
        ],
        "mix_out",
        10,
        grid=(1,),
        in_specs=[VMEM] * (5 + len(mixed)) + [ANY] * len(pieces),
        out_specs=[VMEM] * 3,
        scratch_shapes=[pltpu.VMEM((D, D), BF16), pltpu.SemaphoreType.DMA((lines,))],
    )


def store_rows(src, outs, rows, src_pos_ref, sems, first_col):
    cols = src.shape[1]
    copies = []
    k = 0
    for out in outs:
        for i in range(out.shape[0]):
            start = pl.multiple_of(src_pos_ref[k] * rows, 16)
            copies.append(
                pltpu.make_async_copy(
                    src.at[pl.ds(start, rows), :], out.at[i, :, pl.ds(first_col, cols)], sems.at[k]
                )
            )
            k += 1
    return copies


def gelu_parts(v):
    cdf = 0.5 * (1.0 + lax.erf(v * 0.7071067811865476))
    pdf = jnp.exp(v * v * -0.5) * 0.3989422804014327
    return v * cdf, cdf + v * pdf


def ffn_kernel(lines, n_in, n_parts, n_out, first, pos_ref, n2_ref, g_ref, vec_ref, *rest):
    pieces = rest[:n_in]
    y_ref, gn2_ref, gb_ref = rest[n_in : n_in + 3]
    outs = rest[n_in + 3 : n_in + 3 + n_out]
    w_in_s, w_down_s, act_s, gpre_s, gw_s, y_s, gn2_s, sems, out_sems = rest[n_in + 3 + n_out :]
    part = pl.program_id(0)
    piece_rows = outs[0].shape[1]

    def weights(i, start):
        copies = load_rows(pieces, pos_ref, lines, w_in_s.at[i], sems.at[2 * i], i * D, start)
        return copies + load_rows(
            pieces, pos_ref, lines, w_down_s.at[i], sems.at[2 * i + 1], (n_parts + i) * D, start
        )

    @pl.when(part == 0)
    def _():
        for i in range(n_parts):
            weights(i, True)

    for i in range(n_parts):

        @pl.when(part == i)
        def _(i=i):
            for copy in weights(i, False):
                copy.wait()


    for c in tiles(D):
        pre = dot(n2_ref[...], w_in_s[part, :, c]) + vec_ref[pl.ds(IN_B + first + part, 1), c]
        act, slope = gelu_parts(pre)
        act_s[:, c] = act.astype(BF16)
        gpre = (dot(g_ref[...], w_down_s[part, c, :], NT) * slope).astype(BF16)
        gpre_s[:, c] = gpre
        gb_ref[:, c] = jnp.sum(gpre.astype(F32), axis=0, keepdims=True)

    def flush(which):
        first = pl.multiple_of((which * n_parts + part) * D, 128)
        return store_rows(gw_s.at[which], outs, piece_rows, pos_ref, out_sems.at[which], first)

    for which, (lhs, rhs) in enumerate(((n2_ref, gpre_s), (act_s, g_ref))):
        for c in tiles(D):
            gw_s[which, :, c] = dot(lhs[...], rhs[:, c], TN).astype(BF16)
        for copy in flush(which):
            copy.start()

    def outputs(first_part, last_part):
        for c in tiles(D):
            for total_s, out_ref, part_sum in (
                (y_s, y_ref, dot(act_s[...], w_down_s[part, :, c])),
                (gn2_s, gn2_ref, dot(gpre_s[...], w_in_s[part, c, :], NT)),
            ):
                if not first_part:
                    part_sum = total_s[:, c] + part_sum
                if last_part:
                    out_ref[:, c] = part_sum.astype(BF16)
                else:
                    total_s[:, c] = part_sum

    for i in range(n_parts):
        pl.when(part == i)(functools.partial(outputs, i == 0, i == n_parts - 1))
    for which in range(2):
        for copy in flush(which):
            copy.wait()


def ffn(deps, pos, n2, g, vec, pieces, first, n_parts, out_groups):
    rows = n2.shape[0]
    lines = pos.shape[0]
    full = pl.BlockSpec((rows, D), lambda q, *_: (0, 0))
    return run(
        functools.partial(ffn_kernel, lines, len(pieces), n_parts, len(out_groups), first),
        deps,
        [pos],
        [n2, g, vec, *pieces],
        [
            jax.ShapeDtypeStruct((rows, D), BF16),
            jax.ShapeDtypeStruct((rows, D), BF16),
            jax.ShapeDtypeStruct((1, n_parts * D), F32),
        ]
        + [jax.ShapeDtypeStruct((k, D // lines, 2 * n_parts * D), BF16) for k in out_groups],
        "ffn",
        28,
        grid=(n_parts,),
        in_specs=[full, full, VMEM] + [ANY] * len(pieces),
        out_specs=[full, full, pl.BlockSpec((1, D), lambda q, *_: (0, q))] + [ANY] * len(out_groups),
        scratch_shapes=[
            pltpu.VMEM((n_parts, D, D), BF16),
            pltpu.VMEM((n_parts, D, D), BF16),
            pltpu.VMEM((rows, D), BF16),
            pltpu.VMEM((rows, D), BF16),
            pltpu.VMEM((2, D, D), BF16),
            pltpu.VMEM((rows, D), F32),
            pltpu.VMEM((rows, D), F32),
            pltpu.SemaphoreType.DMA((2 * n_parts, lines)),
            pltpu.SemaphoreType.DMA((2, lines)),
        ],
    )


def mid_kernel(lines, n_in, first_col, n_mix, n_part, pos_ref, len_ref, res_ref, g_ref, vec_ref, *rest):
    ys = rest[:n_part]
    gns = rest[n_part : 2 * n_part]
    mixed = rest[2 * n_part : 2 * n_part + n_mix]
    rest = rest[2 * n_part + n_mix :]
    pieces = rest[:n_in]
    long_ref, glob_ref, gres_ref, gmix_ref, small_ref, gw_ref = rest[n_in : n_in + 6]
    w_s, gattn_s, gw_s, sems = rest[n_in + 6 :]
    s = pl.program_id(0)

    @pl.when(s == 0)
    def _():
        for copy in load_rows(pieces, pos_ref, lines, w_s, sems, first_col):
            copy.wait()
        gw_s[...] = jnp.zeros_like(gw_s)
        small_ref[...] = jnp.zeros_like(small_ref)

    live = live_mask(len_ref[s], D)
    res = res_ref[...]
    y = res + vec_ref[DOWN_B : DOWN_B + 1]
    gn2 = gns[0][...].astype(F32)
    for ref in ys:
        y = y + ref[...].astype(F32)
    for ref in gns[1:]:
        gn2 = gn2 + ref[...].astype(F32)
    y = jnp.where(live, y, 0.0).astype(BF16)
    glob_ref[0, 0] = y[:GLOB]
    long_ref[0, 0] = y[GLOB:]
    xhat, rstd = norm_stats(res)
    g = g_ref[...].astype(F32)
    gres = g + norm_back(gn2, xhat, rstd, vec_ref[GAIN2 : GAIN2 + 1])
    gres_ref[...] = gres
    gattn = gres.astype(BF16)
    gattn_s[...] = gattn
    small_ref[0:1] += jnp.sum(gn2 * xhat, axis=0, keepdims=True)
    small_ref[1:2] += jnp.sum(gn2, axis=0, keepdims=True)
    small_ref[2:3] += jnp.sum(gattn.astype(F32), axis=0, keepdims=True)
    small_ref[3:4] += jnp.sum(g, axis=0, keepdims=True)

    for c in tiles(D):
        gmix_ref[:, c] = dot(gattn_s[...], w_s[c, :], NT).astype(BF16)
        at = 0
        for m in mixed:
            gw_s[at : at + m.shape[1], c] += dot(m[...], gattn_s[:, c], TN)
            at += m.shape[1]

    @pl.when(s == pl.num_programs(0) - 1)
    def _():
        gw_ref[...] = gw_s[...].astype(BF16)


def mid(deps, pos, lengths, res, g, vec, ys, gns, mixed, pieces, first_col, long_shape, glob_shape):
    rows = res.shape[0]
    lines = pos.shape[0]
    spec = pl.BlockSpec((T, D), lambda s, *_: (s, 0))
    return run(
        functools.partial(mid_kernel, lines, len(pieces), first_col, len(mixed), len(ys)),
        deps,
        [pos, lengths],
        [res, g, vec, *ys, *gns, *mixed, *pieces],
        [
            jax.ShapeDtypeStruct(long_shape, BF16),
            jax.ShapeDtypeStruct(glob_shape, BF16),
            jax.ShapeDtypeStruct((rows, D), F32),
            jax.ShapeDtypeStruct((rows, D), BF16),
            jax.ShapeDtypeStruct((8, D), F32),
            jax.ShapeDtypeStruct((D, D), BF16),
        ],
        "mid",
        17,
        grid=(rows // T,),
        in_specs=[spec, spec, VMEM]
        + [spec] * (2 * len(ys))
        + [pl.BlockSpec((T, m.shape[1]), lambda s, *_: (s, 0)) for m in mixed]
        + [ANY] * len(pieces),
        out_specs=[
            pl.BlockSpec((1, 1, SEQ, D), lambda s, *_: (s, 0, 0, 0)),
            pl.BlockSpec((1, 1, GLOB, D), lambda s, *_: (s, 0, 0, 0)),
            spec,
            spec,
            pl.BlockSpec((8, D), lambda s, *_: (0, 0)),
            pl.BlockSpec((D, D), lambda s, *_: (0, 0)),
        ],
        scratch_shapes=[
            pltpu.VMEM((D, D), BF16),
            pltpu.VMEM((T, D), BF16),
            pltpu.VMEM((D, D), F32),
            pltpu.SemaphoreType.DMA((lines,)),
        ],
    )


def weight_kernel(n_grads, n_out, owned, pos_ref, normed_ref, *rest):
    grads = rest[:n_grads]
    extra = rest[n_grads : len(rest) - n_out - 2]
    outs = rest[len(rest) - n_out - 2 : len(rest) - 2]
    gw_s, out_sems = rest[len(rest) - 2 :]
    piece_rows = outs[0].shape[1]
    width = sum(ref.shape[1] for ref in grads) // 3
    at = 3 * width
    if owned:
        grels, (small2_ref, small1_ref, qv_ref, *gbs) = extra[:2], extra[2:]
        sides = dot(qv_ref[:2].astype(BF16), owner_order(owned), NT)
        half = D // 2
        a = jnp.concatenate([sides[:1, :half], sides[1:, :half]], axis=1)
        b = jnp.concatenate([sides[:1, half:], sides[1:, half:]], axis=1)
        vecs = [small1_ref[:2], a, b, small2_ref[:4]]
        vecs += [ref[:, D * i : D * (i + 1)] for ref in gbs for i in range(ref.shape[1] // D)]
        vecs = jnp.concatenate(vecs + [jnp.zeros((128 - 12, D), F32)], axis=0).T
        gw_s[:, at + LABELS :] = vecs.astype(BF16)
        row = 0
        for ref in grels:
            gw_s[row : row + ref.shape[0], at : at + LABELS] = ref[...].astype(BF16)
            row += ref.shape[0]
    else:
        for ref in extra:
            gw_s[:, at : at + ref.shape[1]] = ref[...].astype(BF16)
            at += ref.shape[1]
    first_pair = 0
    for grad_ref in grads:
        cols = grad_ref.shape[1]
        for c in tiles(cols):
            out = dot(normed_ref[...], grad_ref[:, c], TN).astype(BF16)
            for at in range(c.start, c.stop, 128):
                pair, part = at // WAYS, at % WAYS // 128
                to = width * part + 128 * (first_pair + pair)
                gw_s[:, to : to + 128] = out[:, at - c.start : at - c.start + 128]
        first_pair += cols // WAYS
    copies = store_rows(gw_s, outs, piece_rows, pos_ref, out_sems, 0)
    for copy in copies:
        copy.start()
    for copy in copies:
        copy.wait()


def weight_grad(deps, pos, normed, grads, extra, out_groups, owned=0):
    rows = normed.shape[0]
    lines = pos.shape[0]
    cols = sum(g.shape[1] for g in grads)
    cols += LABELS + 128 if owned else sum(r.shape[1] for r in extra)
    return run(
        functools.partial(weight_kernel, len(grads), len(out_groups), owned),
        deps,
        [pos],
        [normed, *grads, *extra],
        [jax.ShapeDtypeStruct((k, D // lines, cols), BF16) for k in out_groups],
        "weight_grad",
        cols / 200,
        grid=(1,),
        in_specs=[VMEM] * (1 + len(grads) + len(extra)),
        out_specs=[ANY] * len(out_groups),
        scratch_shapes=[pltpu.VMEM((D, cols), BF16), pltpu.SemaphoreType.DMA((lines,))],
    )


def input_kernel(lines, n_grads, n_in, pos_ref, long_in_ref, glob_in_ref, gres_ref, vec_ref, *rest):
    grads = rest[:n_grads]
    pieces = rest[n_grads : n_grads + 2 * n_in]
    long_ref, glob_ref, small_ref, qv_ref, w_s, gn1_s, sems = rest[n_grads + 2 * n_in :]
    copies = []
    to = 0
    for i, width in enumerate((FIRST, SECOND)):
        for pair in range(width // 128):
            for part in range(3):
                copies += load_rows(
                    pieces[n_in * i : n_in * (i + 1)],
                    pos_ref,
                    lines,
                    w_s.at[:, to : to + 128],
                    sems.at[to // 128],
                    width * part + 128 * pair,
                )
                to += 128
    at = 0
    for ref in grads:
        for pair in range(ref.shape[1] // WAYS):
            for row, part in ((0, 0), (1, 2)):
                col = WAYS * pair + 128 * part
                qv_ref[row : row + 1, at : at + 128] = jnp.sum(
                    ref[:, col : col + 128].astype(F32), axis=0, keepdims=True
                )
            at += 128
    for copy in copies:
        copy.wait()
    for c in tiles(D):
        total = 0.0
        at = 0
        for ref in grads:
            total = total + dot(ref[...], w_s[c, at : at + ref.shape[1]], NT)
            at += ref.shape[1]
        gn1_s[:, c] = total
    for s in range(long_in_ref.shape[0]):
        for src, dst, at, size in (
            (glob_in_ref, glob_ref, T * s, GLOB),
            (long_in_ref, long_ref, T * s + GLOB, SEQ),
        ):
            rows = slice(at, at + size)
            xhat, rstd = norm_stats(src[s, 0].astype(F32))
            gn1 = gn1_s[rows]
            dst[s, 0] = (gres_ref[rows] + norm_back(gn1, xhat, rstd, vec_ref[GAIN1 : GAIN1 + 1])).astype(BF16)
            sums = [jnp.sum(gn1 * xhat, axis=0, keepdims=True), jnp.sum(gn1, axis=0, keepdims=True)]
            for row in range(2):
                if s == 0 and src is glob_in_ref:
                    small_ref[row : row + 1] = sums[row]
                else:
                    small_ref[row : row + 1] += sums[row]


def input_grad(deps, pos, long_in, glob_in, gres, vec, grads, pieces):
    rows = gres.shape[0]
    lines = pos.shape[0]
    n = len(grads)
    return run(
        functools.partial(input_kernel, lines, n, len(pieces[0])),
        deps,
        [pos],
        [long_in, glob_in, gres, vec, *grads, *[p for group in pieces for p in group]],
        [
            jax.ShapeDtypeStruct(long_in.shape, BF16),
            jax.ShapeDtypeStruct(glob_in.shape, BF16),
            jax.ShapeDtypeStruct((8, D), F32),
            jax.ShapeDtypeStruct((8, D), F32),
        ],
        "input_grad",
        15,
        grid=(1,),
        in_specs=[VMEM] * (4 + n) + [ANY] * sum(len(p) for p in pieces),
        out_specs=[VMEM] * 4,
        scratch_shapes=[
            pltpu.VMEM((D, 3 * D), BF16),
            pltpu.VMEM((rows, D), F32),
            pltpu.SemaphoreType.DMA((3 * D // 128, lines)),
        ],
    )


def pack_kernel(w_qkv_ref, rel_ref, *rest):
    vec_refs, out_ref = rest[:-1], rest[-1]
    width = FIRST
    for n in range(3):
        out_ref[:, width * n : width * (n + 1)] = w_qkv_ref[:, D * n : D * n + width]
    rows = rel_ref.shape[0]
    vecs = []
    for ref in vec_refs:
        v = ref[...].astype(F32)
        vecs += [v[at : at + rows].reshape(1, rows) for at in range(0, v.shape[0], rows)]
    vecs = jnp.concatenate(vecs + [jnp.zeros((128 - len(vecs), rows), F32)], axis=0).T
    rel = jnp.concatenate(
        [
            jnp.zeros((rows, LEAD), F32),
            rel_ref[...].astype(F32),
            jnp.zeros((rows, VEC_AT - LEAD - RELS), F32),
            vecs[:, : LABELS - VEC_AT],
        ],
        axis=1,
    )
    out_ref[:, 3 * width :] = rel.astype(BF16)


def pack(w_qkv, rel_embed, vecs):
    rows = w_qkv.shape[0]
    return run(
        pack_kernel,
        [],
        [],
        [w_qkv, rel_embed, *vecs],
        [jax.ShapeDtypeStruct((rows, 3 * FIRST + LABELS), BF16)],
        "pack",
        1.5,
        grid=(1,),
        in_specs=[VMEM] * (2 + len(vecs)),
        out_specs=[VMEM],
        scratch_shapes=[],
    )[0]


def pack_next_kernel(w_qkv_ref, w_out_ref, out_ref):
    width = SECOND
    for n in range(3):
        out_ref[:, width * n : width * (n + 1)] = w_qkv_ref[:, D * (n + 1) - width : D * (n + 1)]
    out_ref[:, 3 * width :] = w_out_ref[...]


def pack_next(deps, w_qkv, w_out):
    rows = w_qkv.shape[0]
    return run(
        pack_next_kernel,
        deps,
        [],
        [w_qkv, w_out],
        [jax.ShapeDtypeStruct((rows, 3 * SECOND + D), BF16)],
        "pack",
        1.5,
        grid=(1,),
        in_specs=[VMEM] * 2,
        out_specs=[VMEM],
        scratch_shapes=[],
    )[0]


def pack_ffn_kernel(chunks, w_in_ref, w_down_ref, out_ref):
    rows = w_in_ref.shape[0]
    parts = FF // D
    per = parts // chunks
    down = w_down_ref[...].astype(F32)
    for c in range(chunks):
        at = 2 * per * D * c
        out_ref[:, at : at + per * D] = w_in_ref[:, per * D * c : per * D * (c + 1)]
        for i in range(per):
            q = per * c + i
            to = at + (per + i) * D
            out_ref[:, to : to + D] = down[rows * q : rows * (q + 1)].astype(BF16)


def pack_ffn(deps, w_in, w_down, chunks):
    rows = w_in.shape[0]
    return run(
        functools.partial(pack_ffn_kernel, chunks),
        deps,
        [],
        [w_in, w_down],
        [jax.ShapeDtypeStruct((rows, 2 * FF), BF16)],
        "pack",
        1.5,
        grid=(1,),
        in_specs=[VMEM] * 2,
        out_specs=[VMEM],
        scratch_shapes=[],
    )[0]


def unpack_kernel(n, *refs):
    g_qkv_ref, g_out_ref, g_rel_ref, *vec_refs = refs[2 * n :]
    for g, width in enumerate((FIRST, SECOND)):
        total = refs[n * g][...].astype(F32)
        for ref in refs[n * g + 1 : n * (g + 1)]:
            total = total + ref[...].astype(F32)
        for part in range(3):
            at = D * part + FIRST * g
            g_qkv_ref[:, at : at + width] = total[:, width * part : width * (part + 1)]
        if g == 1:
            g_out_ref[...] = total[:, 3 * width :]
        else:
            g_rel_ref[...] = total[:, 3 * width + BACK_LEAD : 3 * width + BACK_LEAD + RELS]
            rows = total.shape[0]
            vecs = total[:, 3 * width + LABELS :]
            vecs = jnp.concatenate([vecs, jnp.zeros((128 - rows, 128), F32)], axis=0).T
            row = 0
            for ref in vec_refs:
                for at in range(0, ref.shape[0], rows):
                    ref[pl.ds(at, rows)] = vecs[row : row + 1, :rows].reshape(rows)
                    row += 1


def unpack(first, second, sizes):
    rows = first[0].shape[0]
    shape = lambda cols: jax.ShapeDtypeStruct((rows, cols), F32)
    return run(
        functools.partial(unpack_kernel, len(first)),
        [],
        [],
        [*first, *second],
        [shape(3 * D), shape(D), shape(RELS)] + [jax.ShapeDtypeStruct((n,), F32) for n in sizes],
        "unpack",
        2,
        grid=(1,),
        in_specs=[VMEM] * (2 * len(first)),
        out_specs=[VMEM] * (3 + len(sizes)),
        scratch_shapes=[],
    )


def order_kernel(count, z_ref, *refs):
    parts, outs, total_s = refs[: -1 - count], refs[-1 - count : -1], refs[-1]
    for mask, part in enumerate(parts):
        total_s[z_ref[0] ^ mask] = part[...].astype(F32)
    cols = outs[0].shape[1]
    for i, out in enumerate(outs):
        out[...] = total_s[:, :, cols * i : cols * (i + 1)].reshape(out.shape).astype(out.dtype)


def order(deps, z, parts, count):
    rows, cols = parts[0].shape
    lines = len(parts)
    return run(
        functools.partial(order_kernel, count),
        deps,
        [z],
        parts,
        [jax.ShapeDtypeStruct((lines * rows, cols // count), parts[0].dtype)] * count,
        "order",
        1.5,
        grid=(1,),
        in_specs=[VMEM] * lines,
        out_specs=[VMEM] * count,
        scratch_shapes=[pltpu.VMEM((lines, rows, cols), F32)],
    )


def unpack_ffn_kernel(chunks, *refs):
    terms, (g_in_ref, g_down_ref) = refs[:-2], refs[-2:]
    rows = g_in_ref.shape[0]
    parts = FF // D
    per = parts // chunks
    for q in range(parts):
        at = 2 * per * D * (q // per) + D * (q % per)
        for out, first in ((g_in_ref, at), (g_down_ref, at + per * D)):
            total = terms[0][:, first : first + D].astype(F32)
            for ref in terms[1:]:
                total = total + ref[:, first : first + D].astype(F32)
            if out is g_in_ref:
                out[:, D * q : D * (q + 1)] = total
            else:
                out[rows * q : rows * (q + 1), :] = total


def unpack_ffn(deps, terms, chunks):
    rows = terms[0].shape[0]
    return run(
        functools.partial(unpack_ffn_kernel, chunks),
        deps,
        [],
        terms,
        [jax.ShapeDtypeStruct((rows, FF), F32), jax.ShapeDtypeStruct((rows * (FF // D), D), F32)],
        "unpack",
        2,
        grid=(1,),
        in_specs=[VMEM] * len(terms),
        out_specs=[VMEM] * 2,
        scratch_shapes=[],
    )


def split_kernel(lines, counts, z_ref, *refs):
    outs = refs[sum(counts) : sum(counts) + lines]
    total_s = refs[-1]
    first = 0
    at = 0
    for n in counts:
        terms = refs[first : first + n]
        rows, cols = terms[0].shape[-2:]
        total = terms[0][...].reshape(rows, cols).astype(F32)
        for ref in terms[1:]:
            total = total + ref[...].reshape(rows, cols).astype(F32)
        total_s[:, :, at : at + cols] = total.reshape(lines, rows // lines, cols)
        first += n
        at += cols
    for mask, out in enumerate(outs):
        out[...] = total_s[z_ref[0] ^ mask].astype(out.dtype)


def split(deps, z, sums, lines):
    kind = sums[0][0].dtype
    specs = []
    for t in [t for terms in sums for t in terms]:
        if t.ndim == 3:
            specs.append(pl.BlockSpec((1,) + t.shape[1:], lambda i, *_: (0, 0, 0)))
        else:
            specs.append(pl.BlockSpec(t.shape, lambda i, *_: (0, 0)))
    rows = sums[0][0].shape[-2] // lines
    cols = sum(terms[0].shape[-1] for terms in sums)
    return run(
        functools.partial(split_kernel, lines, [len(terms) for terms in sums]),
        deps,
        [z],
        [t for terms in sums for t in terms],
        [jax.ShapeDtypeStruct((rows, cols), F32 if m == 0 else kind) for m in range(lines)],
        "split",
        2,
        grid=(1,),
        in_specs=specs,
        out_specs=[VMEM] * lines,
        scratch_shapes=[pltpu.VMEM((lines, rows, cols), F32)],
    )


def sum_kernel(*refs):
    total = refs[0][...].astype(F32)
    for ref in refs[1:-1]:
        total = total + ref[...].astype(F32)
    refs[-1][...] = total.reshape(refs[-1].shape).astype(refs[-1].dtype)


def second(deps, terms):
    _, rows, cols = terms[0].shape
    return run(
        sum_kernel,
        deps,
        [],
        terms,
        [jax.ShapeDtypeStruct((rows, cols), terms[0].dtype)],
        "second",
        2,
        grid=(1,),
        in_specs=[pl.BlockSpec((1, rows, cols), lambda i: (1, 0, 0))] * len(terms),
        out_specs=[VMEM],
        scratch_shapes=[],
    )[0]


def both(deps, terms):
    lines, rows, cols = terms[0].shape
    spec = pl.BlockSpec((1, rows, cols), lambda i: (i, 0, 0))
    return run(
        sum_kernel,
        deps,
        [],
        terms,
        [jax.ShapeDtypeStruct(terms[0].shape, terms[0].dtype)],
        "both",
        2,
        grid=(lines,),
        in_specs=[spec] * len(terms),
        out_specs=[spec],
        scratch_shapes=[],
    )[0]


AXES = ("wide", "narrow")


class Links:
    def __init__(self, mesh):
        self.wide = mesh.shape["wide"]
        self.narrow = mesh.shape["narrow"]
        self.count = self.wide * self.narrow
        self.pairwise = self.wide == 8 and self.narrow == 4
        self.lines = self.wide if self.pairwise else 1
        self.groups = (2, 2, 2, 2) if self.pairwise else (1,)

    def setup(self):
        if not self.pairwise:
            self.pos = jnp.zeros((1,), jnp.int32)
            return
        w = lax.axis_index("wide")
        self.z = lax.axis_index("narrow")
        near = jnp.where(w % 2 == 0, 2, 4)
        far = 6 - near
        order = [0, near, far, 6, 1, 1 ^ far, 1 ^ near, 7]
        self.pos = jnp.stack([w ^ m for m in order]).astype(jnp.int32)

    def slot(self, *marks):
        self.marks = list(marks)

    def swap(self, x, wide_mask=0, narrow_mask=0):
        masks = wide_mask if isinstance(wide_mask, tuple) else (wide_mask, wide_mask)
        pairs = []
        for w in range(self.wide):
            for z in range(self.narrow):
                pairs.append(
                    (w * self.narrow + z, (w ^ masks[w % 2]) * self.narrow + (z ^ narrow_mask))
                )
        return lax.ppermute(x, AXES, pairs)

    def line(self, x):
        if not self.pairwise:
            return [lax.all_gather(x, AXES, axis=0, tiled=True)]
        return [x] + [self.swap(x, 0, mask) for mask in (1, 2, 3)]

    def own(self, parts):
        if not self.pairwise:
            return parts
        (x,) = order(self.marks, self.z.reshape(1), parts, 1)
        return self.around(x)

    def around(self, x):
        return [x, self.swap(x, (2, 4)), self.swap(x, (4, 2)), self.swap(x, 1)]

    def onward(self, lines):
        if not self.pairwise:
            return lines
        own, near, far, own_core = lines
        if self.marks:
            near = after(near, self.marks)
            far = after(far, self.marks)
        return [own, near, far, self.swap(near, (4, 2)), own_core, self.swap(near, 1), self.swap(far, 1)]

    def core(self, lines):
        if not self.pairwise:
            return lines
        own, near, far, both, *core = lines
        if self.marks:
            both = after(both, self.marks)
        return [own, near, far, both, *core, self.swap(both, 1)]

    def add(self, *parts):
        total = parts[0].astype(F32)
        for p in parts[1:]:
            total = total + p.astype(F32)
        return total


class Sum:
    def __init__(self, links, parts):
        self.links = links
        self.parts = parts
        self.kind = parts[0].dtype

    def core(self, marks=()):
        links = self.links
        if not links.pairwise:
            self.src = self.out = lax.psum_scatter(self.parts[0][0].astype(F32), AXES, scatter_dimension=0, tiled=True)
            return (self.out,)
        send_a, send_b = self.parts[2], self.parts[3]
        if marks:
            send_a, send_b = after(send_a, marks), after(send_b, marks)
        self.got_b = links.swap(send_b, 1)
        self.got_a = links.swap(send_a, 1)
        return (self.got_b, self.got_a)

    def far(self):
        links = self.links
        if not links.pairwise:
            return (self.out,)
        self.src = both(links.marks, [self.parts[1], self.got_b])
        self.from_far = links.swap(self.src, (4, 2))
        return (self.from_far,)

    def near(self):
        links = self.links
        if not links.pairwise:
            return (self.out,)
        self.src = second(links.marks, [self.parts[0], self.got_a, self.from_far])
        self.from_near = links.swap(self.src, (2, 4))
        return (self.from_near,)

    def line(self, *more):
        links = self.links
        sums = (self,) + more
        if not links.pairwise:
            self.terms = [jnp.concatenate([x.out for x in sums], axis=1)]
            return self.terms
        terms = [[x.parts[0], x.got_a, x.from_far, x.from_near] for x in sums]
        mine, *others = split(links.marks, links.z.reshape(1), terms, links.narrow)
        self.src = mine
        self.terms = [mine] + [links.swap(x, 0, mask) for mask, x in enumerate(others, 1)]
        return self.terms[1:]

    def total(self):
        return self.links.add(*self.terms)


CHUNKS = 2
PARTS = FF // D
PAIRS = 6


def body(links, long_in, glob_in, lengths, ln1_gain, ln1_bias, w_qkv, qv_bias, rel_embed, w_out, out_bias, ln2_gain, ln2_bias, w_in, in_bias, w_down, down_bias, cot_long, cot_glob):
    links.setup()
    pos = links.pos
    groups = links.groups
    count = links.count
    micro = long_in.shape[0]
    r = w_qkv.shape[0]
    lens = lengths.reshape(micro)
    per = PARTS // CHUNKS
    first, second = 3 * FIRST, 3 * SECOND
    n_first, n_second = FIRST // 128, SECOND // 128

    vectors = [ln1_gain, ln1_bias, qv_bias, out_bias, ln2_gain, ln2_bias, down_bias, in_bias]
    w_in_parts = w_in.reshape(r, count, PARTS, r).transpose(0, 2, 1, 3).reshape(r, FF)

    links.slot()
    own_a0 = links.own(links.line(pack(w_qkv, rel_embed, vectors)))
    line_a1 = links.line(pack_next([own_a0[0]], w_qkv, w_out))
    ffn_shard = pack_ffn([], w_in_parts, w_down, CHUNKS)
    links.slot(own_a0[len(own_a0) // 2])
    most_a0 = links.onward(own_a0)
    links.slot(*line_a1[1:], ffn_shard)
    attn = [links.core(most_a0)]
    line_f = links.line(after(ffn_shard, [attn[0][-1]]))

    proj0, normed, rel_all, rel_turned, vec = project_first([], pos, long_in, glob_in, attn[0], r, first)
    links.slot(attn[0][-1])
    own_a1 = links.own(line_a1)
    mixed0, inv0, p0, pg0 = attend([own_a1[-1], own_a1[0]], lens, proj0, rel_all, 0)
    links.slot(proj0)
    most_a1 = links.onward(own_a1)
    links.slot(mixed0)
    if links.pairwise:
        line_f = order(links.marks, links.z.reshape(1), line_f, CHUNKS)
        own_f = [links.around(line_f[0])]
    else:
        own_f = [[line_f[0][:, 2 * per * D * c : 2 * per * D * (c + 1)]] for c in range(CHUNKS)]
    links.slot(mixed0)
    attn.append(links.core(most_a1))
    proj1 = project_next([mixed0, own_f[0][0]], pos, normed, vec, attn[1], second)
    mixed1, inv1, p1, pg1 = attend([], lens, proj1, rel_all, n_first)
    mixed = [mixed0, mixed1]
    if links.pairwise:
        own_f.append(links.around(after(line_f[1], [proj1])))
    links.slot(mixed1)
    most_f0 = links.onward(own_f[0])
    most_f1 = links.onward(own_f[1])
    res, n2, g_ffn = mix_out(
        [most_f0[0]], pos, lens, long_in, glob_in, cot_long, cot_glob, vec, mixed, attn[1], second
    )
    links.slot(n2)
    ffn0 = links.core(most_f0)
    y0, gn0, gb0, *gw0 = ffn([], pos, n2, g_ffn, vec, ffn0, 0, per, groups)
    links.slot(y0)
    ffn1 = links.core(most_f1)
    sum0 = Sum(links, gw0)
    y1, gn1, gb1, *gw1 = ffn([y0], pos, n2, g_ffn, vec, ffn1, per, per, groups)
    core0 = sum0.core()
    sum1 = Sum(links, gw1)
    links.slot(y1)
    far0 = sum0.far()
    block_long, block_glob, gres, gmix, small2, gw_out = mid(
        [sum0.src], pos, lens, res, g_ffn, vec, [y0, y1], [gn0, gn1], mixed, attn[1], second, long_in.shape, glob_in.shape
    )
    core1 = sum1.core()
    links.slot(gmix)
    near0 = sum0.near()
    sum1.far()
    gproj1, grel1 = attend_back([sum0.src, sum1.src], proj1, rel_turned, gmix, mixed1, inv1, p1, pg1, n_first, 0, n_second)
    links.slot(gproj1)
    sum1.near()
    gw_a1 = weight_grad([sum1.src, *near0], pos, normed, [gproj1], [gw_out], groups)
    sum2 = Sum(links, gw_a1)
    sum2.core()
    links.slot(gw_a1[0])
    line01 = sum0.line(sum1)
    gproj0, grel0 = attend_back([sum0.src], proj0, rel_turned, gmix, mixed0, inv0, p0, pg0, 0, 0, n_first)
    links.slot(gproj0)
    sum2.far()
    grad_long, grad_glob, small1, small_qv = input_grad(
        [sum2.src], pos, long_in, glob_in, gres, vec, [gproj0, gproj1], attn
    )
    links.slot(small1)
    near2 = sum2.near()
    gw_a0 = weight_grad(
        [sum2.src, *line01], pos, normed, [gproj0], [grel0, grel1, small2, small1, small_qv, gb0, gb1], groups, r
    )
    sum3 = Sum(links, gw_a0)
    sum3.core(near2)
    links.slot(gw_a0[0])
    sum3.far()
    links.slot(sum3.src)
    sum2.line()
    g_in, g_down = unpack_ffn([sum3.src], sum0.terms, CHUNKS)
    links.slot(sum2.src, g_in)
    sum3.near()
    g_in = g_in.reshape(r, PARTS, count, r).transpose(0, 2, 1, 3).reshape(r, FF)
    links.slot()
    sum3.line()
    order_out = [ln1_gain, ln1_bias, qv_bias, ln2_gain, ln2_bias, out_bias, down_bias, in_bias]
    g_qkv, g_out, g_rel, g_gain1, g_bias1, g_qv, g_gain2, g_bias2, g_out_b, g_down_b, g_in_b = unpack(
        sum3.terms, sum2.terms, [v.shape[0] for v in order_out]
    )
    return (
        block_long, block_glob, grad_long, grad_glob,
        g_gain1, g_bias1, g_qkv, g_qv, g_rel, g_out, g_out_b,
        g_gain2, g_bias2, g_in, g_in_b, g_down, g_down_b,
    )


def solution(mesh):
    rows = P(None, AXES, None, None)
    vec = P(AXES)
    mat = P(AXES, None)
    placed = (rows, rows, P(None, AXES), vec, vec, mat, vec, mat, mat, vec, vec, vec, mat, vec, mat, vec, rows, rows)
    return jax.shard_map(
        functools.partial(body, Links(mesh)),
        mesh=mesh,
        in_specs=placed,
        out_specs=(rows, rows, rows, rows, vec, vec, mat, vec, mat, mat, vec, vec, vec, mat, vec, mat, vec),
        check_vma=False,
    )
```

```python
import functools
import jax
import jax.numpy as jnp
from jax import lax
from jax.experimental import pallas as pl
from jax.experimental.pallas import tpu as pltpu
from jax.sharding import PartitionSpec as P

HEAD_DIM = 64
RADIUS = 84
STRIDE = 16
SEQ = 512
GLOB = 32
RELS = 169
T = GLOB + SEQ
D = 768
FF = 3072
PAIRS = 6
LABELS = 256
LEAD = 4
BACK_LEAD = 3
LABEL_END = LEAD + RELS
EPS = 1e-06
NEG = -1e30
F32 = jnp.float32
BF16 = jnp.bfloat16
VMEM_LIMIT = (64 << 20) - (256 << 10)
WINDOWS = ((0, 0, 256, 328, 0), (0, 0, 384, 72, 0), (1, 160, 384, 8, 352), (1, 288, 256, 8, 224))
OFFSETS = (0, 256, 640, 1024)
WAYS = 3 * 128
VEC_AT = 176
GAIN1, BIAS1, QV, OUT_B, GAIN2, BIAS2, DOWN_B, IN_B, VECS = 0, 1, 2, 4, 5, 6, 7, 8, 16
P_COLS = 1280
NN = (((1,), (0,)), ((), ()))
NT = (((1,), (1,)), ((), ()))
TN = (((0,), (0,)), ((), ()))


def dot(a, b, dims=NN):
    return lax.dot_general(a, b, dims, preferred_element_type=F32)


def run(kernel, deps, prefetch, inputs, out_shape, name, cost, grid, in_specs, out_specs, scratch_shapes):
    n = len(prefetch)

    def with_deps(*refs):
        kernel(*refs[:n], *refs[n + len(deps) :])

    anywhere = pl.BlockSpec(memory_space=pl.ANY)
    return pl.pallas_call(
        with_deps,
        grid_spec=pltpu.PrefetchScalarGridSpec(
            num_scalar_prefetch=n,
            grid=grid,
            in_specs=[anywhere] * len(deps) + in_specs,
            out_specs=out_specs,
            scratch_shapes=scratch_shapes,
        ),
        out_shape=out_shape,
        compiler_params=pltpu.CompilerParams(vmem_limit_bytes=VMEM_LIMIT),
        cost_estimate=pl.CostEstimate(flops=int(cost * 1.15e9), bytes_accessed=1 << 20, transcendentals=0),
        name=name,
    )(*prefetch, *deps, *inputs)


def after(x, deps):
    anywhere = pl.BlockSpec(memory_space=pl.ANY)
    return pl.pallas_call(
        lambda *refs: None,
        in_specs=[anywhere] * (1 + len(deps)),
        out_specs=anywhere,
        out_shape=jax.ShapeDtypeStruct(x.shape, x.dtype),
        input_output_aliases={0: 0},
        name="after",
    )(x, *deps)


def iota(shape, dim):
    return lax.broadcasted_iota(jnp.int32, shape, dim)


def norm_stats(x):
    cen = x - jnp.mean(x, axis=1, keepdims=True)
    rstd = lax.rsqrt(jnp.mean(cen * cen, axis=1, keepdims=True) + EPS)
    return cen * rstd, rstd


def norm_back(grad, xhat, rstd, gain):
    gg = grad * gain
    return rstd * (
        gg - jnp.mean(gg, axis=1, keepdims=True) - xhat * jnp.mean(gg * xhat, axis=1, keepdims=True)
    )


def tiles(cols, size=256):
    return [slice(at, min(at + size, cols)) for at in range(0, cols, size)]


def live_mask(length, cols):
    row = iota((T, cols), 0)
    glob_count = (length + STRIDE - 1) // STRIDE
    return row < jnp.where(row < GLOB, glob_count, length + GLOB)


def load_rows(pieces, pos_ref, lines, dst, sems, first_col, start=True):
    rows = dst.shape[0] // lines
    cols = dst.shape[1]
    copies = []
    k = 0
    for piece in pieces:
        for i in range(piece.shape[0] // rows):
            to = pl.multiple_of(pos_ref[k] * rows, 16)
            copies.append(
                pltpu.make_async_copy(
                    piece.at[pl.ds(i * rows, rows), pl.ds(first_col, cols)],
                    dst.at[pl.ds(to, rows), :],
                    sems.at[k],
                )
            )
            k += 1
    if start:
        for copy in copies:
            copy.start()
    return copies


FIRST = 2 * 128
SECOND = D - FIRST


def owner_order(rows):
    k = iota((D, 1), 0)
    late = (k >= D // 2).astype(jnp.int32)
    k = k - late * (D // 2)
    owner = ((k.astype(F32) + 0.5) * (1.0 / rows)).astype(jnp.int32)
    col = rows * owner + k + late * rows
    return (iota((D, D), 1) == col).astype(F32).astype(BF16)


def project_kernel(lines, n_pieces, first, rows, pos_ref, *rest):
    if first:
        long_ref, glob_ref = rest[:2]
    else:
        normed_ref, vec_ref = rest[:2]
    pieces = rest[2 : 2 + n_pieces]
    if first:
        proj_ref, normed_ref, rel_ref, relt_ref, vec_ref, w_s, sems = rest[2 + n_pieces :]
    else:
        proj_ref, w_s, sems = rest[2 + n_pieces :]
    cols = proj_ref.shape[1]
    width = cols // 3
    copies = load_rows(pieces, pos_ref, lines, w_s, sems.at[0], 0)
    if first:
        for copy in load_rows(pieces, pos_ref, lines, rel_ref, sems.at[1], cols):
            copy.wait()
        turned = rel_ref[...].astype(F32).T
        vec_ref[...] = turned[VEC_AT : VEC_AT + VECS]
        drop = LEAD - BACK_LEAD
        labels = jnp.concatenate([turned[drop:], turned[:drop]], axis=0)
        label = iota((LABELS, D), 0) - BACK_LEAD
        relt_ref[...] = jnp.where((label >= 0) & (label < RELS), labels, 0.0).astype(BF16)
        a, b = vec_ref[QV : QV + 1], vec_ref[QV + 1 : QV + 2]
        half = D // 2
        sides = jnp.concatenate(
            [
                jnp.concatenate([a[:, :half], b[:, :half]], axis=1),
                jnp.concatenate([a[:, half:], b[:, half:]], axis=1),
            ],
            axis=0,
        )
        vec_ref[QV : QV + 2] = dot(sides.astype(BF16), owner_order(rows))
        for s in range(long_ref.shape[0]):
            for part, at, size in ((glob_ref, T * s, GLOB), (long_ref, T * s + GLOB, SEQ)):
                xhat, _ = norm_stats(part[s, 0].astype(F32))
                normed_ref[at : at + size] = (
                    xhat * vec_ref[GAIN1 : GAIN1 + 1] + vec_ref[BIAS1 : BIAS1 + 1]
                ).astype(BF16)
    own = slice(0, width) if first else slice(D - width, D)
    full_bias = jnp.concatenate(
        [vec_ref[QV : QV + 1, own], jnp.zeros((1, width), F32), vec_ref[QV + 1 : QV + 2, own]], axis=1
    )
    for copy in copies:
        copy.wait()
    for c in tiles(cols):
        out = (dot(normed_ref[...], w_s[:, c]) + full_bias[:, c]).astype(BF16)
        for at in range(c.start, c.stop, 128):
            to = by_pair(at, width)
            proj_ref[:, to : to + 128] = out[:, at - c.start : at - c.start + 128]


def by_pair(col, width):
    return WAYS * (col % width // 128) + 128 * (col // width)


VMEM = pl.BlockSpec(memory_space=pltpu.VMEM)
ANY = pl.BlockSpec(memory_space=pl.ANY)


def project_first(deps, pos, long_in, glob_in, pieces, owned, cols):
    rows = long_in.shape[0] * T
    lines = pos.shape[0]
    shape = lambda *dims: jax.ShapeDtypeStruct(dims, BF16)
    return run(
        functools.partial(project_kernel, lines, len(pieces), True, owned),
        deps,
        [pos],
        [long_in, glob_in, *pieces],
        [
            shape(rows, cols),
            shape(rows, D),
            shape(D, LABELS),
            shape(LABELS, D),
            jax.ShapeDtypeStruct((VECS, D), F32),
        ],
        "project",
        9,
        grid=(1,),
        in_specs=[VMEM] * 2 + [ANY] * len(pieces),
        out_specs=[VMEM] * 5,
        scratch_shapes=[pltpu.VMEM((D, cols), BF16), pltpu.SemaphoreType.DMA((2, lines))],
    )


def project_next(deps, pos, normed, vec, pieces, cols):
    rows = normed.shape[0]
    lines = pos.shape[0]
    return run(
        functools.partial(project_kernel, lines, len(pieces), False, 0),
        deps,
        [pos],
        [normed, vec, *pieces],
        [jax.ShapeDtypeStruct((rows, cols), BF16)],
        "project",
        8,
        grid=(1,),
        in_specs=[VMEM] * 2 + [ANY] * len(pieces),
        out_specs=[VMEM],
        scratch_shapes=[pltpu.VMEM((D, cols), BF16), pltpu.SemaphoreType.DMA((2, lines))],
    )[0]


def flip_matrix(size):
    row, col = iota((size, size), 0), iota((size, size), 1)
    return ((row // 128 == col // 128) & (row % 128 + col % 128 == 127)).astype(F32).astype(BF16)


def by_head(x):
    even = iota(x.shape, 1) < HEAD_DIM
    return jnp.concatenate([jnp.where(even, x, 0.0), jnp.where(even, 0.0, x)], axis=0)


def by_lane(x):
    half = x.shape[0] // 2
    even = iota((half, x.shape[1]), 1) < HEAD_DIM
    return jnp.where(even, x[:half], x[half:])


def spread(x, b):
    _, _, width, shift, _ = WINDOWS[b]
    shift = shift if shift < 256 else shift - 384
    lane = iota((64, 128), 1)
    none = jnp.full((64, 128), NEG, F32)
    parts = []
    for at in range(0, 256, 64):
        start = shift + at % 128
        turned = pltpu.roll(x[at : at + 64], start % 256, 1, stride=1, stride_axis=0)
        low, high = turned[:, :128], turned[:, 128:]
        if start < 0:
            cols = [low, jnp.where(lane < 64, high, NEG), none]
        elif start + 64 + LABEL_END <= 256:
            cols = [low, high, none]
        elif start >= 128:
            cols = [none, high, low]
        else:
            cols = [jnp.where(lane >= 64, low, NEG), high, jnp.where(lane < 64, low, NEG)]
        parts.append(jnp.concatenate(cols[: width // 128], axis=1))
    return jnp.concatenate(parts, axis=0)


def collect(cols, b):
    _, _, width, shift, _ = WINDOWS[b]
    shift = shift if shift < 256 else shift - 384
    lane = iota((64, 128), 1)
    parts = []
    for at in range(0, 256, 64):
        start = shift + 64 - at % 128
        tiles_ = [c[at : at + 64] for c in cols]
        if start < 0:
            low, high = tiles_[0], jnp.where(lane < 64, tiles_[1], 0.0)
        elif start + 64 + LABEL_END <= 256:
            low, high = tiles_[0], tiles_[1]
        elif start >= 128:
            low, high = tiles_[2], tiles_[1]
        elif len(tiles_) > 2:
            low, high = jnp.where(lane >= 64, tiles_[0], tiles_[2]), tiles_[1]
        else:
            low, high = jnp.where(lane >= 64, tiles_[0], 0.0), tiles_[1]
        back = (BACK_LEAD - LEAD - 63 - start) % 256
        parts.append(
            pltpu.roll(jnp.concatenate([low, high], axis=1), back, 1, stride=1, stride_axis=0)
        )
    return jnp.concatenate(parts, axis=0)


def zero_glob(x, at):
    cols = [x[:, 128 * i : 128 * (i + 1)] for i in range(x.shape[1] // 128)]
    lane = iota(cols[0].shape, 1) - at % 128
    cols[at // 128] = jnp.where((lane >= 0) & (lane < GLOB), 0.0, cols[at // 128])
    return cols


def attend_kernel(len_ref, qkv_ref, rel_ref, mix_ref, inv_ref, p_ref, pg_ref, k_s, v_s, rel_s):
    dead = jnp.where(live_mask(len_ref[pl.program_id(0)], 128), 0.0, NEG)
    flag = iota((T, 128), 1) == 0
    k = jnp.concatenate(
        [qkv_ref[:, 128:256], jnp.where(flag, dead, 0.0).astype(BF16)], axis=1
    )
    v = jnp.concatenate([qkv_ref[:, 256:384], jnp.ones((T, 128), BF16)], axis=1)
    for s, m in ((k_s, k), (v_s, v)):
        s[0] = m
        s[1, :SEQ] = m[GLOB:]
        s[1, SEQ:] = m[:GLOB]
    label = iota((128, LABELS), 1)
    outside = ((label < LEAD) | (label >= LEAD + RELS)) & (iota((128, LABELS), 0) == 0)
    rel_s[:128] = rel_ref[...]
    rel_s[128:] = jnp.where(outside, NEG, 0.0).astype(BF16)
    flip = flip_matrix(256)

    def queries(rows):
        x = by_head(qkv_ref[rows, :128].astype(F32) * 0.125)
        one = (iota(x.shape, 1) == 0).astype(F32)
        return jnp.concatenate([x, one], axis=1).astype(BF16)

    def weights(scores):
        return jnp.exp(scores - jnp.max(scores, axis=1, keepdims=True)).astype(BF16)

    rows = [slice(0, GLOB)] + [slice(GLOB + 128 * b, GLOB + 128 * (b + 1)) for b in range(4)]
    wins = [(0, slice(0, T))] + [(arr, slice(first, first + width)) for arr, first, width, _, _ in WINDOWS]
    qs = [queries(r) for r in rows]
    scores = [dot(q, k_s[arr, win], NT) for q, (arr, win) in zip(qs, wins)]
    biases = [dot(q, rel_s[...]) for q in qs[1:]]
    for b, window in enumerate(WINDOWS):
        bias = zero_glob(spread(biases[b], b), window[-1])
        scores[b + 1] = scores[b + 1] + jnp.concatenate(bias, axis=1)
    ps = [weights(x) for x in scores]
    pg_ref[0, 0] = ps[0]
    outs = [dot(p, v_s[arr, win]) for p, (arr, win) in zip(ps, wins)]
    turned = [dot(flip, p) for p in ps[1:]]
    for r, out in zip(rows, outs):
        inv = by_lane(1.0 / out[:, 128:])
        inv_ref[r] = inv
        mix_ref[r] = (by_lane(out[:, :128]) * inv).astype(BF16)
    for b, p in enumerate(turned):
        p_ref[0, 0, :, OFFSETS[b] : OFFSETS[b] + p.shape[1]] = p.astype(BF16)


def attend(deps, lengths, proj, rel, first_pair):
    rows = proj.shape[0]
    seqs = rows // T
    pairs = proj.shape[1] // WAYS
    return run(
        attend_kernel,
        deps,
        [lengths],
        [proj, rel],
        [
            jax.ShapeDtypeStruct((rows, pairs * 128), BF16),
            jax.ShapeDtypeStruct((rows, pairs * 128), F32),
            jax.ShapeDtypeStruct((seqs, pairs, 256, P_COLS), BF16),
            jax.ShapeDtypeStruct((seqs, pairs, 2 * GLOB, T), BF16),
        ],
        "attend",
        6.2 * pairs,
        grid=(seqs, pairs),
        in_specs=[
            pl.BlockSpec((T, WAYS), lambda s, p, *_: (s, p)),
            pl.BlockSpec((128, LABELS), lambda s, p, *_: (first_pair + p, 0)),
        ],
        out_specs=[
            pl.BlockSpec((T, 128), lambda s, p, *_: (s, p)),
            pl.BlockSpec((T, 128), lambda s, p, *_: (s, p)),
            pl.BlockSpec((1, 1, 256, P_COLS), lambda s, p, *_: (s, p, 0, 0)),
            pl.BlockSpec((1, 1, 2 * GLOB, T), lambda s, p, *_: (s, p, 0, 0)),
        ],
        scratch_shapes=[
            pltpu.VMEM((2, T, 256), BF16),
            pltpu.VMEM((2, T, 256), BF16),
            pltpu.VMEM((256, LABELS), BF16),
        ],
    )


def attend_back_kernel(qkv_ref, relt_ref, do_ref, o_ref, inv_ref, p_ref, pg_ref, grad_ref, grel_ref, gk_s, gv_s, k_s, v_s):
    k = qkv_ref[:, 128:256]
    v = qkv_ref[:, 256:384]
    for s, m in ((k_s, k), (v_s, v)):
        s[0] = m
        s[1, :SEQ] = m[GLOB:]
        s[1, SEQ:] = m[:GLOB]
    flip = flip_matrix(128)

    @pl.when(pl.program_id(1) == 0)
    def _():
        grel_ref[...] = jnp.zeros_like(grel_ref)

    ones = jnp.ones((256, 128), BF16)

    def score_grads(do, o, p, v_win):
        prod = by_head(do * o)
        high = prod.astype(BF16)
        low = (prod - high.astype(F32)).astype(BF16)
        centre = dot(jnp.concatenate([high, low], axis=1), ones)
        dom = by_head(do).astype(BF16)
        dp = dot(dom, v_win, NT)
        width = dp.shape[1]
        cols = [dp[:, c] - centre[:, : c.stop - c.start] for c in tiles(width, 128)]
        return dom, p.astype(F32) * jnp.concatenate(cols, axis=1)

    do = (do_ref[:GLOB].astype(F32) * inv_ref[:GLOB]).astype(BF16).astype(F32)
    p = pg_ref[0, 0]
    dom, ds = score_grads(do, o_ref[:GLOB].astype(F32), p, v_s[0])
    ds = ds.astype(BF16)
    qm = by_head(qkv_ref[:GLOB, :128].astype(F32)).astype(BF16)
    grad_ref[:GLOB, :128] = (by_lane(dot(ds, k_s[0])) * 0.125).astype(BF16)
    gk_s[...] = dot(ds, qm, TN)
    gv_s[...] = dot(p, dom, TN)
    blocks = range(4)
    rows = [slice(GLOB + 128 * b, GLOB + 128 * (b + 1)) for b in blocks]
    wins = [(arr, slice(first, first + width)) for arr, first, width, _, _ in WINDOWS]
    turned = [
        dot(
            flip,
            jnp.concatenate(
                [
                    qkv_ref[r, :128],
                    (do_ref[r].astype(F32) * inv_ref[r]).astype(BF16),
                    o_ref[r],
                ],
                axis=1,
            ),
        )
        for r in rows
    ]
    qms = [by_head(x[:, :128]) for x in turned]
    qm_ts = [x.T.astype(BF16) for x in qms]
    qms = [x.astype(BF16) for x in qms]
    ps = [p_ref[0, 0, :, OFFSETS[b] : OFFSETS[b] + WINDOWS[b][2]] for b in blocks]
    grads = [
        score_grads(x[:, 128:256], x[:, 256:], p, v_s[arr, win])
        for x, p, (arr, win) in zip(turned, ps, wins)
    ]
    doms = [dom for dom, _ in grads]
    dss = [ds.astype(BF16) for _, ds in grads]
    labs = []
    for b, window in enumerate(WINDOWS):
        labs.append(collect(zero_glob(grads[b][1], window[-1]), b).astype(BF16))
    gqs = [
        by_lane(dot(ds, k_s[arr, win]) + dot(lab, relt_ref[...])) * 0.125
        for ds, lab, (arr, win) in zip(dss, labs, wins)
    ]
    gks = [dot(ds, qm, TN) for ds, qm in zip(dss, qms)]
    gvs = [dot(p, dom, TN) for p, dom in zip(ps, doms)]
    grel = sum(dot(qm_t, lab) for qm_t, lab in zip(qm_ts, labs))
    grel_ref[...] += grel * 0.125
    for r, gq in zip(rows, gqs):
        grad_ref[r, :128] = dot(flip, gq.astype(BF16)).astype(BF16)
    for b, (arr, first, width, _, _) in enumerate(WINDOWS):
        win = wins[b][1]
        for acc, part in ((gk_s, gks[b]), (gv_s, gvs[b])):
            if arr == 0:
                acc[win] += part
            else:
                acc[GLOB + first : T] += part[: width - GLOB]
                acc[:GLOB] += part[width - GLOB :]
    grad_ref[:, 128:256] = (gk_s[...] * 0.125).astype(BF16)
    grad_ref[:, 256:384] = gv_s[...].astype(BF16)


def attend_back(deps, proj, relt, gmixed, mixed, inv, p, pg, first_pair, start, pairs):
    rows = proj.shape[0]
    seqs = rows // T
    return run(
        attend_back_kernel,
        deps,
        [],
        [proj, relt, gmixed, mixed, inv, p, pg],
        [
            jax.ShapeDtypeStruct((rows, pairs * WAYS), BF16),
            jax.ShapeDtypeStruct((pairs * 128, LABELS), F32),
        ],
        "attend_back",
        8 * pairs,
        grid=(pairs, seqs),
        in_specs=[
            pl.BlockSpec((T, WAYS), lambda p, s: (s, start + p)),
            pl.BlockSpec((LABELS, 128), lambda p, s: (0, first_pair + start + p)),
            pl.BlockSpec((T, 128), lambda p, s: (s, first_pair + start + p)),
            pl.BlockSpec((T, 128), lambda p, s: (s, start + p)),
            pl.BlockSpec((T, 128), lambda p, s: (s, start + p)),
            pl.BlockSpec((1, 1, 256, P_COLS), lambda p, s: (s, start + p, 0, 0)),
            pl.BlockSpec((1, 1, 2 * GLOB, T), lambda p, s: (s, start + p, 0, 0)),
        ],
        out_specs=[pl.BlockSpec((T, WAYS), lambda p, s: (s, p)), pl.BlockSpec((128, LABELS), lambda p, s: (p, 0))],
        scratch_shapes=[
            pltpu.VMEM((T, 128), F32),
            pltpu.VMEM((T, 128), F32),
            pltpu.VMEM((2, T, 128), BF16),
            pltpu.VMEM((2, T, 128), BF16),
        ],
    )


def mix_out_kernel(lines, n_pieces, first_col, n_mix, pos_ref, len_ref, long_ref, glob_ref, clong_ref, cglob_ref, vec_ref, *rest):
    mixed = rest[:n_mix]
    pieces = rest[n_mix : n_mix + n_pieces]
    res_ref, n2_ref, g_ref, w_s, long_s, glob_s, sems, late_sems = rest[n_mix + n_pieces :]
    copies = load_rows(pieces, pos_ref, lines, w_s, sems, first_col)
    late = [
        pltpu.make_async_copy(src, dst, late_sems.at[i])
        for i, (src, dst) in enumerate(((long_ref, long_s), (glob_ref, glob_s)))
    ]
    for copy in late:
        copy.start()
    seqs = long_ref.shape[0]
    for s in range(seqs):
        live = live_mask(len_ref[s], D)
        at = T * s
        g_ref[at : at + GLOB] = jnp.where(live[:GLOB], cglob_ref[s, 0].astype(F32), 0.0).astype(BF16)
        g_ref[at + GLOB : at + T] = jnp.where(live[GLOB:], clong_ref[s, 0].astype(F32), 0.0).astype(BF16)
    for copy in copies:
        copy.wait()
    for c in tiles(D):
        acc = vec_ref[OUT_B : OUT_B + 1, c]
        at = 0
        for m in mixed:
            acc = acc + dot(m[...], w_s[at : at + m.shape[1], c])
            at += m.shape[1]
        res_ref[:, c] = acc
    for copy in late:
        copy.wait()
    for s in range(seqs):
        for part, at, size in ((glob_s, T * s, GLOB), (long_s, T * s + GLOB, SEQ)):
            res = res_ref[at : at + size] + part[s, 0].astype(F32)
            res_ref[at : at + size] = res
            xhat, _ = norm_stats(res)
            n2_ref[at : at + size] = (
                xhat * vec_ref[GAIN2 : GAIN2 + 1] + vec_ref[BIAS2 : BIAS2 + 1]
            ).astype(BF16)


def mix_out(deps, pos, lengths, long_in, glob_in, cot_long, cot_glob, vec, mixed, pieces, first_col):
    rows = long_in.shape[0] * T
    lines = pos.shape[0]
    return run(
        functools.partial(mix_out_kernel, lines, len(pieces), first_col, len(mixed)),
        deps,
        [pos, lengths],
        [long_in, glob_in, cot_long, cot_glob, vec, *mixed, *pieces],
        [
            jax.ShapeDtypeStruct((rows, D), F32),
            jax.ShapeDtypeStruct((rows, D), BF16),
            jax.ShapeDtypeStruct((rows, D), BF16),
        ],
        "mix_out",
        10,
        grid=(1,),
        in_specs=[ANY] * 2 + [VMEM] * (3 + len(mixed)) + [ANY] * len(pieces),
        out_specs=[VMEM] * 3,
        scratch_shapes=[
            pltpu.VMEM((D, D), BF16),
            pltpu.VMEM(long_in.shape, BF16),
            pltpu.VMEM(glob_in.shape, BF16),
            pltpu.SemaphoreType.DMA((lines,)),
            pltpu.SemaphoreType.DMA((2,)),
        ],
    )


def store_rows(src, outs, rows, src_pos_ref, sems, first_col):
    cols = src.shape[1]
    copies = []
    k = 0
    for out in outs:
        for i in range(out.shape[0]):
            start = pl.multiple_of(src_pos_ref[k] * rows, 16)
            copies.append(
                pltpu.make_async_copy(
                    src.at[pl.ds(start, rows), :], out.at[i, :, pl.ds(first_col, cols)], sems.at[k]
                )
            )
            k += 1
    return copies


def gelu_parts(v):
    cdf = 0.5 * (1.0 + lax.erf(v * 0.7071067811865476))
    pdf = jnp.exp(v * v * -0.5) * 0.3989422804014327
    return v * cdf, cdf + v * pdf


def ffn_kernel(lines, n_in, n_parts, n_out, first, pos_ref, n2_ref, g_ref, vec_ref, *rest):
    pieces = rest[:n_in]
    y_ref, gn2_ref, gb_ref = rest[n_in : n_in + 3]
    outs = rest[n_in + 3 : n_in + 3 + n_out]
    w_in_s, w_down_s, act_s, gpre_s, gw_s, y_s, gn2_s, sems, out_sems = rest[n_in + 3 + n_out :]
    part = pl.program_id(0)
    piece_rows = outs[0].shape[1]

    def weights(i, start):
        copies = load_rows(pieces, pos_ref, lines, w_in_s.at[i], sems.at[2 * i], i * D, start)
        return copies + load_rows(
            pieces, pos_ref, lines, w_down_s.at[i], sems.at[2 * i + 1], (n_parts + i) * D, start
        )

    @pl.when(part == 0)
    def _():
        for i in range(n_parts):
            weights(i, True)

    for i in range(n_parts):

        @pl.when(part == i)
        def _(i=i):
            for copy in weights(i, False):
                copy.wait()


    for c in tiles(D):
        pre = dot(n2_ref[...], w_in_s[part, :, c]) + vec_ref[pl.ds(IN_B + first + part, 1), c]
        act, slope = gelu_parts(pre)
        act_s[:, c] = act.astype(BF16)
        gpre = (dot(g_ref[...], w_down_s[part, c, :], NT) * slope).astype(BF16)
        gpre_s[:, c] = gpre
        gb_ref[:, c] = jnp.sum(gpre.astype(F32), axis=0, keepdims=True)

    def flush(which):
        first = pl.multiple_of((which * n_parts + part) * D, 128)
        return store_rows(gw_s.at[which], outs, piece_rows, pos_ref, out_sems.at[which], first)

    for which, (lhs, rhs) in enumerate(((n2_ref, gpre_s), (act_s, g_ref))):
        for c in tiles(D):
            gw_s[which, :, c] = dot(lhs[...], rhs[:, c], TN).astype(BF16)
        for copy in flush(which):
            copy.start()

    def outputs(first_part, last_part):
        for c in tiles(D):
            for total_s, out_ref, part_sum in (
                (y_s, y_ref, dot(act_s[...], w_down_s[part, :, c])),
                (gn2_s, gn2_ref, dot(gpre_s[...], w_in_s[part, c, :], NT)),
            ):
                if not first_part:
                    part_sum = total_s[:, c] + part_sum
                if last_part:
                    out_ref[:, c] = part_sum.astype(BF16)
                else:
                    total_s[:, c] = part_sum

    for i in range(n_parts):
        pl.when(part == i)(functools.partial(outputs, i == 0, i == n_parts - 1))
    for which in range(2):
        for copy in flush(which):
            copy.wait()


def ffn(deps, pos, n2, g, vec, pieces, first, n_parts, out_groups):
    rows = n2.shape[0]
    lines = pos.shape[0]
    full = pl.BlockSpec((rows, D), lambda q, *_: (0, 0))
    return run(
        functools.partial(ffn_kernel, lines, len(pieces), n_parts, len(out_groups), first),
        deps,
        [pos],
        [n2, g, vec, *pieces],
        [
            jax.ShapeDtypeStruct((rows, D), BF16),
            jax.ShapeDtypeStruct((rows, D), BF16),
            jax.ShapeDtypeStruct((1, n_parts * D), F32),
        ]
        + [jax.ShapeDtypeStruct((k, D // lines, 2 * n_parts * D), BF16) for k in out_groups],
        "ffn",
        28,
        grid=(n_parts,),
        in_specs=[full, full, VMEM] + [ANY] * len(pieces),
        out_specs=[full, full, pl.BlockSpec((1, D), lambda q, *_: (0, q))] + [ANY] * len(out_groups),
        scratch_shapes=[
            pltpu.VMEM((n_parts, D, D), BF16),
            pltpu.VMEM((n_parts, D, D), BF16),
            pltpu.VMEM((rows, D), BF16),
            pltpu.VMEM((rows, D), BF16),
            pltpu.VMEM((2, D, D), BF16),
            pltpu.VMEM((rows, D), F32),
            pltpu.VMEM((rows, D), F32),
            pltpu.SemaphoreType.DMA((2 * n_parts, lines)),
            pltpu.SemaphoreType.DMA((2, lines)),
        ],
    )


def mid_kernel(lines, n_in, first_col, n_mix, n_part, pos_ref, len_ref, res_ref, g_ref, vec_ref, *rest):
    ys = rest[:n_part]
    gns = rest[n_part : 2 * n_part]
    mixed = rest[2 * n_part : 2 * n_part + n_mix]
    rest = rest[2 * n_part + n_mix :]
    pieces = rest[:n_in]
    long_ref, glob_ref, gres_ref, gmix_ref, small_ref, gw_ref = rest[n_in : n_in + 6]
    w_s, gattn_s, gw_s, sems = rest[n_in + 6 :]
    s = pl.program_id(0)

    @pl.when(s == 0)
    def _():
        for copy in load_rows(pieces, pos_ref, lines, w_s, sems, first_col):
            copy.wait()
        gw_s[...] = jnp.zeros_like(gw_s)
        small_ref[...] = jnp.zeros_like(small_ref)

    live = live_mask(len_ref[s], D)
    res = res_ref[...]
    y = res + vec_ref[DOWN_B : DOWN_B + 1]
    gn2 = gns[0][...].astype(F32)
    for ref in ys:
        y = y + ref[...].astype(F32)
    for ref in gns[1:]:
        gn2 = gn2 + ref[...].astype(F32)
    y = jnp.where(live, y, 0.0).astype(BF16)
    glob_ref[0, 0] = y[:GLOB]
    long_ref[0, 0] = y[GLOB:]
    xhat, rstd = norm_stats(res)
    g = g_ref[...].astype(F32)
    gres = g + norm_back(gn2, xhat, rstd, vec_ref[GAIN2 : GAIN2 + 1])
    gattn = gres.astype(BF16)
    gres_ref[...] = gattn
    gattn_s[...] = gattn
    small_ref[0:1] += jnp.sum(gn2 * xhat, axis=0, keepdims=True)
    small_ref[1:2] += jnp.sum(gn2, axis=0, keepdims=True)
    small_ref[2:3] += jnp.sum(gattn.astype(F32), axis=0, keepdims=True)
    small_ref[3:4] += jnp.sum(g, axis=0, keepdims=True)

    for c in tiles(D):
        gmix_ref[:, c] = dot(gattn_s[...], w_s[c, :], NT).astype(BF16)
        at = 0
        for m in mixed:
            gw_s[at : at + m.shape[1], c] += dot(m[...], gattn_s[:, c], TN)
            at += m.shape[1]

    @pl.when(s == pl.num_programs(0) - 1)
    def _():
        gw_ref[...] = gw_s[...].astype(BF16)


def mid(deps, pos, lengths, res, g, vec, ys, gns, mixed, pieces, first_col, long_shape, glob_shape):
    rows = res.shape[0]
    lines = pos.shape[0]
    spec = pl.BlockSpec((T, D), lambda s, *_: (s, 0))
    return run(
        functools.partial(mid_kernel, lines, len(pieces), first_col, len(mixed), len(ys)),
        deps,
        [pos, lengths],
        [res, g, vec, *ys, *gns, *mixed, *pieces],
        [
            jax.ShapeDtypeStruct(long_shape, BF16),
            jax.ShapeDtypeStruct(glob_shape, BF16),
            jax.ShapeDtypeStruct((rows, D), BF16),
            jax.ShapeDtypeStruct((rows, D), BF16),
            jax.ShapeDtypeStruct((8, D), F32),
            jax.ShapeDtypeStruct((D, D), BF16),
        ],
        "mid",
        17,
        grid=(rows // T,),
        in_specs=[spec, spec, VMEM]
        + [spec] * (2 * len(ys))
        + [pl.BlockSpec((T, m.shape[1]), lambda s, *_: (s, 0)) for m in mixed]
        + [ANY] * len(pieces),
        out_specs=[
            pl.BlockSpec((1, 1, SEQ, D), lambda s, *_: (s, 0, 0, 0)),
            pl.BlockSpec((1, 1, GLOB, D), lambda s, *_: (s, 0, 0, 0)),
            spec,
            spec,
            pl.BlockSpec((8, D), lambda s, *_: (0, 0)),
            pl.BlockSpec((D, D), lambda s, *_: (0, 0)),
        ],
        scratch_shapes=[
            pltpu.VMEM((D, D), BF16),
            pltpu.VMEM((T, D), BF16),
            pltpu.VMEM((D, D), F32),
            pltpu.SemaphoreType.DMA((lines,)),
        ],
    )


def weight_kernel(n_grads, n_out, owned, pos_ref, normed_ref, *rest):
    grads = rest[:n_grads]
    extra = rest[n_grads : len(rest) - n_out - 2]
    outs = rest[len(rest) - n_out - 2 : len(rest) - 2]
    gw_s, out_sems = rest[len(rest) - 2 :]
    piece_rows = outs[0].shape[1]
    width = sum(ref.shape[1] for ref in grads) // 3
    at = 3 * width
    if owned:
        grels, (small2_ref, small1_ref, qv_ref, *gbs) = extra[:2], extra[2:]
        sides = dot(qv_ref[:2].astype(BF16), owner_order(owned), NT)
        half = D // 2
        a = jnp.concatenate([sides[:1, :half], sides[1:, :half]], axis=1)
        b = jnp.concatenate([sides[:1, half:], sides[1:, half:]], axis=1)
        vecs = [small1_ref[:2], a, b, small2_ref[:4]]
        vecs += [ref[:, D * i : D * (i + 1)] for ref in gbs for i in range(ref.shape[1] // D)]
        vecs = jnp.concatenate(vecs + [jnp.zeros((128 - 12, D), F32)], axis=0).T
        gw_s[:, at + LABELS :] = vecs.astype(BF16)
        row = 0
        for ref in grels:
            gw_s[row : row + ref.shape[0], at : at + LABELS] = ref[...].astype(BF16)
            row += ref.shape[0]
    else:
        for ref in extra:
            gw_s[:, at : at + ref.shape[1]] = ref[...].astype(BF16)
            at += ref.shape[1]
    first_pair = 0
    for grad_ref in grads:
        cols = grad_ref.shape[1]
        for c in tiles(cols):
            out = dot(normed_ref[...], grad_ref[:, c], TN).astype(BF16)
            for at in range(c.start, c.stop, 128):
                pair, part = at // WAYS, at % WAYS // 128
                to = width * part + 128 * (first_pair + pair)
                gw_s[:, to : to + 128] = out[:, at - c.start : at - c.start + 128]
        first_pair += cols // WAYS
    copies = store_rows(gw_s, outs, piece_rows, pos_ref, out_sems, 0)
    for copy in copies:
        copy.start()
    for copy in copies:
        copy.wait()


def weight_grad(deps, pos, normed, grads, extra, out_groups, owned=0):
    rows = normed.shape[0]
    lines = pos.shape[0]
    cols = sum(g.shape[1] for g in grads)
    cols += LABELS + 128 if owned else sum(r.shape[1] for r in extra)
    return run(
        functools.partial(weight_kernel, len(grads), len(out_groups), owned),
        deps,
        [pos],
        [normed, *grads, *extra],
        [jax.ShapeDtypeStruct((k, D // lines, cols), BF16) for k in out_groups],
        "weight_grad",
        cols / 200,
        grid=(1,),
        in_specs=[VMEM] * (1 + len(grads) + len(extra)),
        out_specs=[ANY] * len(out_groups),
        scratch_shapes=[pltpu.VMEM((D, cols), BF16), pltpu.SemaphoreType.DMA((lines,))],
    )


def input_kernel(lines, n_grads, n_in, pos_ref, long_in_ref, glob_in_ref, gres_ref, vec_ref, *rest):
    grads = rest[:n_grads]
    pieces = rest[n_grads : n_grads + 2 * n_in]
    long_ref, glob_ref, small_ref, qv_ref, w_s, gn1_s, long_s, glob_s, gres_s, sems, late_sems = rest[
        n_grads + 2 * n_in :
    ]
    copies = []
    to = 0
    for i, width in enumerate((FIRST, SECOND)):
        for pair in range(width // 128):
            for part in range(3):
                copies += load_rows(
                    pieces[n_in * i : n_in * (i + 1)],
                    pos_ref,
                    lines,
                    w_s.at[:, to : to + 128],
                    sems.at[to // 128],
                    width * part + 128 * pair,
                )
                to += 128
    late = [
        pltpu.make_async_copy(src, dst, late_sems.at[i])
        for i, (src, dst) in enumerate(
            ((long_in_ref, long_s), (glob_in_ref, glob_s), (gres_ref, gres_s))
        )
    ]
    for copy in late:
        copy.start()
    at = 0
    for ref in grads:
        for pair in range(ref.shape[1] // WAYS):
            for row, part in ((0, 0), (1, 2)):
                col = WAYS * pair + 128 * part
                qv_ref[row : row + 1, at : at + 128] = jnp.sum(
                    ref[:, col : col + 128].astype(F32), axis=0, keepdims=True
                )
            at += 128
    for copy in copies:
        copy.wait()
    for c in tiles(D):
        total = 0.0
        at = 0
        for ref in grads:
            total = total + dot(ref[...], w_s[c, at : at + ref.shape[1]], NT)
            at += ref.shape[1]
        gn1_s[:, c] = total
    for copy in late:
        copy.wait()
    for s in range(long_in_ref.shape[0]):
        for src, dst, at, size in (
            (glob_s, glob_ref, T * s, GLOB),
            (long_s, long_ref, T * s + GLOB, SEQ),
        ):
            rows = slice(at, at + size)
            xhat, rstd = norm_stats(src[s, 0].astype(F32))
            gn1 = gn1_s[rows]
            dst[s, 0] = (gres_s[rows].astype(F32) + norm_back(gn1, xhat, rstd, vec_ref[GAIN1 : GAIN1 + 1])).astype(BF16)
            sums = [jnp.sum(gn1 * xhat, axis=0, keepdims=True), jnp.sum(gn1, axis=0, keepdims=True)]
            for row in range(2):
                if s == 0 and src is glob_s:
                    small_ref[row : row + 1] = sums[row]
                else:
                    small_ref[row : row + 1] += sums[row]


def input_grad(deps, pos, long_in, glob_in, gres, vec, grads, pieces):
    rows = gres.shape[0]
    lines = pos.shape[0]
    n = len(grads)
    return run(
        functools.partial(input_kernel, lines, n, len(pieces[0])),
        deps,
        [pos],
        [long_in, glob_in, gres, vec, *grads, *[p for group in pieces for p in group]],
        [
            jax.ShapeDtypeStruct(long_in.shape, BF16),
            jax.ShapeDtypeStruct(glob_in.shape, BF16),
            jax.ShapeDtypeStruct((8, D), F32),
            jax.ShapeDtypeStruct((8, D), F32),
        ],
        "input_grad",
        15,
        grid=(1,),
        in_specs=[ANY] * 3 + [VMEM] * (1 + n) + [ANY] * sum(len(p) for p in pieces),
        out_specs=[VMEM] * 4,
        scratch_shapes=[
            pltpu.VMEM((D, 3 * D), BF16),
            pltpu.VMEM((rows, D), F32),
            pltpu.VMEM(long_in.shape, BF16),
            pltpu.VMEM(glob_in.shape, BF16),
            pltpu.VMEM(gres.shape, BF16),
            pltpu.SemaphoreType.DMA((3 * D // 128, lines)),
            pltpu.SemaphoreType.DMA((3,)),
        ],
    )


def pack_kernel(w_qkv_ref, rel_ref, *rest):
    vec_refs, out_ref = rest[:-1], rest[-1]
    width = FIRST
    for n in range(3):
        out_ref[:, width * n : width * (n + 1)] = w_qkv_ref[:, D * n : D * n + width]
    rows = rel_ref.shape[0]
    vecs = []
    for ref in vec_refs:
        v = ref[...].astype(F32)
        vecs += [v[at : at + rows].reshape(1, rows) for at in range(0, v.shape[0], rows)]
    vecs = jnp.concatenate(vecs + [jnp.zeros((128 - len(vecs), rows), F32)], axis=0).T
    rel = jnp.concatenate(
        [
            jnp.zeros((rows, LEAD), F32),
            rel_ref[...].astype(F32),
            jnp.zeros((rows, VEC_AT - LEAD - RELS), F32),
            vecs[:, : LABELS - VEC_AT],
        ],
        axis=1,
    )
    out_ref[:, 3 * width :] = rel.astype(BF16)


def pack(w_qkv, rel_embed, vecs):
    rows = w_qkv.shape[0]
    return run(
        pack_kernel,
        [],
        [],
        [w_qkv, rel_embed, *vecs],
        [jax.ShapeDtypeStruct((rows, 3 * FIRST + LABELS), BF16)],
        "pack",
        1.5,
        grid=(1,),
        in_specs=[VMEM] * (2 + len(vecs)),
        out_specs=[VMEM],
        scratch_shapes=[],
    )[0]


def pack_next_kernel(w_qkv_ref, w_out_ref, out_ref):
    width = SECOND
    for n in range(3):
        out_ref[:, width * n : width * (n + 1)] = w_qkv_ref[:, D * (n + 1) - width : D * (n + 1)]
    out_ref[:, 3 * width :] = w_out_ref[...]


def pack_next(deps, w_qkv, w_out):
    rows = w_qkv.shape[0]
    return run(
        pack_next_kernel,
        deps,
        [],
        [w_qkv, w_out],
        [jax.ShapeDtypeStruct((rows, 3 * SECOND + D), BF16)],
        "pack",
        1.5,
        grid=(1,),
        in_specs=[VMEM] * 2,
        out_specs=[VMEM],
        scratch_shapes=[],
    )[0]


def pack_ffn_kernel(chunks, w_in_ref, w_down_ref, out_ref):
    rows = w_in_ref.shape[0]
    parts = FF // D
    per = parts // chunks
    down = w_down_ref[...].astype(F32)
    for c in range(chunks):
        at = 2 * per * D * c
        out_ref[:, at : at + per * D] = w_in_ref[:, per * D * c : per * D * (c + 1)]
        for i in range(per):
            q = per * c + i
            to = at + (per + i) * D
            out_ref[:, to : to + D] = down[rows * q : rows * (q + 1)].astype(BF16)


def pack_ffn(deps, w_in, w_down, chunks):
    rows = w_in.shape[0]
    return run(
        functools.partial(pack_ffn_kernel, chunks),
        deps,
        [],
        [w_in, w_down],
        [jax.ShapeDtypeStruct((rows, 2 * FF), BF16)],
        "pack",
        1.5,
        grid=(1,),
        in_specs=[VMEM] * 2,
        out_specs=[VMEM],
        scratch_shapes=[],
    )[0]


def unpack_kernel(n, *refs):
    g_qkv_ref, g_out_ref, g_rel_ref, *vec_refs = refs[2 * n :]
    for g, width in enumerate((FIRST, SECOND)):
        total = refs[n * g][...].astype(F32)
        for ref in refs[n * g + 1 : n * (g + 1)]:
            total = total + ref[...].astype(F32)
        for part in range(3):
            at = D * part + FIRST * g
            g_qkv_ref[:, at : at + width] = total[:, width * part : width * (part + 1)]
        if g == 1:
            g_out_ref[...] = total[:, 3 * width :]
        else:
            g_rel_ref[...] = total[:, 3 * width + BACK_LEAD : 3 * width + BACK_LEAD + RELS]
            rows = total.shape[0]
            vecs = total[:, 3 * width + LABELS :]
            vecs = jnp.concatenate([vecs, jnp.zeros((128 - rows, 128), F32)], axis=0).T
            row = 0
            for ref in vec_refs:
                for at in range(0, ref.shape[0], rows):
                    ref[pl.ds(at, rows)] = vecs[row : row + 1, :rows].reshape(rows)
                    row += 1


def unpack(first, second, sizes):
    rows = first[0].shape[0]
    shape = lambda cols: jax.ShapeDtypeStruct((rows, cols), F32)
    return run(
        functools.partial(unpack_kernel, len(first)),
        [],
        [],
        [*first, *second],
        [shape(3 * D), shape(D), shape(RELS)] + [jax.ShapeDtypeStruct((n,), F32) for n in sizes],
        "unpack",
        2,
        grid=(1,),
        in_specs=[VMEM] * (2 * len(first)),
        out_specs=[VMEM] * (3 + len(sizes)),
        scratch_shapes=[],
    )


def order_kernel(count, z_ref, *refs):
    parts, outs, total_s = refs[: -1 - count], refs[-1 - count : -1], refs[-1]
    for mask, part in enumerate(parts):
        total_s[z_ref[0] ^ mask] = part[...].astype(F32)
    cols = outs[0].shape[1]
    for i, out in enumerate(outs):
        out[...] = total_s[:, :, cols * i : cols * (i + 1)].reshape(out.shape).astype(out.dtype)


def order(deps, z, parts, count):
    rows, cols = parts[0].shape
    lines = len(parts)
    return run(
        functools.partial(order_kernel, count),
        deps,
        [z],
        parts,
        [jax.ShapeDtypeStruct((lines * rows, cols // count), parts[0].dtype)] * count,
        "order",
        1.5,
        grid=(1,),
        in_specs=[VMEM] * lines,
        out_specs=[VMEM] * count,
        scratch_shapes=[pltpu.VMEM((lines, rows, cols), F32)],
    )


def unpack_ffn_kernel(chunks, *refs):
    terms, (g_in_ref, g_down_ref) = refs[:-2], refs[-2:]
    rows = g_in_ref.shape[0]
    parts = FF // D
    per = parts // chunks
    for q in range(parts):
        at = 2 * per * D * (q // per) + D * (q % per)
        for out, first in ((g_in_ref, at), (g_down_ref, at + per * D)):
            total = terms[0][:, first : first + D].astype(F32)
            for ref in terms[1:]:
                total = total + ref[:, first : first + D].astype(F32)
            if out is g_in_ref:
                out[:, D * q : D * (q + 1)] = total
            else:
                out[rows * q : rows * (q + 1), :] = total


def unpack_ffn(deps, terms, chunks):
    rows = terms[0].shape[0]
    return run(
        functools.partial(unpack_ffn_kernel, chunks),
        deps,
        [],
        terms,
        [jax.ShapeDtypeStruct((rows, FF), F32), jax.ShapeDtypeStruct((rows * (FF // D), D), F32)],
        "unpack",
        2,
        grid=(1,),
        in_specs=[VMEM] * len(terms),
        out_specs=[VMEM] * 2,
        scratch_shapes=[],
    )


def split_kernel(lines, counts, z_ref, *refs):
    outs = refs[sum(counts) : sum(counts) + lines]
    total_s = refs[-1]
    first = 0
    at = 0
    for n in counts:
        terms = refs[first : first + n]
        rows, cols = terms[0].shape[-2:]
        total = terms[0][...].reshape(rows, cols).astype(F32)
        for ref in terms[1:]:
            total = total + ref[...].reshape(rows, cols).astype(F32)
        total_s[:, :, at : at + cols] = total.reshape(lines, rows // lines, cols)
        first += n
        at += cols
    for mask, out in enumerate(outs):
        out[...] = total_s[z_ref[0] ^ mask].astype(out.dtype)


def split(deps, z, sums, lines):
    kind = sums[0][0].dtype
    specs = []
    for t in [t for terms in sums for t in terms]:
        if t.ndim == 3:
            specs.append(pl.BlockSpec((1,) + t.shape[1:], lambda i, *_: (0, 0, 0)))
        else:
            specs.append(pl.BlockSpec(t.shape, lambda i, *_: (0, 0)))
    rows = sums[0][0].shape[-2] // lines
    cols = sum(terms[0].shape[-1] for terms in sums)
    return run(
        functools.partial(split_kernel, lines, [len(terms) for terms in sums]),
        deps,
        [z],
        [t for terms in sums for t in terms],
        [jax.ShapeDtypeStruct((rows, cols), F32 if m == 0 else kind) for m in range(lines)],
        "split",
        2,
        grid=(1,),
        in_specs=specs,
        out_specs=[VMEM] * lines,
        scratch_shapes=[pltpu.VMEM((lines, rows, cols), F32)],
    )


def sum_kernel(*refs):
    total = refs[0][...].astype(F32)
    for ref in refs[1:-1]:
        total = total + ref[...].astype(F32)
    refs[-1][...] = total.reshape(refs[-1].shape).astype(refs[-1].dtype)


def second(deps, terms):
    _, rows, cols = terms[0].shape
    return run(
        sum_kernel,
        deps,
        [],
        terms,
        [jax.ShapeDtypeStruct((rows, cols), terms[0].dtype)],
        "second",
        2,
        grid=(1,),
        in_specs=[pl.BlockSpec((1, rows, cols), lambda i: (1, 0, 0))] * len(terms),
        out_specs=[VMEM],
        scratch_shapes=[],
    )[0]


def both(deps, terms):
    lines, rows, cols = terms[0].shape
    spec = pl.BlockSpec((1, rows, cols), lambda i: (i, 0, 0))
    return run(
        sum_kernel,
        deps,
        [],
        terms,
        [jax.ShapeDtypeStruct(terms[0].shape, terms[0].dtype)],
        "both",
        2,
        grid=(lines,),
        in_specs=[spec] * len(terms),
        out_specs=[spec],
        scratch_shapes=[],
    )[0]


AXES = ("wide", "narrow")


class Links:
    def __init__(self, mesh):
        self.wide = mesh.shape["wide"]
        self.narrow = mesh.shape["narrow"]
        self.count = self.wide * self.narrow
        self.pairwise = self.wide == 8 and self.narrow == 4
        self.lines = self.wide if self.pairwise else 1
        self.groups = (2, 2, 2, 2) if self.pairwise else (1,)

    def setup(self):
        if not self.pairwise:
            self.pos = jnp.zeros((1,), jnp.int32)
            return
        w = lax.axis_index("wide")
        self.z = lax.axis_index("narrow")
        near = jnp.where(w % 2 == 0, 2, 4)
        far = 6 - near
        order = [0, near, far, 6, 1, 1 ^ far, 1 ^ near, 7]
        self.pos = jnp.stack([w ^ m for m in order]).astype(jnp.int32)

    def slot(self, *marks):
        self.marks = list(marks)

    def swap(self, x, wide_mask=0, narrow_mask=0):
        masks = wide_mask if isinstance(wide_mask, tuple) else (wide_mask, wide_mask)
        pairs = []
        for w in range(self.wide):
            for z in range(self.narrow):
                pairs.append(
                    (w * self.narrow + z, (w ^ masks[w % 2]) * self.narrow + (z ^ narrow_mask))
                )
        return lax.ppermute(x, AXES, pairs)

    def line(self, x):
        if not self.pairwise:
            return [lax.all_gather(x, AXES, axis=0, tiled=True)]
        return [x] + [self.swap(x, 0, mask) for mask in (1, 2, 3)]

    def own(self, parts):
        if not self.pairwise:
            return parts
        (x,) = order(self.marks, self.z.reshape(1), parts, 1)
        return self.around(x)

    def around(self, x):
        return [x, self.swap(x, (2, 4)), self.swap(x, (4, 2)), self.swap(x, 1)]

    def onward(self, lines):
        if not self.pairwise:
            return lines
        own, near, far, own_core = lines
        if self.marks:
            near = after(near, self.marks)
            far = after(far, self.marks)
        return [own, near, far, self.swap(near, (4, 2)), own_core, self.swap(near, 1), self.swap(far, 1)]

    def core(self, lines):
        if not self.pairwise:
            return lines
        own, near, far, both, *core = lines
        if self.marks:
            both = after(both, self.marks)
        return [own, near, far, both, *core, self.swap(both, 1)]

    def add(self, *parts):
        total = parts[0].astype(F32)
        for p in parts[1:]:
            total = total + p.astype(F32)
        return total


class Sum:
    def __init__(self, links, parts):
        self.links = links
        self.parts = parts
        self.kind = parts[0].dtype

    def core(self, marks=()):
        links = self.links
        if not links.pairwise:
            self.src = self.out = lax.psum_scatter(self.parts[0][0].astype(F32), AXES, scatter_dimension=0, tiled=True)
            return (self.out,)
        send_a, send_b = self.parts[2], self.parts[3]
        if marks:
            send_a, send_b = after(send_a, marks), after(send_b, marks)
        self.got_b = links.swap(send_b, 1)
        self.got_a = links.swap(send_a, 1)
        return (self.got_b, self.got_a)

    def far(self):
        links = self.links
        if not links.pairwise:
            return (self.out,)
        self.src = both(links.marks, [self.parts[1], self.got_b])
        self.from_far = links.swap(self.src, (4, 2))
        return (self.from_far,)

    def near(self):
        links = self.links
        if not links.pairwise:
            return (self.out,)
        self.src = second(links.marks, [self.parts[0], self.got_a, self.from_far])
        self.from_near = links.swap(self.src, (2, 4))
        return (self.from_near,)

    def line(self, *more):
        links = self.links
        sums = (self,) + more
        if not links.pairwise:
            self.terms = [jnp.concatenate([x.out for x in sums], axis=1)]
            return self.terms
        terms = [[x.parts[0], x.got_a, x.from_far, x.from_near] for x in sums]
        mine, *others = split(links.marks, links.z.reshape(1), terms, links.narrow)
        self.src = mine
        self.terms = [mine] + [links.swap(x, 0, mask) for mask, x in enumerate(others, 1)]
        return self.terms[1:]

    def total(self):
        return self.links.add(*self.terms)


CHUNKS = 2
PARTS = FF // D
PAIRS = 6


def body(links, long_in, glob_in, lengths, ln1_gain, ln1_bias, w_qkv, qv_bias, rel_embed, w_out, out_bias, ln2_gain, ln2_bias, w_in, in_bias, w_down, down_bias, cot_long, cot_glob):
    links.setup()
    pos = links.pos
    groups = links.groups
    count = links.count
    micro = long_in.shape[0]
    r = w_qkv.shape[0]
    lens = lengths.reshape(micro)
    per = PARTS // CHUNKS
    first, second = 3 * FIRST, 3 * SECOND
    n_first, n_second = FIRST // 128, SECOND // 128

    vectors = [ln1_gain, ln1_bias, qv_bias, out_bias, ln2_gain, ln2_bias, down_bias, in_bias]
    w_in_parts = w_in.reshape(r, count, PARTS, r).transpose(0, 2, 1, 3).reshape(r, FF)

    links.slot()
    own_a0 = links.own(links.line(pack(w_qkv, rel_embed, vectors)))
    line_a1 = links.line(pack_next([own_a0[0]], w_qkv, w_out))
    ffn_shard = pack_ffn([], w_in_parts, w_down, CHUNKS)
    links.slot(own_a0[len(own_a0) // 2])
    most_a0 = links.onward(own_a0)
    links.slot(*line_a1[1:], ffn_shard)
    attn = [links.core(most_a0)]
    line_f = links.line(after(ffn_shard, [attn[0][-1]]))

    proj0, normed, rel_all, rel_turned, vec = project_first([], pos, long_in, glob_in, attn[0], r, first)
    links.slot(attn[0][-1])
    own_a1 = links.own(line_a1)
    mixed0, inv0, p0, pg0 = attend([own_a1[-1], own_a1[0]], lens, proj0, rel_all, 0)
    links.slot(proj0)
    most_a1 = links.onward(own_a1)
    links.slot(mixed0)
    if links.pairwise:
        line_f = order(links.marks, links.z.reshape(1), line_f, CHUNKS)
        own_f = [links.around(line_f[0])]
    else:
        own_f = [[line_f[0][:, 2 * per * D * c : 2 * per * D * (c + 1)]] for c in range(CHUNKS)]
    links.slot(mixed0)
    attn.append(links.core(most_a1))
    proj1 = project_next([mixed0, own_f[0][0]], pos, normed, vec, attn[1], second)
    mixed1, inv1, p1, pg1 = attend([], lens, proj1, rel_all, n_first)
    mixed = [mixed0, mixed1]
    if links.pairwise:
        own_f.append(links.around(after(line_f[1], [proj1])))
    links.slot(mixed1)
    most_f0 = links.onward(own_f[0])
    most_f1 = links.onward(own_f[1])
    res, n2, g_ffn = mix_out(
        [most_f0[0]], pos, lens, long_in, glob_in, cot_long, cot_glob, vec, mixed, attn[1], second
    )
    links.slot(n2)
    ffn0 = links.core(most_f0)
    y0, gn0, gb0, *gw0 = ffn([], pos, n2, g_ffn, vec, ffn0, 0, per, groups)
    links.slot(y0)
    ffn1 = links.core(most_f1)
    sum0 = Sum(links, gw0)
    y1, gn1, gb1, *gw1 = ffn([y0], pos, n2, g_ffn, vec, ffn1, per, per, groups)
    core0 = sum0.core()
    sum1 = Sum(links, gw1)
    links.slot(y1)
    far0 = sum0.far()
    block_long, block_glob, gres, gmix, small2, gw_out = mid(
        [sum0.src], pos, lens, res, g_ffn, vec, [y0, y1], [gn0, gn1], mixed, attn[1], second, long_in.shape, glob_in.shape
    )
    core1 = sum1.core()
    links.slot(gmix)
    near0 = sum0.near()
    sum1.far()
    gproj1, grel1 = attend_back([sum0.src, sum1.src], proj1, rel_turned, gmix, mixed1, inv1, p1, pg1, n_first, 0, n_second)
    links.slot(gproj1)
    sum1.near()
    gw_a1 = weight_grad([sum1.src, *near0], pos, normed, [gproj1], [gw_out], groups)
    sum2 = Sum(links, gw_a1)
    sum2.core()
    links.slot(gw_a1[0])
    line01 = sum0.line(sum1)
    gproj0, grel0 = attend_back([sum0.src], proj0, rel_turned, gmix, mixed0, inv0, p0, pg0, 0, 0, n_first)
    links.slot(gproj0)
    sum2.far()
    grad_long, grad_glob, small1, small_qv = input_grad(
        [sum2.src], pos, long_in, glob_in, gres, vec, [gproj0, gproj1], attn
    )
    links.slot(small1)
    near2 = sum2.near()
    gw_a0 = weight_grad(
        [sum2.src, *line01], pos, normed, [gproj0], [grel0, grel1, small2, small1, small_qv, gb0, gb1], groups, r
    )
    sum3 = Sum(links, gw_a0)
    sum3.core(near2)
    links.slot(gw_a0[0])
    sum3.far()
    links.slot(sum3.src)
    sum2.line()
    g_in, g_down = unpack_ffn([sum3.src], sum0.terms, CHUNKS)
    links.slot(sum2.src, g_in)
    sum3.near()
    g_in = g_in.reshape(r, PARTS, count, r).transpose(0, 2, 1, 3).reshape(r, FF)
    links.slot()
    sum3.line()
    order_out = [ln1_gain, ln1_bias, qv_bias, ln2_gain, ln2_bias, out_bias, down_bias, in_bias]
    g_qkv, g_out, g_rel, g_gain1, g_bias1, g_qv, g_gain2, g_bias2, g_out_b, g_down_b, g_in_b = unpack(
        sum3.terms, sum2.terms, [v.shape[0] for v in order_out]
    )
    return (
        block_long, block_glob, grad_long, grad_glob,
        g_gain1, g_bias1, g_qkv, g_qv, g_rel, g_out, g_out_b,
        g_gain2, g_bias2, g_in, g_in_b, g_down, g_down_b,
    )


def solution(mesh):
    rows = P(None, AXES, None, None)
    vec = P(AXES)
    mat = P(AXES, None)
    placed = (rows, rows, P(None, AXES), vec, vec, mat, vec, mat, mat, vec, vec, vec, mat, vec, mat, vec, rows, rows)
    return jax.shard_map(
        functools.partial(body, Links(mesh)),
        mesh=mesh,
        in_specs=placed,
        out_specs=(rows, rows, rows, rows, vec, vec, mat, vec, mat, mat, vec, vec, vec, mat, vec, mat, vec),
        check_vma=False,
    )
```

```python
import functools
import jax
import jax.numpy as jnp
from jax import lax
from jax.experimental import pallas as pl
from jax.experimental.pallas import tpu as pltpu
from jax.sharding import PartitionSpec as P

HEAD_DIM = 64
RADIUS = 84
STRIDE = 16
SEQ = 512
GLOB = 32
RELS = 169
T = GLOB + SEQ
D = 768
FF = 3072
PAIRS = 6
LABELS = 256
LEAD = 4
BACK_LEAD = 3
LABEL_END = LEAD + RELS
EPS = 1e-06
NEG = -1e30
F32 = jnp.float32
BF16 = jnp.bfloat16
VMEM_LIMIT = (64 << 20) - (256 << 10)
WINDOWS = ((0, 0, 256, 328, 0), (0, 0, 384, 72, 0), (1, 160, 384, 8, 352), (1, 288, 256, 8, 224))
OFFSETS = (0, 256, 640, 1024)
WAYS = 3 * 128
VEC_AT = 176
GAIN1, BIAS1, QV, OUT_B, GAIN2, BIAS2, DOWN_B, IN_B, VECS = 0, 1, 2, 4, 5, 6, 7, 8, 16
P_COLS = 1280
NN = (((1,), (0,)), ((), ()))
NT = (((1,), (1,)), ((), ()))
TN = (((0,), (0,)), ((), ()))


def dot(a, b, dims=NN):
    return lax.dot_general(a, b, dims, preferred_element_type=F32)


def run(kernel, deps, prefetch, inputs, out_shape, name, cost, grid, in_specs, out_specs, scratch_shapes):
    n = len(prefetch)

    def with_deps(*refs):
        kernel(*refs[:n], *refs[n + len(deps) :])

    anywhere = pl.BlockSpec(memory_space=pl.ANY)
    return pl.pallas_call(
        with_deps,
        grid_spec=pltpu.PrefetchScalarGridSpec(
            num_scalar_prefetch=n,
            grid=grid,
            in_specs=[anywhere] * len(deps) + in_specs,
            out_specs=out_specs,
            scratch_shapes=scratch_shapes,
        ),
        out_shape=out_shape,
        compiler_params=pltpu.CompilerParams(vmem_limit_bytes=VMEM_LIMIT),
        cost_estimate=pl.CostEstimate(flops=int(cost * 1.15e9), bytes_accessed=1 << 20, transcendentals=0),
        name=name,
    )(*prefetch, *deps, *inputs)


def after(x, deps):
    anywhere = pl.BlockSpec(memory_space=pl.ANY)
    return pl.pallas_call(
        lambda *refs: None,
        in_specs=[anywhere] * (1 + len(deps)),
        out_specs=anywhere,
        out_shape=jax.ShapeDtypeStruct(x.shape, x.dtype),
        input_output_aliases={0: 0},
        name="after",
    )(x, *deps)


def iota(shape, dim):
    return lax.broadcasted_iota(jnp.int32, shape, dim)


def norm_stats(x):
    cen = x - jnp.mean(x, axis=1, keepdims=True)
    rstd = lax.rsqrt(jnp.mean(cen * cen, axis=1, keepdims=True) + EPS)
    return cen * rstd, rstd


def norm_back(grad, xhat, rstd, gain):
    gg = grad * gain
    return rstd * (
        gg - jnp.mean(gg, axis=1, keepdims=True) - xhat * jnp.mean(gg * xhat, axis=1, keepdims=True)
    )


def tiles(cols, size=256):
    return [slice(at, min(at + size, cols)) for at in range(0, cols, size)]


def live_mask(length, cols):
    row = iota((T, cols), 0)
    glob_count = (length + STRIDE - 1) // STRIDE
    return row < jnp.where(row < GLOB, glob_count, length + GLOB)


def load_rows(pieces, pos_ref, lines, dst, sems, first_col, start=True):
    rows = dst.shape[0] // lines
    cols = dst.shape[1]
    copies = []
    k = 0
    for piece in pieces:
        for i in range(piece.shape[0] // rows):
            to = pl.multiple_of(pos_ref[k] * rows, 16)
            copies.append(
                pltpu.make_async_copy(
                    piece.at[pl.ds(i * rows, rows), pl.ds(first_col, cols)],
                    dst.at[pl.ds(to, rows), :],
                    sems.at[k],
                )
            )
            k += 1
    if start:
        for copy in copies:
            copy.start()
    return copies


FIRST = 2 * 128
SECOND = D - FIRST


def owner_order(rows):
    k = iota((D, 1), 0)
    late = (k >= D // 2).astype(jnp.int32)
    k = k - late * (D // 2)
    owner = ((k.astype(F32) + 0.5) * (1.0 / rows)).astype(jnp.int32)
    col = rows * owner + k + late * rows
    return (iota((D, D), 1) == col).astype(F32).astype(BF16)


def project_kernel(lines, n_pieces, first, rows, pos_ref, *rest):
    if first:
        long_ref, glob_ref = rest[:2]
    else:
        normed_ref, vec_ref = rest[:2]
    pieces = rest[2 : 2 + n_pieces]
    if first:
        proj_ref, normed_ref, rel_ref, relt_ref, vec_ref, w_s, sems = rest[2 + n_pieces :]
    else:
        proj_ref, w_s, sems = rest[2 + n_pieces :]
    cols = proj_ref.shape[1]
    width = cols // 3
    copies = load_rows(pieces, pos_ref, lines, w_s, sems.at[0], 0)
    if first:
        for copy in load_rows(pieces, pos_ref, lines, rel_ref, sems.at[1], cols):
            copy.wait()
        turned = rel_ref[...].astype(F32).T
        vec_ref[...] = turned[VEC_AT : VEC_AT + VECS]
        drop = LEAD - BACK_LEAD
        labels = jnp.concatenate([turned[drop:], turned[:drop]], axis=0)
        label = iota((LABELS, D), 0) - BACK_LEAD
        relt_ref[...] = jnp.where((label >= 0) & (label < RELS), labels, 0.0).astype(BF16)
        a, b = vec_ref[QV : QV + 1], vec_ref[QV + 1 : QV + 2]
        half = D // 2
        sides = jnp.concatenate(
            [
                jnp.concatenate([a[:, :half], b[:, :half]], axis=1),
                jnp.concatenate([a[:, half:], b[:, half:]], axis=1),
            ],
            axis=0,
        )
        vec_ref[QV : QV + 2] = dot(sides.astype(BF16), owner_order(rows))
        for s in range(long_ref.shape[0]):
            for part, at, size in ((glob_ref, T * s, GLOB), (long_ref, T * s + GLOB, SEQ)):
                xhat, _ = norm_stats(part[s, 0].astype(F32))
                normed_ref[at : at + size] = (
                    xhat * vec_ref[GAIN1 : GAIN1 + 1] + vec_ref[BIAS1 : BIAS1 + 1]
                ).astype(BF16)
    own = slice(0, width) if first else slice(D - width, D)
    full_bias = jnp.concatenate(
        [vec_ref[QV : QV + 1, own], jnp.zeros((1, width), F32), vec_ref[QV + 1 : QV + 2, own]], axis=1
    )
    for copy in copies:
        copy.wait()
    for c in tiles(cols):
        out = (dot(normed_ref[...], w_s[:, c]) + full_bias[:, c]).astype(BF16)
        for at in range(c.start, c.stop, 128):
            to = by_pair(at, width)
            proj_ref[:, to : to + 128] = out[:, at - c.start : at - c.start + 128]


def by_pair(col, width):
    return WAYS * (col % width // 128) + 128 * (col // width)


VMEM = pl.BlockSpec(memory_space=pltpu.VMEM)
ANY = pl.BlockSpec(memory_space=pl.ANY)


def project_first(deps, pos, long_in, glob_in, pieces, owned, cols):
    rows = long_in.shape[0] * T
    lines = pos.shape[0]
    shape = lambda *dims: jax.ShapeDtypeStruct(dims, BF16)
    return run(
        functools.partial(project_kernel, lines, len(pieces), True, owned),
        deps,
        [pos],
        [long_in, glob_in, *pieces],
        [
            shape(rows, cols),
            shape(rows, D),
            shape(D, LABELS),
            shape(LABELS, D),
            jax.ShapeDtypeStruct((VECS, D), F32),
        ],
        "project",
        9,
        grid=(1,),
        in_specs=[VMEM] * 2 + [ANY] * len(pieces),
        out_specs=[VMEM] * 5,
        scratch_shapes=[pltpu.VMEM((D, cols), BF16), pltpu.SemaphoreType.DMA((2, lines))],
    )


def project_next(deps, pos, normed, vec, pieces, cols):
    rows = normed.shape[0]
    lines = pos.shape[0]
    return run(
        functools.partial(project_kernel, lines, len(pieces), False, 0),
        deps,
        [pos],
        [normed, vec, *pieces],
        [jax.ShapeDtypeStruct((rows, cols), BF16)],
        "project",
        8,
        grid=(1,),
        in_specs=[VMEM] * 2 + [ANY] * len(pieces),
        out_specs=[VMEM],
        scratch_shapes=[pltpu.VMEM((D, cols), BF16), pltpu.SemaphoreType.DMA((2, lines))],
    )[0]


def flip_matrix(size):
    row, col = iota((size, size), 0), iota((size, size), 1)
    return ((row // 128 == col // 128) & (row % 128 + col % 128 == 127)).astype(F32).astype(BF16)


def by_head(x):
    even = iota(x.shape, 1) < HEAD_DIM
    return jnp.concatenate([jnp.where(even, x, 0.0), jnp.where(even, 0.0, x)], axis=0)


def by_lane(x):
    half = x.shape[0] // 2
    even = iota((half, x.shape[1]), 1) < HEAD_DIM
    return jnp.where(even, x[:half], x[half:])


def spread(x, b):
    _, _, width, shift, _ = WINDOWS[b]
    shift = shift if shift < 256 else shift - 384
    lane = iota((64, 128), 1)
    none = jnp.full((64, 128), NEG, F32)
    parts = []
    for at in range(0, 256, 64):
        start = shift + at % 128
        turned = pltpu.roll(x[at : at + 64], start % 256, 1, stride=1, stride_axis=0)
        low, high = turned[:, :128], turned[:, 128:]
        if start < 0:
            cols = [low, jnp.where(lane < 64, high, NEG), none]
        elif start + 64 + LABEL_END <= 256:
            cols = [low, high, none]
        elif start >= 128:
            cols = [none, high, low]
        else:
            cols = [jnp.where(lane >= 64, low, NEG), high, jnp.where(lane < 64, low, NEG)]
        parts.append(jnp.concatenate(cols[: width // 128], axis=1))
    return jnp.concatenate(parts, axis=0)


def collect(cols, b):
    _, _, width, shift, _ = WINDOWS[b]
    shift = shift if shift < 256 else shift - 384
    lane = iota((64, 128), 1)
    parts = []
    for at in range(0, 256, 64):
        start = shift + 64 - at % 128
        tiles_ = [c[at : at + 64] for c in cols]
        if start < 0:
            low, high = tiles_[0], jnp.where(lane < 64, tiles_[1], 0.0)
        elif start + 64 + LABEL_END <= 256:
            low, high = tiles_[0], tiles_[1]
        elif start >= 128:
            low, high = tiles_[2], tiles_[1]
        elif len(tiles_) > 2:
            low, high = jnp.where(lane >= 64, tiles_[0], tiles_[2]), tiles_[1]
        else:
            low, high = jnp.where(lane >= 64, tiles_[0], 0.0), tiles_[1]
        back = (BACK_LEAD - LEAD - 63 - start) % 256
        parts.append(
            pltpu.roll(jnp.concatenate([low, high], axis=1), back, 1, stride=1, stride_axis=0)
        )
    return jnp.concatenate(parts, axis=0)


def zero_glob(x, at):
    cols = [x[:, 128 * i : 128 * (i + 1)] for i in range(x.shape[1] // 128)]
    lane = iota(cols[0].shape, 1) - at % 128
    cols[at // 128] = jnp.where((lane >= 0) & (lane < GLOB), 0.0, cols[at // 128])
    return cols


def attend_kernel(len_ref, qkv_ref, rel_ref, mix_ref, inv_ref, p_ref, pg_ref, k_s, v_s, rel_s):
    dead = jnp.where(live_mask(len_ref[pl.program_id(0)], 128), 0.0, NEG)
    flag = iota((T, 128), 1) == 0
    k = jnp.concatenate(
        [qkv_ref[:, 128:256], jnp.where(flag, dead, 0.0).astype(BF16)], axis=1
    )
    v = jnp.concatenate([qkv_ref[:, 256:384], jnp.ones((T, 128), BF16)], axis=1)
    for s, m in ((k_s, k), (v_s, v)):
        s[0] = m
        s[1, :SEQ] = m[GLOB:]
        s[1, SEQ:] = m[:GLOB]
    label = iota((128, LABELS), 1)
    outside = ((label < LEAD) | (label >= LEAD + RELS)) & (iota((128, LABELS), 0) == 0)
    rel_s[:128] = rel_ref[...]
    rel_s[128:] = jnp.where(outside, NEG, 0.0).astype(BF16)
    flip = flip_matrix(256)

    def queries(rows):
        x = by_head(qkv_ref[rows, :128].astype(F32) * 0.125)
        one = (iota(x.shape, 1) == 0).astype(F32)
        return jnp.concatenate([x, one], axis=1).astype(BF16)

    def weights(scores):
        return jnp.exp(scores - jnp.max(scores, axis=1, keepdims=True)).astype(BF16)

    rows = [slice(0, GLOB)] + [slice(GLOB + 128 * b, GLOB + 128 * (b + 1)) for b in range(4)]
    wins = [(0, slice(0, T))] + [(arr, slice(first, first + width)) for arr, first, width, _, _ in WINDOWS]
    qs = [queries(r) for r in rows]
    scores = [dot(q, k_s[arr, win], NT) for q, (arr, win) in zip(qs, wins)]
    biases = [dot(q, rel_s[...]) for q in qs[1:]]
    for b, window in enumerate(WINDOWS):
        bias = zero_glob(spread(biases[b], b), window[-1])
        scores[b + 1] = scores[b + 1] + jnp.concatenate(bias, axis=1)
    ps = [weights(x) for x in scores]
    pg_ref[0, 0] = ps[0]
    outs = [dot(p, v_s[arr, win]) for p, (arr, win) in zip(ps, wins)]
    turned = [dot(flip, p) for p in ps[1:]]
    for r, out in zip(rows, outs):
        inv = by_lane(1.0 / out[:, 128:])
        inv_ref[r] = inv
        mix_ref[r] = (by_lane(out[:, :128]) * inv).astype(BF16)
    for b, p in enumerate(turned):
        p_ref[0, 0, :, OFFSETS[b] : OFFSETS[b] + p.shape[1]] = p.astype(BF16)


def attend(deps, lengths, proj, rel, first_pair):
    rows = proj.shape[0]
    seqs = rows // T
    pairs = proj.shape[1] // WAYS
    return run(
        attend_kernel,
        deps,
        [lengths],
        [proj, rel],
        [
            jax.ShapeDtypeStruct((rows, pairs * 128), BF16),
            jax.ShapeDtypeStruct((rows, pairs * 128), F32),
            jax.ShapeDtypeStruct((seqs, pairs, 256, P_COLS), BF16),
            jax.ShapeDtypeStruct((seqs, pairs, 2 * GLOB, T), BF16),
        ],
        "attend",
        6.2 * pairs,
        grid=(seqs, pairs),
        in_specs=[
            pl.BlockSpec((T, WAYS), lambda s, p, *_: (s, p)),
            pl.BlockSpec((128, LABELS), lambda s, p, *_: (first_pair + p, 0)),
        ],
        out_specs=[
            pl.BlockSpec((T, 128), lambda s, p, *_: (s, p)),
            pl.BlockSpec((T, 128), lambda s, p, *_: (s, p)),
            pl.BlockSpec((1, 1, 256, P_COLS), lambda s, p, *_: (s, p, 0, 0)),
            pl.BlockSpec((1, 1, 2 * GLOB, T), lambda s, p, *_: (s, p, 0, 0)),
        ],
        scratch_shapes=[
            pltpu.VMEM((2, T, 256), BF16),
            pltpu.VMEM((2, T, 256), BF16),
            pltpu.VMEM((256, LABELS), BF16),
        ],
    )


def attend_back_kernel(qkv_ref, relt_ref, do_ref, o_ref, inv_ref, p_ref, pg_ref, grad_ref, grel_ref, gk_s, gv_s, k_s, v_s):
    k = qkv_ref[:, 128:256]
    v = qkv_ref[:, 256:384]
    for s, m in ((k_s, k), (v_s, v)):
        s[0] = m
        s[1, :SEQ] = m[GLOB:]
        s[1, SEQ:] = m[:GLOB]
    flip = flip_matrix(128)

    @pl.when(pl.program_id(1) == 0)
    def _():
        grel_ref[...] = jnp.zeros_like(grel_ref)

    ones = jnp.ones((256, 128), BF16)

    def score_grads(do, o, p, v_win):
        prod = by_head(do * o)
        high = prod.astype(BF16)
        low = (prod - high.astype(F32)).astype(BF16)
        centre = dot(jnp.concatenate([high, low], axis=1), ones)
        dom = by_head(do).astype(BF16)
        dp = dot(dom, v_win, NT)
        width = dp.shape[1]
        cols = [dp[:, c] - centre[:, : c.stop - c.start] for c in tiles(width, 128)]
        return dom, p.astype(F32) * jnp.concatenate(cols, axis=1)

    do = (do_ref[:GLOB].astype(F32) * inv_ref[:GLOB]).astype(BF16).astype(F32)
    p = pg_ref[0, 0]
    dom, ds = score_grads(do, o_ref[:GLOB].astype(F32), p, v_s[0])
    ds = ds.astype(BF16)
    qm = by_head(qkv_ref[:GLOB, :128].astype(F32)).astype(BF16)
    grad_ref[:GLOB, :128] = (by_lane(dot(ds, k_s[0])) * 0.125).astype(BF16)
    gk_s[...] = dot(ds, qm, TN)
    gv_s[...] = dot(p, dom, TN)
    blocks = range(4)
    rows = [slice(GLOB + 128 * b, GLOB + 128 * (b + 1)) for b in blocks]
    wins = [(arr, slice(first, first + width)) for arr, first, width, _, _ in WINDOWS]
    turned = [
        dot(
            flip,
            jnp.concatenate(
                [
                    qkv_ref[r, :128],
                    (do_ref[r].astype(F32) * inv_ref[r]).astype(BF16),
                    o_ref[r],
                ],
                axis=1,
            ),
        )
        for r in rows
    ]
    qms = [by_head(x[:, :128]) for x in turned]
    qm_ts = [x.T.astype(BF16) for x in qms]
    qms = [x.astype(BF16) for x in qms]
    ps = [p_ref[0, 0, :, OFFSETS[b] : OFFSETS[b] + WINDOWS[b][2]] for b in blocks]
    grads = [
        score_grads(x[:, 128:256], x[:, 256:], p, v_s[arr, win])
        for x, p, (arr, win) in zip(turned, ps, wins)
    ]
    doms = [dom for dom, _ in grads]
    dss = [ds.astype(BF16) for _, ds in grads]
    labs = []
    for b, window in enumerate(WINDOWS):
        labs.append(collect(zero_glob(grads[b][1], window[-1]), b).astype(BF16))
    gqs = [
        by_lane(dot(ds, k_s[arr, win]) + dot(lab, relt_ref[...])) * 0.125
        for ds, lab, (arr, win) in zip(dss, labs, wins)
    ]
    gks = [dot(ds, qm, TN) for ds, qm in zip(dss, qms)]
    gvs = [dot(p, dom, TN) for p, dom in zip(ps, doms)]
    grel = sum(dot(qm_t, lab) for qm_t, lab in zip(qm_ts, labs))
    grel_ref[...] += grel * 0.125
    for r, gq in zip(rows, gqs):
        grad_ref[r, :128] = dot(flip, gq.astype(BF16)).astype(BF16)
    for b, (arr, first, width, _, _) in enumerate(WINDOWS):
        win = wins[b][1]
        for acc, part in ((gk_s, gks[b]), (gv_s, gvs[b])):
            if arr == 0:
                acc[win] += part
            else:
                acc[GLOB + first : T] += part[: width - GLOB]
                acc[:GLOB] += part[width - GLOB :]
    grad_ref[:, 128:256] = (gk_s[...] * 0.125).astype(BF16)
    grad_ref[:, 256:384] = gv_s[...].astype(BF16)


def attend_back(deps, proj, relt, gmixed, mixed, inv, p, pg, first_pair, start, pairs):
    rows = proj.shape[0]
    seqs = rows // T
    return run(
        attend_back_kernel,
        deps,
        [],
        [proj, relt, gmixed, mixed, inv, p, pg],
        [
            jax.ShapeDtypeStruct((rows, pairs * WAYS), BF16),
            jax.ShapeDtypeStruct((pairs * 128, LABELS), F32),
        ],
        "attend_back",
        8 * pairs,
        grid=(pairs, seqs),
        in_specs=[
            pl.BlockSpec((T, WAYS), lambda p, s: (s, start + p)),
            pl.BlockSpec((LABELS, 128), lambda p, s: (0, first_pair + start + p)),
            pl.BlockSpec((T, 128), lambda p, s: (s, first_pair + start + p)),
            pl.BlockSpec((T, 128), lambda p, s: (s, start + p)),
            pl.BlockSpec((T, 128), lambda p, s: (s, start + p)),
            pl.BlockSpec((1, 1, 256, P_COLS), lambda p, s: (s, start + p, 0, 0)),
            pl.BlockSpec((1, 1, 2 * GLOB, T), lambda p, s: (s, start + p, 0, 0)),
        ],
        out_specs=[pl.BlockSpec((T, WAYS), lambda p, s: (s, p)), pl.BlockSpec((128, LABELS), lambda p, s: (p, 0))],
        scratch_shapes=[
            pltpu.VMEM((T, 128), F32),
            pltpu.VMEM((T, 128), F32),
            pltpu.VMEM((2, T, 128), BF16),
            pltpu.VMEM((2, T, 128), BF16),
        ],
    )


def mix_out_kernel(lines, n_pieces, first_col, n_mix, pos_ref, len_ref, long_ref, glob_ref, clong_ref, cglob_ref, vec_ref, *rest):
    mixed = rest[:n_mix]
    pieces = rest[n_mix : n_mix + n_pieces]
    res_ref, n2_ref, g_ref, w_s, long_s, glob_s, res_s, sems, late_sems = rest[n_mix + n_pieces :]
    copies = load_rows(pieces, pos_ref, lines, w_s, sems, first_col)
    late = [
        pltpu.make_async_copy(src, dst, late_sems.at[i])
        for i, (src, dst) in enumerate(((long_ref, long_s), (glob_ref, glob_s)))
    ]
    for copy in late:
        copy.start()
    seqs = long_ref.shape[0]
    for s in range(seqs):
        live = live_mask(len_ref[s], D)
        at = T * s
        g_ref[at : at + GLOB] = jnp.where(live[:GLOB], cglob_ref[s, 0].astype(F32), 0.0).astype(BF16)
        g_ref[at + GLOB : at + T] = jnp.where(live[GLOB:], clong_ref[s, 0].astype(F32), 0.0).astype(BF16)
    for copy in copies:
        copy.wait()
    for c in tiles(D):
        acc = vec_ref[OUT_B : OUT_B + 1, c]
        at = 0
        for m in mixed:
            acc = acc + dot(m[...], w_s[at : at + m.shape[1], c])
            at += m.shape[1]
        res_s[:, c] = acc
    for copy in late:
        copy.wait()
    for s in range(seqs):
        for part, at, size in ((glob_s, T * s, GLOB), (long_s, T * s + GLOB, SEQ)):
            res = res_s[at : at + size] + part[s, 0].astype(F32)
            res_ref[at : at + size] = res.astype(BF16)
            xhat, _ = norm_stats(res)
            n2_ref[at : at + size] = (
                xhat * vec_ref[GAIN2 : GAIN2 + 1] + vec_ref[BIAS2 : BIAS2 + 1]
            ).astype(BF16)


def mix_out(deps, pos, lengths, long_in, glob_in, cot_long, cot_glob, vec, mixed, pieces, first_col):
    rows = long_in.shape[0] * T
    lines = pos.shape[0]
    return run(
        functools.partial(mix_out_kernel, lines, len(pieces), first_col, len(mixed)),
        deps,
        [pos, lengths],
        [long_in, glob_in, cot_long, cot_glob, vec, *mixed, *pieces],
        [
            jax.ShapeDtypeStruct((rows, D), BF16),
            jax.ShapeDtypeStruct((rows, D), BF16),
            jax.ShapeDtypeStruct((rows, D), BF16),
        ],
        "mix_out",
        10,
        grid=(1,),
        in_specs=[ANY] * 2 + [VMEM] * (3 + len(mixed)) + [ANY] * len(pieces),
        out_specs=[VMEM] * 3,
        scratch_shapes=[
            pltpu.VMEM((D, D), BF16),
            pltpu.VMEM(long_in.shape, BF16),
            pltpu.VMEM(glob_in.shape, BF16),
            pltpu.VMEM((rows, D), F32),
            pltpu.SemaphoreType.DMA((lines,)),
            pltpu.SemaphoreType.DMA((2,)),
        ],
    )


def store_rows(src, outs, rows, src_pos_ref, sems, first_col):
    cols = src.shape[1]
    copies = []
    k = 0
    for out in outs:
        for i in range(out.shape[0]):
            start = pl.multiple_of(src_pos_ref[k] * rows, 16)
            copies.append(
                pltpu.make_async_copy(
                    src.at[pl.ds(start, rows), :], out.at[i, :, pl.ds(first_col, cols)], sems.at[k]
                )
            )
            k += 1
    return copies


def gelu_parts(v):
    cdf = 0.5 * (1.0 + lax.erf(v * 0.7071067811865476))
    pdf = jnp.exp(v * v * -0.5) * 0.3989422804014327
    return v * cdf, cdf + v * pdf


def ffn_kernel(lines, n_in, n_parts, n_out, first, pos_ref, n2_ref, g_ref, vec_ref, *rest):
    pieces = rest[:n_in]
    y_ref, gn2_ref, gb_ref = rest[n_in : n_in + 3]
    outs = rest[n_in + 3 : n_in + 3 + n_out]
    w_in_s, w_down_s, act_s, gpre_s, gw_s, y_s, gn2_s, sems, out_sems = rest[n_in + 3 + n_out :]
    part = pl.program_id(0)
    piece_rows = outs[0].shape[1]

    def weights(i, start):
        copies = load_rows(pieces, pos_ref, lines, w_in_s.at[i], sems.at[2 * i], i * D, start)
        return copies + load_rows(
            pieces, pos_ref, lines, w_down_s.at[i], sems.at[2 * i + 1], (n_parts + i) * D, start
        )

    @pl.when(part == 0)
    def _():
        for i in range(n_parts):
            weights(i, True)

    for i in range(n_parts):

        @pl.when(part == i)
        def _(i=i):
            for copy in weights(i, False):
                copy.wait()


    for c in tiles(D):
        pre = dot(n2_ref[...], w_in_s[part, :, c]) + vec_ref[pl.ds(IN_B + first + part, 1), c]
        act, slope = gelu_parts(pre)
        act_s[:, c] = act.astype(BF16)
        gpre = (dot(g_ref[...], w_down_s[part, c, :], NT) * slope).astype(BF16)
        gpre_s[:, c] = gpre
        gb_ref[:, c] = jnp.sum(gpre.astype(F32), axis=0, keepdims=True)

    def flush(which):
        first = pl.multiple_of((which * n_parts + part) * D, 128)
        return store_rows(gw_s.at[which], outs, piece_rows, pos_ref, out_sems.at[which], first)

    for which, (lhs, rhs) in enumerate(((n2_ref, gpre_s), (act_s, g_ref))):
        for c in tiles(D):
            gw_s[which, :, c] = dot(lhs[...], rhs[:, c], TN).astype(BF16)
        for copy in flush(which):
            copy.start()

    def outputs(first_part, last_part):
        for c in tiles(D):
            for total_s, out_ref, part_sum in (
                (y_s, y_ref, dot(act_s[...], w_down_s[part, :, c])),
                (gn2_s, gn2_ref, dot(gpre_s[...], w_in_s[part, c, :], NT)),
            ):
                if not first_part:
                    part_sum = total_s[:, c] + part_sum
                if last_part:
                    out_ref[:, c] = part_sum.astype(BF16)
                else:
                    total_s[:, c] = part_sum

    for i in range(n_parts):
        pl.when(part == i)(functools.partial(outputs, i == 0, i == n_parts - 1))
    for which in range(2):
        for copy in flush(which):
            copy.wait()


def ffn(deps, pos, n2, g, vec, pieces, first, n_parts, out_groups):
    rows = n2.shape[0]
    lines = pos.shape[0]
    full = pl.BlockSpec((rows, D), lambda q, *_: (0, 0))
    return run(
        functools.partial(ffn_kernel, lines, len(pieces), n_parts, len(out_groups), first),
        deps,
        [pos],
        [n2, g, vec, *pieces],
        [
            jax.ShapeDtypeStruct((rows, D), BF16),
            jax.ShapeDtypeStruct((rows, D), BF16),
            jax.ShapeDtypeStruct((1, n_parts * D), F32),
        ]
        + [jax.ShapeDtypeStruct((k, D // lines, 2 * n_parts * D), BF16) for k in out_groups],
        "ffn",
        28,
        grid=(n_parts,),
        in_specs=[full, full, VMEM] + [ANY] * len(pieces),
        out_specs=[full, full, pl.BlockSpec((1, D), lambda q, *_: (0, q))] + [ANY] * len(out_groups),
        scratch_shapes=[
            pltpu.VMEM((n_parts, D, D), BF16),
            pltpu.VMEM((n_parts, D, D), BF16),
            pltpu.VMEM((rows, D), BF16),
            pltpu.VMEM((rows, D), BF16),
            pltpu.VMEM((2, D, D), BF16),
            pltpu.VMEM((rows, D), F32),
            pltpu.VMEM((rows, D), F32),
            pltpu.SemaphoreType.DMA((2 * n_parts, lines)),
            pltpu.SemaphoreType.DMA((2, lines)),
        ],
    )


def mid_kernel(lines, n_in, first_col, n_mix, n_part, pos_ref, len_ref, res_ref, g_ref, vec_ref, *rest):
    ys = rest[:n_part]
    gns = rest[n_part : 2 * n_part]
    mixed = rest[2 * n_part : 2 * n_part + n_mix]
    rest = rest[2 * n_part + n_mix :]
    pieces = rest[:n_in]
    long_ref, glob_ref, gres_ref, gmix_ref, small_ref, gw_ref = rest[n_in : n_in + 6]
    w_s, gattn_s, gw_s, sems = rest[n_in + 6 :]
    s = pl.program_id(0)

    @pl.when(s == 0)
    def _():
        for copy in load_rows(pieces, pos_ref, lines, w_s, sems, first_col):
            copy.wait()
        gw_s[...] = jnp.zeros_like(gw_s)
        small_ref[...] = jnp.zeros_like(small_ref)

    live = live_mask(len_ref[s], D)
    res = res_ref[...].astype(F32)
    y = res + vec_ref[DOWN_B : DOWN_B + 1]
    gn2 = gns[0][...].astype(F32)
    for ref in ys:
        y = y + ref[...].astype(F32)
    for ref in gns[1:]:
        gn2 = gn2 + ref[...].astype(F32)
    y = jnp.where(live, y, 0.0).astype(BF16)
    glob_ref[0, 0] = y[:GLOB]
    long_ref[0, 0] = y[GLOB:]
    xhat, rstd = norm_stats(res)
    g = g_ref[...].astype(F32)
    gres = g + norm_back(gn2, xhat, rstd, vec_ref[GAIN2 : GAIN2 + 1])
    gattn = gres.astype(BF16)
    gres_ref[...] = gattn
    gattn_s[...] = gattn
    small_ref[0:1] += jnp.sum(gn2 * xhat, axis=0, keepdims=True)
    small_ref[1:2] += jnp.sum(gn2, axis=0, keepdims=True)
    small_ref[2:3] += jnp.sum(gattn.astype(F32), axis=0, keepdims=True)
    small_ref[3:4] += jnp.sum(g, axis=0, keepdims=True)

    for c in tiles(D):
        gmix_ref[:, c] = dot(gattn_s[...], w_s[c, :], NT).astype(BF16)
        at = 0
        for m in mixed:
            gw_s[at : at + m.shape[1], c] += dot(m[...], gattn_s[:, c], TN)
            at += m.shape[1]

    @pl.when(s == pl.num_programs(0) - 1)
    def _():
        gw_ref[...] = gw_s[...].astype(BF16)


def mid(deps, pos, lengths, res, g, vec, ys, gns, mixed, pieces, first_col, long_shape, glob_shape):
    rows = res.shape[0]
    lines = pos.shape[0]
    spec = pl.BlockSpec((T, D), lambda s, *_: (s, 0))
    return run(
        functools.partial(mid_kernel, lines, len(pieces), first_col, len(mixed), len(ys)),
        deps,
        [pos, lengths],
        [res, g, vec, *ys, *gns, *mixed, *pieces],
        [
            jax.ShapeDtypeStruct(long_shape, BF16),
            jax.ShapeDtypeStruct(glob_shape, BF16),
            jax.ShapeDtypeStruct((rows, D), BF16),
            jax.ShapeDtypeStruct((rows, D), BF16),
            jax.ShapeDtypeStruct((8, D), F32),
            jax.ShapeDtypeStruct((D, D), BF16),
        ],
        "mid",
        17,
        grid=(rows // T,),
        in_specs=[spec, spec, VMEM]
        + [spec] * (2 * len(ys))
        + [pl.BlockSpec((T, m.shape[1]), lambda s, *_: (s, 0)) for m in mixed]
        + [ANY] * len(pieces),
        out_specs=[
            pl.BlockSpec((1, 1, SEQ, D), lambda s, *_: (s, 0, 0, 0)),
            pl.BlockSpec((1, 1, GLOB, D), lambda s, *_: (s, 0, 0, 0)),
            spec,
            spec,
            pl.BlockSpec((8, D), lambda s, *_: (0, 0)),
            pl.BlockSpec((D, D), lambda s, *_: (0, 0)),
        ],
        scratch_shapes=[
            pltpu.VMEM((D, D), BF16),
            pltpu.VMEM((T, D), BF16),
            pltpu.VMEM((D, D), F32),
            pltpu.SemaphoreType.DMA((lines,)),
        ],
    )


def weight_kernel(n_grads, n_out, owned, pos_ref, normed_ref, *rest):
    grads = rest[:n_grads]
    extra = rest[n_grads : len(rest) - n_out - 2]
    outs = rest[len(rest) - n_out - 2 : len(rest) - 2]
    gw_s, out_sems = rest[len(rest) - 2 :]
    piece_rows = outs[0].shape[1]
    width = sum(ref.shape[1] for ref in grads) // 3
    at = 3 * width
    if owned:
        grels, (small2_ref, small1_ref, qv_ref, *gbs) = extra[:2], extra[2:]
        sides = dot(qv_ref[:2].astype(BF16), owner_order(owned), NT)
        half = D // 2
        a = jnp.concatenate([sides[:1, :half], sides[1:, :half]], axis=1)
        b = jnp.concatenate([sides[:1, half:], sides[1:, half:]], axis=1)
        vecs = [small1_ref[:2], a, b, small2_ref[:4]]
        vecs += [ref[:, D * i : D * (i + 1)] for ref in gbs for i in range(ref.shape[1] // D)]
        vecs = jnp.concatenate(vecs + [jnp.zeros((128 - 12, D), F32)], axis=0).T
        gw_s[:, at + LABELS :] = vecs.astype(BF16)
        row = 0
        for ref in grels:
            gw_s[row : row + ref.shape[0], at : at + LABELS] = ref[...].astype(BF16)
            row += ref.shape[0]
    else:
        for ref in extra:
            gw_s[:, at : at + ref.shape[1]] = ref[...].astype(BF16)
            at += ref.shape[1]
    first_pair = 0
    for grad_ref in grads:
        cols = grad_ref.shape[1]
        for c in tiles(cols):
            out = dot(normed_ref[...], grad_ref[:, c], TN).astype(BF16)
            for at in range(c.start, c.stop, 128):
                pair, part = at // WAYS, at % WAYS // 128
                to = width * part + 128 * (first_pair + pair)
                gw_s[:, to : to + 128] = out[:, at - c.start : at - c.start + 128]
        first_pair += cols // WAYS
    copies = store_rows(gw_s, outs, piece_rows, pos_ref, out_sems, 0)
    for copy in copies:
        copy.start()
    for copy in copies:
        copy.wait()


def weight_grad(deps, pos, normed, grads, extra, out_groups, owned=0):
    rows = normed.shape[0]
    lines = pos.shape[0]
    cols = sum(g.shape[1] for g in grads)
    cols += LABELS + 128 if owned else sum(r.shape[1] for r in extra)
    return run(
        functools.partial(weight_kernel, len(grads), len(out_groups), owned),
        deps,
        [pos],
        [normed, *grads, *extra],
        [jax.ShapeDtypeStruct((k, D // lines, cols), BF16) for k in out_groups],
        "weight_grad",
        cols / 200,
        grid=(1,),
        in_specs=[VMEM] * (1 + len(grads) + len(extra)),
        out_specs=[ANY] * len(out_groups),
        scratch_shapes=[pltpu.VMEM((D, cols), BF16), pltpu.SemaphoreType.DMA((lines,))],
    )


def input_kernel(lines, n_grads, n_in, pos_ref, long_in_ref, glob_in_ref, gres_ref, vec_ref, *rest):
    grads = rest[:n_grads]
    pieces = rest[n_grads : n_grads + 2 * n_in]
    long_ref, glob_ref, small_ref, qv_ref, w_s, gn1_s, long_s, glob_s, gres_s, sems, late_sems = rest[
        n_grads + 2 * n_in :
    ]
    copies = []
    to = 0
    for i, width in enumerate((FIRST, SECOND)):
        for pair in range(width // 128):
            for part in range(3):
                copies += load_rows(
                    pieces[n_in * i : n_in * (i + 1)],
                    pos_ref,
                    lines,
                    w_s.at[:, to : to + 128],
                    sems.at[to // 128],
                    width * part + 128 * pair,
                )
                to += 128
    late = [
        pltpu.make_async_copy(src, dst, late_sems.at[i])
        for i, (src, dst) in enumerate(
            ((long_in_ref, long_s), (glob_in_ref, glob_s), (gres_ref, gres_s))
        )
    ]
    for copy in late:
        copy.start()
    at = 0
    for ref in grads:
        for pair in range(ref.shape[1] // WAYS):
            for row, part in ((0, 0), (1, 2)):
                col = WAYS * pair + 128 * part
                qv_ref[row : row + 1, at : at + 128] = jnp.sum(
                    ref[:, col : col + 128].astype(F32), axis=0, keepdims=True
                )
            at += 128
    for copy in copies:
        copy.wait()
    for c in tiles(D):
        total = 0.0
        at = 0
        for ref in grads:
            total = total + dot(ref[...], w_s[c, at : at + ref.shape[1]], NT)
            at += ref.shape[1]
        gn1_s[:, c] = total
    for copy in late:
        copy.wait()
    for s in range(long_in_ref.shape[0]):
        for src, dst, at, size in (
            (glob_s, glob_ref, T * s, GLOB),
            (long_s, long_ref, T * s + GLOB, SEQ),
        ):
            rows = slice(at, at + size)
            xhat, rstd = norm_stats(src[s, 0].astype(F32))
            gn1 = gn1_s[rows]
            dst[s, 0] = (gres_s[rows].astype(F32) + norm_back(gn1, xhat, rstd, vec_ref[GAIN1 : GAIN1 + 1])).astype(BF16)
            sums = [jnp.sum(gn1 * xhat, axis=0, keepdims=True), jnp.sum(gn1, axis=0, keepdims=True)]
            for row in range(2):
                if s == 0 and src is glob_s:
                    small_ref[row : row + 1] = sums[row]
                else:
                    small_ref[row : row + 1] += sums[row]


def input_grad(deps, pos, long_in, glob_in, gres, vec, grads, pieces):
    rows = gres.shape[0]
    lines = pos.shape[0]
    n = len(grads)
    return run(
        functools.partial(input_kernel, lines, n, len(pieces[0])),
        deps,
        [pos],
        [long_in, glob_in, gres, vec, *grads, *[p for group in pieces for p in group]],
        [
            jax.ShapeDtypeStruct(long_in.shape, BF16),
            jax.ShapeDtypeStruct(glob_in.shape, BF16),
            jax.ShapeDtypeStruct((8, D), F32),
            jax.ShapeDtypeStruct((8, D), F32),
        ],
        "input_grad",
        15,
        grid=(1,),
        in_specs=[ANY] * 3 + [VMEM] * (1 + n) + [ANY] * sum(len(p) for p in pieces),
        out_specs=[VMEM] * 4,
        scratch_shapes=[
            pltpu.VMEM((D, 3 * D), BF16),
            pltpu.VMEM((rows, D), F32),
            pltpu.VMEM(long_in.shape, BF16),
            pltpu.VMEM(glob_in.shape, BF16),
            pltpu.VMEM(gres.shape, BF16),
            pltpu.SemaphoreType.DMA((3 * D // 128, lines)),
            pltpu.SemaphoreType.DMA((3,)),
        ],
    )


def pack_kernel(w_qkv_ref, rel_ref, *rest):
    vec_refs, out_ref = rest[:-1], rest[-1]
    width = FIRST
    for n in range(3):
        out_ref[:, width * n : width * (n + 1)] = w_qkv_ref[:, D * n : D * n + width]
    rows = rel_ref.shape[0]
    vecs = []
    for ref in vec_refs:
        v = ref[...].astype(F32)
        vecs += [v[at : at + rows].reshape(1, rows) for at in range(0, v.shape[0], rows)]
    vecs = jnp.concatenate(vecs + [jnp.zeros((128 - len(vecs), rows), F32)], axis=0).T
    rel = jnp.concatenate(
        [
            jnp.zeros((rows, LEAD), F32),
            rel_ref[...].astype(F32),
            jnp.zeros((rows, VEC_AT - LEAD - RELS), F32),
            vecs[:, : LABELS - VEC_AT],
        ],
        axis=1,
    )
    out_ref[:, 3 * width :] = rel.astype(BF16)


def pack(w_qkv, rel_embed, vecs):
    rows = w_qkv.shape[0]
    return run(
        pack_kernel,
        [],
        [],
        [w_qkv, rel_embed, *vecs],
        [jax.ShapeDtypeStruct((rows, 3 * FIRST + LABELS), BF16)],
        "pack",
        1.5,
        grid=(1,),
        in_specs=[VMEM] * (2 + len(vecs)),
        out_specs=[VMEM],
        scratch_shapes=[],
    )[0]


def pack_next_kernel(w_qkv_ref, w_out_ref, out_ref):
    width = SECOND
    for n in range(3):
        out_ref[:, width * n : width * (n + 1)] = w_qkv_ref[:, D * (n + 1) - width : D * (n + 1)]
    out_ref[:, 3 * width :] = w_out_ref[...]


def pack_next(deps, w_qkv, w_out):
    rows = w_qkv.shape[0]
    return run(
        pack_next_kernel,
        deps,
        [],
        [w_qkv, w_out],
        [jax.ShapeDtypeStruct((rows, 3 * SECOND + D), BF16)],
        "pack",
        1.5,
        grid=(1,),
        in_specs=[VMEM] * 2,
        out_specs=[VMEM],
        scratch_shapes=[],
    )[0]


def pack_ffn_kernel(chunks, w_in_ref, w_down_ref, out_ref):
    rows = w_in_ref.shape[0]
    parts = FF // D
    per = parts // chunks
    down = w_down_ref[...].astype(F32)
    for c in range(chunks):
        at = 2 * per * D * c
        out_ref[:, at : at + per * D] = w_in_ref[:, per * D * c : per * D * (c + 1)]
        for i in range(per):
            q = per * c + i
            to = at + (per + i) * D
            out_ref[:, to : to + D] = down[rows * q : rows * (q + 1)].astype(BF16)


def pack_ffn(deps, w_in, w_down, chunks):
    rows = w_in.shape[0]
    return run(
        functools.partial(pack_ffn_kernel, chunks),
        deps,
        [],
        [w_in, w_down],
        [jax.ShapeDtypeStruct((rows, 2 * FF), BF16)],
        "pack",
        1.5,
        grid=(1,),
        in_specs=[VMEM] * 2,
        out_specs=[VMEM],
        scratch_shapes=[],
    )[0]


def unpack_kernel(n, *refs):
    g_qkv_ref, g_out_ref, g_rel_ref, *vec_refs = refs[2 * n :]
    for g, width in enumerate((FIRST, SECOND)):
        total = refs[n * g][...].astype(F32)
        for ref in refs[n * g + 1 : n * (g + 1)]:
            total = total + ref[...].astype(F32)
        for part in range(3):
            at = D * part + FIRST * g
            g_qkv_ref[:, at : at + width] = total[:, width * part : width * (part + 1)]
        if g == 1:
            g_out_ref[...] = total[:, 3 * width :]
        else:
            g_rel_ref[...] = total[:, 3 * width + BACK_LEAD : 3 * width + BACK_LEAD + RELS]
            rows = total.shape[0]
            vecs = total[:, 3 * width + LABELS :]
            vecs = jnp.concatenate([vecs, jnp.zeros((128 - rows, 128), F32)], axis=0).T
            row = 0
            for ref in vec_refs:
                for at in range(0, ref.shape[0], rows):
                    ref[pl.ds(at, rows)] = vecs[row : row + 1, :rows].reshape(rows)
                    row += 1


def unpack(first, second, sizes):
    rows = first[0].shape[0]
    shape = lambda cols: jax.ShapeDtypeStruct((rows, cols), F32)
    return run(
        functools.partial(unpack_kernel, len(first)),
        [],
        [],
        [*first, *second],
        [shape(3 * D), shape(D), shape(RELS)] + [jax.ShapeDtypeStruct((n,), F32) for n in sizes],
        "unpack",
        2,
        grid=(1,),
        in_specs=[VMEM] * (2 * len(first)),
        out_specs=[VMEM] * (3 + len(sizes)),
        scratch_shapes=[],
    )


def order_kernel(count, z_ref, *refs):
    parts, outs, total_s = refs[: -1 - count], refs[-1 - count : -1], refs[-1]
    for mask, part in enumerate(parts):
        total_s[z_ref[0] ^ mask] = part[...].astype(F32)
    cols = outs[0].shape[1]
    for i, out in enumerate(outs):
        out[...] = total_s[:, :, cols * i : cols * (i + 1)].reshape(out.shape).astype(out.dtype)


def order(deps, z, parts, count):
    rows, cols = parts[0].shape
    lines = len(parts)
    return run(
        functools.partial(order_kernel, count),
        deps,
        [z],
        parts,
        [jax.ShapeDtypeStruct((lines * rows, cols // count), parts[0].dtype)] * count,
        "order",
        1.5,
        grid=(1,),
        in_specs=[VMEM] * lines,
        out_specs=[VMEM] * count,
        scratch_shapes=[pltpu.VMEM((lines, rows, cols), F32)],
    )


def unpack_ffn_kernel(chunks, *refs):
    terms, (g_in_ref, g_down_ref) = refs[:-2], refs[-2:]
    rows = g_in_ref.shape[0]
    parts = FF // D
    per = parts // chunks
    for q in range(parts):
        at = 2 * per * D * (q // per) + D * (q % per)
        for out, first in ((g_in_ref, at), (g_down_ref, at + per * D)):
            total = terms[0][:, first : first + D].astype(F32)
            for ref in terms[1:]:
                total = total + ref[:, first : first + D].astype(F32)
            if out is g_in_ref:
                out[:, D * q : D * (q + 1)] = total
            else:
                out[rows * q : rows * (q + 1), :] = total


def unpack_ffn(deps, terms, chunks):
    rows = terms[0].shape[0]
    return run(
        functools.partial(unpack_ffn_kernel, chunks),
        deps,
        [],
        terms,
        [jax.ShapeDtypeStruct((rows, FF), F32), jax.ShapeDtypeStruct((rows * (FF // D), D), F32)],
        "unpack",
        2,
        grid=(1,),
        in_specs=[VMEM] * len(terms),
        out_specs=[VMEM] * 2,
        scratch_shapes=[],
    )


def split_kernel(lines, counts, z_ref, *refs):
    outs = refs[sum(counts) : sum(counts) + lines]
    total_s = refs[-1]
    first = 0
    at = 0
    for n in counts:
        terms = refs[first : first + n]
        rows, cols = terms[0].shape[-2:]
        total = terms[0][...].reshape(rows, cols).astype(F32)
        for ref in terms[1:]:
            total = total + ref[...].reshape(rows, cols).astype(F32)
        total_s[:, :, at : at + cols] = total.reshape(lines, rows // lines, cols)
        first += n
        at += cols
    for mask, out in enumerate(outs):
        out[...] = total_s[z_ref[0] ^ mask].astype(out.dtype)


def split(deps, z, sums, lines):
    kind = sums[0][0].dtype
    specs = []
    for t in [t for terms in sums for t in terms]:
        if t.ndim == 3:
            specs.append(pl.BlockSpec((1,) + t.shape[1:], lambda i, *_: (0, 0, 0)))
        else:
            specs.append(pl.BlockSpec(t.shape, lambda i, *_: (0, 0)))
    rows = sums[0][0].shape[-2] // lines
    cols = sum(terms[0].shape[-1] for terms in sums)
    return run(
        functools.partial(split_kernel, lines, [len(terms) for terms in sums]),
        deps,
        [z],
        [t for terms in sums for t in terms],
        [jax.ShapeDtypeStruct((rows, cols), F32 if m == 0 else kind) for m in range(lines)],
        "split",
        2,
        grid=(1,),
        in_specs=specs,
        out_specs=[VMEM] * lines,
        scratch_shapes=[pltpu.VMEM((lines, rows, cols), F32)],
    )


def sum_kernel(*refs):
    total = refs[0][...].astype(F32)
    for ref in refs[1:-1]:
        total = total + ref[...].astype(F32)
    refs[-1][...] = total.reshape(refs[-1].shape).astype(refs[-1].dtype)


def second(deps, terms):
    _, rows, cols = terms[0].shape
    return run(
        sum_kernel,
        deps,
        [],
        terms,
        [jax.ShapeDtypeStruct((rows, cols), terms[0].dtype)],
        "second",
        2,
        grid=(1,),
        in_specs=[pl.BlockSpec((1, rows, cols), lambda i: (1, 0, 0))] * len(terms),
        out_specs=[VMEM],
        scratch_shapes=[],
    )[0]


def both(deps, terms):
    lines, rows, cols = terms[0].shape
    spec = pl.BlockSpec((1, rows, cols), lambda i: (i, 0, 0))
    return run(
        sum_kernel,
        deps,
        [],
        terms,
        [jax.ShapeDtypeStruct(terms[0].shape, terms[0].dtype)],
        "both",
        2,
        grid=(lines,),
        in_specs=[spec] * len(terms),
        out_specs=[spec],
        scratch_shapes=[],
    )[0]


AXES = ("wide", "narrow")


class Links:
    def __init__(self, mesh):
        self.wide = mesh.shape["wide"]
        self.narrow = mesh.shape["narrow"]
        self.count = self.wide * self.narrow
        self.pairwise = self.wide == 8 and self.narrow == 4
        self.lines = self.wide if self.pairwise else 1
        self.groups = (2, 2, 2, 2) if self.pairwise else (1,)

    def setup(self):
        if not self.pairwise:
            self.pos = jnp.zeros((1,), jnp.int32)
            return
        w = lax.axis_index("wide")
        self.z = lax.axis_index("narrow")
        near = jnp.where(w % 2 == 0, 2, 4)
        far = 6 - near
        order = [0, near, far, 6, 1, 1 ^ far, 1 ^ near, 7]
        self.pos = jnp.stack([w ^ m for m in order]).astype(jnp.int32)

    def slot(self, *marks):
        self.marks = list(marks)

    def swap(self, x, wide_mask=0, narrow_mask=0):
        masks = wide_mask if isinstance(wide_mask, tuple) else (wide_mask, wide_mask)
        pairs = []
        for w in range(self.wide):
            for z in range(self.narrow):
                pairs.append(
                    (w * self.narrow + z, (w ^ masks[w % 2]) * self.narrow + (z ^ narrow_mask))
                )
        return lax.ppermute(x, AXES, pairs)

    def line(self, x):
        if not self.pairwise:
            return [lax.all_gather(x, AXES, axis=0, tiled=True)]
        return [x] + [self.swap(x, 0, mask) for mask in (1, 2, 3)]

    def own(self, parts):
        if not self.pairwise:
            return parts
        (x,) = order(self.marks, self.z.reshape(1), parts, 1)
        return self.around(x)

    def around(self, x):
        return [x, self.swap(x, (2, 4)), self.swap(x, (4, 2)), self.swap(x, 1)]

    def onward(self, lines):
        if not self.pairwise:
            return lines
        own, near, far, own_core = lines
        if self.marks:
            near = after(near, self.marks)
            far = after(far, self.marks)
        return [own, near, far, self.swap(near, (4, 2)), own_core, self.swap(near, 1), self.swap(far, 1)]

    def core(self, lines):
        if not self.pairwise:
            return lines
        own, near, far, both, *core = lines
        if self.marks:
            both = after(both, self.marks)
        return [own, near, far, both, *core, self.swap(both, 1)]

    def add(self, *parts):
        total = parts[0].astype(F32)
        for p in parts[1:]:
            total = total + p.astype(F32)
        return total


class Sum:
    def __init__(self, links, parts):
        self.links = links
        self.parts = parts
        self.kind = parts[0].dtype

    def core(self, marks=()):
        links = self.links
        if not links.pairwise:
            self.src = self.out = lax.psum_scatter(self.parts[0][0].astype(F32), AXES, scatter_dimension=0, tiled=True)
            return (self.out,)
        send_a, send_b = self.parts[2], self.parts[3]
        if marks:
            send_a, send_b = after(send_a, marks), after(send_b, marks)
        self.got_b = links.swap(send_b, 1)
        self.got_a = links.swap(send_a, 1)
        return (self.got_b, self.got_a)

    def far(self):
        links = self.links
        if not links.pairwise:
            return (self.out,)
        self.src = both(links.marks, [self.parts[1], self.got_b])
        self.from_far = links.swap(self.src, (4, 2))
        return (self.from_far,)

    def near(self):
        links = self.links
        if not links.pairwise:
            return (self.out,)
        self.src = second(links.marks, [self.parts[0], self.got_a, self.from_far])
        self.from_near = links.swap(self.src, (2, 4))
        return (self.from_near,)

    def line(self, *more):
        links = self.links
        sums = (self,) + more
        if not links.pairwise:
            self.terms = [jnp.concatenate([x.out for x in sums], axis=1)]
            return self.terms
        terms = [[x.parts[0], x.got_a, x.from_far, x.from_near] for x in sums]
        mine, *others = split(links.marks, links.z.reshape(1), terms, links.narrow)
        self.src = mine
        self.terms = [mine] + [links.swap(x, 0, mask) for mask, x in enumerate(others, 1)]
        return self.terms[1:]

    def total(self):
        return self.links.add(*self.terms)


CHUNKS = 2
PARTS = FF // D
PAIRS = 6


def body(links, long_in, glob_in, lengths, ln1_gain, ln1_bias, w_qkv, qv_bias, rel_embed, w_out, out_bias, ln2_gain, ln2_bias, w_in, in_bias, w_down, down_bias, cot_long, cot_glob):
    links.setup()
    pos = links.pos
    groups = links.groups
    count = links.count
    micro = long_in.shape[0]
    r = w_qkv.shape[0]
    lens = lengths.reshape(micro)
    per = PARTS // CHUNKS
    first, second = 3 * FIRST, 3 * SECOND
    n_first, n_second = FIRST // 128, SECOND // 128

    vectors = [ln1_gain, ln1_bias, qv_bias, out_bias, ln2_gain, ln2_bias, down_bias, in_bias]
    w_in_parts = w_in.reshape(r, count, PARTS, r).transpose(0, 2, 1, 3).reshape(r, FF)

    links.slot()
    own_a0 = links.own(links.line(pack(w_qkv, rel_embed, vectors)))
    line_a1 = links.line(pack_next([own_a0[0]], w_qkv, w_out))
    ffn_shard = pack_ffn([], w_in_parts, w_down, CHUNKS)
    links.slot(own_a0[len(own_a0) // 2])
    most_a0 = links.onward(own_a0)
    links.slot(*line_a1[1:], ffn_shard)
    attn = [links.core(most_a0)]
    line_f = links.line(after(ffn_shard, [attn[0][-1]]))

    proj0, normed, rel_all, rel_turned, vec = project_first([], pos, long_in, glob_in, attn[0], r, first)
    links.slot(attn[0][-1])
    own_a1 = links.own(line_a1)
    mixed0, inv0, p0, pg0 = attend([own_a1[-1], own_a1[0]], lens, proj0, rel_all, 0)
    links.slot(proj0)
    most_a1 = links.onward(own_a1)
    links.slot(mixed0)
    if links.pairwise:
        line_f = order(links.marks, links.z.reshape(1), line_f, CHUNKS)
        own_f = [links.around(line_f[0])]
    else:
        own_f = [[line_f[0][:, 2 * per * D * c : 2 * per * D * (c + 1)]] for c in range(CHUNKS)]
    links.slot(mixed0)
    attn.append(links.core(most_a1))
    proj1 = project_next([mixed0, own_f[0][0]], pos, normed, vec, attn[1], second)
    mixed1, inv1, p1, pg1 = attend([], lens, proj1, rel_all, n_first)
    mixed = [mixed0, mixed1]
    if links.pairwise:
        own_f.append(links.around(after(line_f[1], [proj1])))
    links.slot(mixed1)
    most_f0 = links.onward(own_f[0])
    most_f1 = links.onward(own_f[1])
    res, n2, g_ffn = mix_out(
        [most_f0[0]], pos, lens, long_in, glob_in, cot_long, cot_glob, vec, mixed, attn[1], second
    )
    links.slot(n2)
    ffn0 = links.core(most_f0)
    y0, gn0, gb0, *gw0 = ffn([], pos, n2, g_ffn, vec, ffn0, 0, per, groups)
    links.slot(y0)
    ffn1 = links.core(most_f1)
    sum0 = Sum(links, gw0)
    y1, gn1, gb1, *gw1 = ffn([y0], pos, n2, g_ffn, vec, ffn1, per, per, groups)
    core0 = sum0.core()
    sum1 = Sum(links, gw1)
    links.slot(y1)
    far0 = sum0.far()
    block_long, block_glob, gres, gmix, small2, gw_out = mid(
        [sum0.src], pos, lens, res, g_ffn, vec, [y0, y1], [gn0, gn1], mixed, attn[1], second, long_in.shape, glob_in.shape
    )
    core1 = sum1.core()
    links.slot(gmix)
    near0 = sum0.near()
    sum1.far()
    gproj1, grel1 = attend_back([sum0.src, sum1.src], proj1, rel_turned, gmix, mixed1, inv1, p1, pg1, n_first, 0, n_second)
    links.slot(gproj1)
    sum1.near()
    gw_a1 = weight_grad([sum1.src, *near0], pos, normed, [gproj1], [gw_out], groups)
    sum2 = Sum(links, gw_a1)
    sum2.core()
    links.slot(gw_a1[0])
    line01 = sum0.line(sum1)
    gproj0, grel0 = attend_back([sum0.src], proj0, rel_turned, gmix, mixed0, inv0, p0, pg0, 0, 0, n_first)
    links.slot(gproj0)
    sum2.far()
    grad_long, grad_glob, small1, small_qv = input_grad(
        [sum2.src], pos, long_in, glob_in, gres, vec, [gproj0, gproj1], attn
    )
    links.slot(small1)
    near2 = sum2.near()
    gw_a0 = weight_grad(
        [sum2.src, *line01], pos, normed, [gproj0], [grel0, grel1, small2, small1, small_qv, gb0, gb1], groups, r
    )
    sum3 = Sum(links, gw_a0)
    sum3.core(near2)
    links.slot(gw_a0[0])
    sum3.far()
    links.slot(sum3.src)
    sum2.line()
    g_in, g_down = unpack_ffn([sum3.src], sum0.terms, CHUNKS)
    links.slot(sum2.src, g_in)
    sum3.near()
    g_in = g_in.reshape(r, PARTS, count, r).transpose(0, 2, 1, 3).reshape(r, FF)
    links.slot()
    sum3.line()
    order_out = [ln1_gain, ln1_bias, qv_bias, ln2_gain, ln2_bias, out_bias, down_bias, in_bias]
    g_qkv, g_out, g_rel, g_gain1, g_bias1, g_qv, g_gain2, g_bias2, g_out_b, g_down_b, g_in_b = unpack(
        sum3.terms, sum2.terms, [v.shape[0] for v in order_out]
    )
    return (
        block_long, block_glob, grad_long, grad_glob,
        g_gain1, g_bias1, g_qkv, g_qv, g_rel, g_out, g_out_b,
        g_gain2, g_bias2, g_in, g_in_b, g_down, g_down_b,
    )


def solution(mesh):
    rows = P(None, AXES, None, None)
    vec = P(AXES)
    mat = P(AXES, None)
    placed = (rows, rows, P(None, AXES), vec, vec, mat, vec, mat, mat, vec, vec, vec, mat, vec, mat, vec, rows, rows)
    return jax.shard_map(
        functools.partial(body, Links(mesh)),
        mesh=mesh,
        in_specs=placed,
        out_specs=(rows, rows, rows, rows, vec, vec, mat, vec, mat, mat, vec, vec, vec, mat, vec, mat, vec),
        check_vma=False,
    )
```
